32 devices in a mesh: dp: 16 (over z, y, x), tensor: 2 (over core).
Axes of the slice: x: 2, y: 2, z: 4, core: 2. Of those that a mesh axis runs over, the one named last changes fastest.
Arguments:
- enc_params: float32 [2, 7077888], P('tensor', 'dp'), may hold values from -2.44948974 to 2.44948974, as said below
- enc_m1: float32 [2, 7077888], P('tensor', 'dp'), may hold values from -7.4505806e-08 to 7.4505806e-08
- enc_m2: float32 [2, 7077888], P('tensor', 'dp'), may hold values from 2.3901121e-18 to 9.5604485e-18
- pred_params: float32 [2, 1277952], P('tensor', 'dp'), may hold values from -2.44948974 to 2.44948974, as said below
- pred_m1: float32 [2, 1277952], P('tensor', 'dp'), may hold values from -7.4505806e-08 to 7.4505806e-08
- pred_m2: float32 [2, 1277952], P('tensor', 'dp'), may hold values from 2.3901121e-18 to 9.5604485e-18
- target_params: float32 [2, 7077888], P('tensor', 'dp'), may hold values from -2.44948974 to 2.44948974, as said below
- vecs: float32 [23936], replicated, may hold values from -6 to 6, as said below
- vec_m1: float32 [23936], replicated, may hold values from -2.9802322e-07 to 2.9802322e-07
- vec_m2: float32 [23936], replicated, may hold values from 3.8241794e-17 to 1.5535729e-16
- target_vecs: float32 [16384], replicated, may hold values from -6 to 6, as said below
- patches: bfloat16 [18816, 1536], P('dp', 'tensor'), may hold values from -6 to 6
- segment: int32 [18816], P('dp'), may hold values from 0 to 4, as said below
- context: int32 [18816], P('dp'), may hold values from 0 to 1, as said below
- step_count: int32 [1], replicated, may hold values from 1 to 20
Outputs:
- new_enc_params: float32 [2, 7077888], P('tensor', 'dp')
- new_enc_m1: float32 [2, 7077888], P('tensor', 'dp')
- new_enc_m2: float32 [2, 7077888], P('tensor', 'dp')
- enc_bf16: bfloat16 [2, 7077888], P('tensor', 'dp')
- new_pred_params: float32 [2, 1277952], P('tensor', 'dp')
- new_pred_m1: float32 [2, 1277952], P('tensor', 'dp')
- new_pred_m2: float32 [2, 1277952], P('tensor', 'dp')
- pred_bf16: bfloat16 [2, 1277952], P('tensor', 'dp')
- new_target_params: float32 [2, 7077888], P('tensor', 'dp')
- new_vecs: float32 [23936], replicated
- new_vec_m1: float32 [23936], replicated
- new_vec_m2: float32 [23936], replicated
- new_target_vecs: float32 [16384], replicated
- loss: float32 [], replicated
- grad_norm: float32 [], replicated
The draws below stay inside these ranges and needn't reach their ends.
Inputs may be any that keep to these rules, and one draw needn't show every extreme that they name: `segment`: segment numbers count the samples of a pack from 0 and never fall within it. Sample 0 of a pack is a video of 2 to 6 frame pairs of 196 tokens; every later sample is an image of 196 tokens. In every draw some pack holds a video of 1176 tokens. The first token of every sample is a context token. `enc_params`: entries of each matrix block are normal with a deviation of a fixed multiple of one over the root of its fan-in. `pred_params`: as for enc_params. `target_params`: as for enc_params. `vecs`: gains near 1, biases and the mask token of both signs. `target_vecs`: gains near 1, biases of both signs.
All inputs are finite; a program needn't handle non-finite values.
Results may differ from the reference program's by a relative error of at most 0.0034.
Values may be sent and summed in bfloat16 or wider, within the bound.
No kernel may reach another device: no remote copies, remote signals or barrier semaphores. Data moves between devices by JAX's collectives and lax.ppermute only.
A program may use at most 1.0625 GiB of HBM per device.

```python
import math
import jax
import jax.numpy as jnp
from jax import lax

D = 1024
HEADS = 16
HEAD_DIM = 64
MLP = 4096
PATCH = 1536
PD = 384
PHEADS = 12
PHEAD_DIM = 32
PMLP = 1536
FRAME = 196
TP_WAYS = 2
LONGEST = 6
TOK_DEV = 1176
TOKENS = 18816
ENC_T = 7077888
PRED_T = 1277952
ENCVEC = 16384
VEC = 23936


def enc_shapes_drawn(ways):
    return [('w_patch', PATCH // ways, D), ('w_qkv', D, 3 * D // ways), ('w_out', D // ways, D), ('w_up', D, MLP // ways), ('w_down', MLP // ways, D)]


def pred_shapes_drawn(ways):
    return [('w_pin', D, PD // ways), ('w_pqkv', PD, 3 * PD // ways), ('w_pout', PD // ways, PD), ('w_pup', PD, PMLP // ways), ('w_pdown', PMLP // ways, PD), ('w_pproj', PD, D // ways)]


def enc_vectors_drawn():
    return [('b_patch', D), ('ln1_g', D), ('ln1_b', D), ('b_qkv', 3 * D), ('b_out', D), ('ln2_g', D), ('ln2_b', D), ('b_up', MLP), ('b_down', D), ('lnf_g', D), ('lnf_b', D)]


def pred_vectors_drawn():
    return [('b_pin', PD), ('mask_tok', PD), ('pln1_g', PD), ('pln1_b', PD), ('b_pqkv', 3 * PD), ('b_pout', PD), ('pln2_g', PD), ('pln2_b', PD), ('b_pup', PMLP), ('b_pdown', PD), ('plnf_g', PD), ('plnf_b', PD), ('b_pproj', D)]


def matrix_scales():
    return {'w_patch': PATCH ** (-0.5), 'w_qkv': D ** (-0.5), 'w_out': 8.0 * D ** (-0.5), 'w_up': D ** (-0.5), 'w_down': MLP ** (-0.5), 'w_pin': D ** (-0.5), 'w_pqkv': PD ** (-0.5), 'w_pout': 8.0 * PD ** (-0.5), 'w_pup': PD ** (-0.5), 'w_pdown': PMLP ** (-0.5), 'w_pproj': 0.5 * PD ** (-0.5)}


def draw_matrices(key, shapes):
    scales = matrix_scales()
    rows_out = []
    for member in range(TP_WAYS):
        pieces = []
        for position, section in enumerate(shapes):
            label, height, breadth = section
            sample = jax.random.normal(jax.random.fold_in(key, member * 100 + position), (height * breadth,), jnp.float32)
            pieces.append(jnp.clip(sample, -6.0, 6.0) * scales[label])
        rows_out.append(jnp.concatenate(pieces))
    return jnp.stack(rows_out)


def draw_vector_set(key, sections):
    pieces = []
    for position, section in enumerate(sections):
        label, length = section
        sample = jnp.clip(jax.random.normal(jax.random.fold_in(key, position), (length,), jnp.float32), -6.0, 6.0)
        if label[-2:] == '_g':
            pieces.append(1.0 + 0.1 * sample)
        elif label == 'mask_tok':
            pieces.append(sample)
        else:
            pieces.append(0.2 * sample)
    return jnp.concatenate(pieces)


def draw_enc_params(key, part):
    return draw_matrices(jax.random.fold_in(key, 21), enc_shapes_drawn(TP_WAYS))


def draw_pred_params(key, part):
    return draw_matrices(jax.random.fold_in(key, 22), pred_shapes_drawn(TP_WAYS))


def draw_target_params(key, part):
    return draw_matrices(jax.random.fold_in(key, 23), enc_shapes_drawn(TP_WAYS))


def draw_vecs(key, part):
    return draw_vector_set(jax.random.fold_in(key, 24), enc_vectors_drawn() + pred_vectors_drawn())


def draw_target_vecs(key, part):
    return draw_vector_set(jax.random.fold_in(key, 25), enc_vectors_drawn())


def layout_frames(key):
    packs = TOKENS // TOK_DEV
    frames = jax.random.randint(jax.random.fold_in(key, 1), (packs,), 2, LONGEST + 1)
    chosen = jax.random.randint(jax.random.fold_in(key, 2), (), 0, packs)
    return jnp.where(jnp.arange(packs) == chosen, LONGEST, frames)


def draw_segment(key, part):
    frames = layout_frames(jax.random.fold_in(key, 5))
    slot = jnp.arange(TOK_DEV) // FRAME
    numbers = jnp.where(slot[None, :] < frames[:, None], 0, slot[None, :] - frames[:, None] + 1)
    return numbers.reshape(-1).astype(jnp.int32)


def draw_context(key, part):
    frames = layout_frames(jax.random.fold_in(key, 5))
    packs = TOKENS // TOK_DEV
    index_row = jnp.arange(TOK_DEV)[None, :]
    first = (index_row == 0) | (index_row >= frames[:, None] * FRAME) & (index_row % FRAME == 0)
    coin = jax.random.randint(jax.random.fold_in(key, 6), (packs, TOK_DEV), 0, 4) == 0
    return (first | coin).astype(jnp.int32).reshape(-1)


def level_of(stream_key, dims, cuts, low, high):
    level = 1.0
    for dim, blocks in cuts:
        draws = jax.random.uniform(jax.random.fold_in(jax.random.fold_in(stream_key, 6), dim), (blocks,), jnp.float32, low / len(cuts), high / len(cuts))
        level = level * jnp.repeat(jnp.exp(draws), dims[dim] // blocks).reshape((-1,) + (1,) * (len(dims) - 1 - dim))
    return level


def centred(key, extent, deviation, reach, shards=(), kind=jnp.bfloat16):
    drawn = deviation * jax.random.normal(key, extent, jnp.float32)
    if shards:
        drawn = drawn * level_of(key, extent, shards, -0.22, 0.18)
    return jnp.clip(drawn, -reach, reach).astype(kind)


def setup_inputs(seed: int = 0) -> dict:
    key_of = jax.random.split(jax.random.key(seed), 16)
    enc_params = draw_enc_params(jax.random.fold_in(key_of[15], 71), 0)
    enc_m1 = centred(key_of[1], (TP_WAYS, ENC_T), (0.000022 / (2 * ENC_T + 2 * PRED_T + VEC) ** 0.5), 7.450580596923828e-08, ((0, 2), (1, 16)), jnp.float32)
    enc_m2 = jnp.clip(jnp.exp(math.log(9.5604484679501e-18) - 1.3862944 * jax.random.uniform(key_of[2], (TP_WAYS, ENC_T), jnp.float32) ** level_of(key_of[2], (TP_WAYS, ENC_T), ((0, 2), (1, 16)), -0.2, 0.2)), 2.390112116987525e-18, 9.5604484679501e-18)
    pred_params = draw_pred_params(jax.random.fold_in(key_of[15], 71), 0)
    pred_m1 = centred(key_of[4], (TP_WAYS, PRED_T), (0.000022 / (2 * ENC_T + 2 * PRED_T + VEC) ** 0.5), 7.450580596923828e-08, ((0, 2), (1, 16)), jnp.float32)
    pred_m2 = jnp.clip(jnp.exp(math.log(9.5604484679501e-18) - 1.3862944 * jax.random.uniform(key_of[5], (TP_WAYS, PRED_T), jnp.float32) ** level_of(key_of[5], (TP_WAYS, PRED_T), ((0, 2), (1, 16)), -0.2, 0.2)), 2.390112116987525e-18, 9.5604484679501e-18)
    target_params = draw_target_params(jax.random.fold_in(key_of[15], 71), 0)
    vecs = draw_vecs(jax.random.fold_in(key_of[15], 71), 0)
    vec_m1 = centred(key_of[8], (VEC,), (0.000088 / (2 * ENC_T + 2 * PRED_T + VEC) ** 0.5), 2.980232238769531e-07, (), jnp.float32)
    vec_m2 = jnp.clip(jnp.exp(jax.random.uniform(key_of[9], (VEC,), jnp.float32, math.log(3.82417938718004e-17), math.log(1.5535729070611642e-16))), 3.82417938718004e-17, 1.5535729070611642e-16)
    target_vecs = draw_target_vecs(jax.random.fold_in(key_of[15], 71), 0)
    patches = centred(key_of[11], (TOKENS, PATCH), 1.0, 6.0, ((0, 16), (1, 2)))
    segment = draw_segment(jax.random.fold_in(key_of[15], 71), 0)
    context = draw_context(jax.random.fold_in(key_of[15], 71), 0)
    step_count = jax.random.randint(key_of[14], (1,), 1, 21).astype(jnp.int32)
    return dict(enc_params=enc_params, enc_m1=enc_m1, enc_m2=enc_m2, pred_params=pred_params, pred_m1=pred_m1, pred_m2=pred_m2, target_params=target_params, vecs=vecs, vec_m1=vec_m1, vec_m2=vec_m2, target_vecs=target_vecs, patches=patches, segment=segment, context=context, step_count=step_count)


HIGH = lax.Precision.HIGHEST
BETA_ONE = 0.9
BETA_TWO = 0.999
ADAM_EPS = 1e-08
RATE_MAT = 0.01
RATE_VEC = 0.05
DECAY = 0.05
CLIP = 0.0002
TAU = 0.75
NORM_EPS = 1e-06
VAR_EPS = 0.0001
ROW_JOIN = ('w_patch', 'w_out', 'w_down', 'w_pout', 'w_pdown')
TRIPLE = ('w_qkv', 'w_pqkv')

@jax.custom_vjp
def low(v):
    return lax.optimization_barrier(v.astype(jnp.bfloat16)).astype(jnp.float32)

@jax.custom_vjp
def low_back(v):
    return v

def low_keep(v):
    return (low(v), None)

def low_pass(kept, grad):
    return (grad,)

def back_keep(v):
    return (v, None)

def back_low(kept, grad):
    return (low(grad),)
low.defvjp(low_keep, low_pass)
low_back.defvjp(back_keep, back_low)

def enc_shapes(ways):
    return [('w_patch', PATCH // ways, D), ('w_qkv', D, 3 * D // ways), ('w_out', D // ways, D), ('w_up', D, MLP // ways), ('w_down', MLP // ways, D)]

def pred_shapes(ways):
    return [('w_pin', D, PD // ways), ('w_pqkv', PD, 3 * PD // ways), ('w_pout', PD // ways, PD), ('w_pup', PD, PMLP // ways), ('w_pdown', PMLP // ways, PD), ('w_pproj', PD, D // ways)]

def enc_vectors():
    return [('b_patch', D), ('ln1_g', D), ('ln1_b', D), ('b_qkv', 3 * D), ('b_out', D), ('ln2_g', D), ('ln2_b', D), ('b_up', MLP), ('b_down', D), ('lnf_g', D), ('lnf_b', D)]

def pred_vectors():
    return [('b_pin', PD), ('mask_tok', PD), ('pln1_g', PD), ('pln1_b', PD), ('b_pqkv', 3 * PD), ('b_pout', PD), ('pln2_g', PD), ('pln2_b', PD), ('b_pup', PMLP), ('b_pdown', PD), ('plnf_g', PD), ('plnf_b', PD), ('b_pproj', D)]

def unflat(flat_row, shapes):
    result = {}
    offset = 0
    for label, height, breadth in shapes:
        result[label] = flat_row[offset:offset + height * breadth].reshape(height, breadth)
        offset += height * breadth
    return result

def split_vector(vector, sections):
    result = {}
    offset = 0
    for label, length in sections:
        result[label] = vector[offset:offset + length]
        offset += length
    return result

def assemble(stacked, shapes):
    shard_sets = [unflat(stacked[member], shapes) for member in range(TP_WAYS)]
    joined = {}
    for label, _, _ in shapes:
        pieces = [shard_set[label] for shard_set in shard_sets]
        if label in ROW_JOIN:
            whole = jnp.concatenate(pieces, 0)
        elif label in TRIPLE:
            thirds = [jnp.split(piece, 3, axis=1) for piece in pieces]
            whole = jnp.concatenate([jnp.concatenate([third[member] for third in thirds], 1) for member in range(3)], 1)
        else:
            whole = jnp.concatenate(pieces, 1)
        joined[label] = low(whole)
    return joined

def positions(segment_row):
    earlier = lax.optimization_barrier(jnp.sum((segment_row[None, :] < segment_row[:, None]).astype(jnp.int32), axis=1))
    return (jnp.arange(segment_row.shape[0], dtype=jnp.int32) - earlier).astype(jnp.float32)

def sincos(places, width):
    half_width = width // 2
    freqs = jnp.exp(-math.log(10000.0) * jnp.arange(half_width).astype(jnp.float32) / half_width)
    angles = places[:, None] * freqs[None, :]
    return jnp.concatenate([jnp.sin(angles), jnp.cos(angles)], axis=1)

def layer_norm(values, gain, shift):
    centered = values - lax.optimization_barrier(jnp.mean(values, axis=-1, keepdims=True))
    spread = lax.optimization_barrier(jnp.mean(centered * centered, axis=-1, keepdims=True))
    return centered * lax.rsqrt(spread + NORM_EPS) * gain + shift

def plain_norm(values):
    centered = values - lax.optimization_barrier(jnp.mean(values, axis=-1, keepdims=True))
    return centered * lax.rsqrt(lax.optimization_barrier(jnp.mean(centered * centered, axis=-1, keepdims=True)) + NORM_EPS)

def attention(normed, w_qkv, b_qkv, w_out, b_out, heads, head_dim, allowed):
    row_count = normed.shape[0]
    width = heads * head_dim
    packed = low(low_back(jnp.dot(low(normed), w_qkv, precision=HIGH) + b_qkv))
    queries = packed[:, :width].reshape(row_count, heads, head_dim)
    keys_all = packed[:, width:2 * width].reshape(row_count, heads, head_dim)
    values = packed[:, 2 * width:].reshape(row_count, heads, head_dim)
    scores = low_back(jnp.einsum('qhd,khd->hqk', queries, keys_all, precision=HIGH) * head_dim ** (-0.5))
    scores = jnp.where(allowed[None], scores, -1e+30)
    weights = jax.nn.softmax(scores, axis=-1)
    mixed = low(low_back(jnp.einsum('hqk,khd->qhd', low(weights), values, precision=HIGH))).reshape(row_count, width)
    return low_back(jnp.dot(mixed, w_out, precision=HIGH)) + b_out

def feed_forward(normed, w_up, b_up, w_down, b_down):
    hidden = low_back(jnp.dot(low(normed), w_up, precision=HIGH) + b_up)
    activated = low(jax.nn.gelu(hidden))
    return low_back(jnp.dot(activated, w_down, precision=HIGH)) + b_down

def block(stream, weights, vectors, tag, heads, head_dim, allowed):
    normed = layer_norm(stream, vectors[tag + 'ln1_g'], vectors[tag + 'ln1_b'])
    middle = stream + attention(normed, weights['w_' + tag + 'qkv'], vectors['b_' + tag + 'qkv'], weights['w_' + tag + 'out'], vectors['b_' + tag + 'out'], heads, head_dim, allowed)
    normed_two = layer_norm(middle, vectors[tag + 'ln2_g'], vectors[tag + 'ln2_b'])
    return middle + feed_forward(normed_two, weights['w_' + tag + 'up'], vectors['b_' + tag + 'up'], weights['w_' + tag + 'down'], vectors['b_' + tag + 'down'])

def encode(patch_rows, segment_row, key_mask, weights, vectors):
    stream = low_back(jnp.dot(low(patch_rows), weights['w_patch'], precision=HIGH)) + vectors['b_patch']
    stream = stream + sincos(positions(segment_row), D)
    allowed = (segment_row[:, None] == segment_row[None, :]) & (key_mask[None, :] > 0)
    stream = block(stream, weights, vectors, '', HEADS, HEAD_DIM, allowed)
    return layer_norm(stream, vectors['lnf_g'], vectors['lnf_b'])

def predict(encoded, segment_row, context_row, weights, vectors):
    inner = low_back(jnp.dot(low(encoded), weights['w_pin'], precision=HIGH)) + vectors['b_pin']
    stream = jnp.where(context_row[:, None] > 0, inner, vectors['mask_tok'][None, :])
    stream = stream + sincos(positions(segment_row), PD)
    allowed = segment_row[:, None] == segment_row[None, :]
    stream = block(stream, weights, vectors, 'p', PHEADS, PHEAD_DIM, allowed)
    normed = layer_norm(stream, vectors['plnf_g'], vectors['plnf_b'])
    return low_back(jnp.dot(low(normed), weights['w_pproj'], precision=HIGH)) + vectors['b_pproj']

def adam(weight, first, second, grad, rate, decay, count):
    first_new = BETA_ONE * first + (1 - BETA_ONE) * grad
    second_new = BETA_TWO * second + (1 - BETA_TWO) * grad * grad
    first_hat = first_new / (1 - BETA_ONE ** count)
    second_hat = second_new / (1 - BETA_TWO ** count)
    weight_new = weight - rate * (first_hat / (jnp.sqrt(second_hat) + ADAM_EPS) + decay * weight)
    return (weight_new, first_new, second_new)

def reference(enc_params, enc_m1, enc_m2, pred_params, pred_m1, pred_m2, target_params, vecs, vec_m1, vec_m2, target_vecs, patches, segment, context, step_count):
    packs = TOKENS // TOK_DEV
    patch_packs = patches.astype(jnp.float32).reshape(packs, TOK_DEV, PATCH)
    segment_packs = segment.reshape(packs, TOK_DEV)
    context_packs = context.reshape(packs, TOK_DEV)
    target_weights = assemble(target_params, enc_shapes(TP_WAYS))
    target_vectors = split_vector(target_vecs, enc_vectors())

    def target_pack(inputs):
        patch_rows, segment_row, context_row = inputs
        encoded = encode(patch_rows, segment_row, jnp.ones_like(context_row), target_weights, target_vectors)
        return plain_norm(encoded)
    targets = lax.map(target_pack, (patch_packs, segment_packs, context_packs)).reshape(TOKENS, D)
    target_mask = (1 - context).astype(jnp.float32)

    def loss_of(enc_flat, pred_flat, vector_all):
        weights = assemble(enc_flat, enc_shapes(TP_WAYS))
        weights.update(assemble(pred_flat, pred_shapes(TP_WAYS)))
        vectors = split_vector(vector_all, enc_vectors() + pred_vectors())

        def one_pack(inputs):
            patch_rows, segment_row, context_row = inputs
            encoded = encode(patch_rows, segment_row, context_row, weights, vectors)
            return predict(encoded, segment_row, context_row, weights, vectors)
        predicted = lax.map(jax.checkpoint(one_pack), (patch_packs, segment_packs, context_packs)).reshape(TOKENS, D)
        target_count = jnp.sum(target_mask)
        error = jnp.sum(target_mask[:, None] * jnp.abs(predicted - targets)) / (target_count * D)
        column_mean = lax.optimization_barrier(jnp.sum(target_mask[:, None] * predicted, axis=0)) / target_count
        column_var = lax.optimization_barrier(jnp.sum(target_mask[:, None] * predicted * predicted, axis=0)) / target_count - column_mean * column_mean
        spread = jnp.sqrt(column_var + VAR_EPS)
        return error + jnp.mean((spread - 1.0) ** 2)
    loss_value, pullback = jax.vjp(loss_of, enc_params, pred_params, vecs)
    grad_enc, grad_pred, grad_vec = pullback(jnp.ones_like(loss_value))
    grad_norm = jnp.sqrt(jnp.sum(grad_enc * grad_enc) + jnp.sum(grad_pred * grad_pred) + jnp.sum(grad_vec * grad_vec))
    factor = jnp.minimum(1.0, CLIP / (grad_norm + 1e-06))
    count = step_count[0].astype(jnp.float32)
    new_enc, enc_first, enc_second = adam(enc_params, enc_m1, enc_m2, grad_enc * factor, RATE_MAT, DECAY, count)
    new_pred, pred_first, pred_second = adam(pred_params, pred_m1, pred_m2, grad_pred * factor, RATE_MAT, DECAY, count)
    new_vec, vec_first, vec_second = adam(vecs, vec_m1, vec_m2, grad_vec * factor, RATE_VEC, 0.0, count)
    new_target = TAU * target_params + (1 - TAU) * new_enc
    new_target_vec = TAU * target_vecs + (1 - TAU) * new_vec[:ENCVEC]
    return (new_enc, enc_first, enc_second, new_enc.astype(jnp.bfloat16), new_pred, pred_first, pred_second, new_pred.astype(jnp.bfloat16), new_target, new_vec, vec_first, vec_second, new_target_vec, loss_value, grad_norm)
```

```python
import functools
import math

import jax
import jax.numpy as jnp
from jax import lax
from jax.experimental import pallas as pl
from jax.experimental.pallas import tpu as pltpu
from jax.sharding import PartitionSpec as P

D = 1024
HEADS = 16
HEAD_DIM = 64
MLP = 4096
PATCH = 1536
PD = 384
PHEADS = 12
PHEAD_DIM = 32
PMLP = 1536


BETA_ONE = 0.9
BETA_TWO = 0.999
ADAM_EPS = 1e-08
RATE_MAT = 0.01
RATE_VEC = 0.05
DECAY = 0.05
CLIP = 0.0002
TAU = 0.75
NORM_EPS = 1e-06
VAR_EPS = 0.0001
LOCAL_BIAS = {
    "b_qkv": True,
    "b_pqkv": True,
    "b_up": False,
    "b_pup": False,
    "b_pin": False,
    "b_pproj": False,
}
ROW_GAINS = ("ln2_g", "ln2_b", "pln2_g", "pln2_b")


def enc_shapes(ways):
    return [
        ("w_patch", PATCH // ways, D),
        ("w_qkv", D, 3 * D // ways),
        ("w_out", D // ways, D),
        ("w_up", D, MLP // ways),
        ("w_down", MLP // ways, D),
    ]


def pred_shapes(ways):
    return [
        ("w_pin", D, PD // ways),
        ("w_pqkv", PD, 3 * PD // ways),
        ("w_pout", PD // ways, PD),
        ("w_pup", PD, PMLP // ways),
        ("w_pdown", PMLP // ways, PD),
        ("w_pproj", PD, D // ways),
    ]


def enc_vectors():
    return [
        ("b_patch", D),
        ("ln1_g", D),
        ("ln1_b", D),
        ("b_qkv", 3 * D),
        ("b_out", D),
        ("ln2_g", D),
        ("ln2_b", D),
        ("b_up", MLP),
        ("b_down", D),
        ("lnf_g", D),
        ("lnf_b", D),
    ]


def pred_vectors():
    return [
        ("b_pin", PD),
        ("mask_tok", PD),
        ("pln1_g", PD),
        ("pln1_b", PD),
        ("b_pqkv", 3 * PD),
        ("b_pout", PD),
        ("pln2_g", PD),
        ("pln2_b", PD),
        ("b_pup", PMLP),
        ("b_pdown", PD),
        ("plnf_g", PD),
        ("plnf_b", PD),
        ("b_pproj", D),
    ]


def unflat(flat_row, shapes):
    result = {}
    offset = 0
    for label, height, breadth in shapes:
        result[label] = flat_row[offset : offset + height * breadth].reshape(height, breadth)
        offset += height * breadth
    return result


def split_vector(vector, sections):
    result = {}
    offset = 0
    for label, length in sections:
        result[label] = vector[offset : offset + length]
        offset += length
    return result


def positions(segment_row):
    earlier = jnp.sum((segment_row[None, :] < segment_row[:, None]).astype(jnp.int32), axis=1)
    return (jnp.arange(segment_row.shape[0], dtype=jnp.int32) - earlier).astype(jnp.float32)


def sincos(places, width):
    half_width = width // 2
    freqs = jnp.exp(-math.log(10000.0) * jnp.arange(half_width).astype(jnp.float32) / half_width)
    angles = places[:, None] * freqs[None, :]
    return jnp.concatenate([jnp.sin(angles), jnp.cos(angles)], axis=1)


def layer_norm(values, gain, shift):
    centered = values - jnp.mean(values, axis=-1, keepdims=True)
    spread = jnp.mean(centered * centered, axis=-1, keepdims=True)
    return centered * lax.rsqrt(spread + NORM_EPS) * gain + shift


def plain_norm(values):
    centered = values - jnp.mean(values, axis=-1, keepdims=True)
    return centered * lax.rsqrt(jnp.mean(centered * centered, axis=-1, keepdims=True) + NORM_EPS)


def norm_backward(values, gain, shift, cotangent):
    return jax.vjp(layer_norm, values, gain, shift)[1](cotangent)


def matmul(left, right):
    return jnp.dot(left, right, preferred_element_type=jnp.float32)


def matmul_tn(left, right):
    return lax.dot_general(
        left, right, (((0,), (0,)), ((), ())), preferred_element_type=jnp.float32
    )


def matmul_nt(left, right):
    return lax.dot_general(
        left, right, (((1,), (1,)), ((), ())), preferred_element_type=jnp.float32
    )


def local_columns(vector, thirds, ways, member):
    if thirds:
        width = vector.shape[0] // 3
        slab = vector.reshape(3, width)
        return lax.dynamic_slice_in_dim(slab, member * (width // ways), width // ways, 1).reshape(
            -1
        )
    return lax.dynamic_slice_in_dim(
        vector, member * (vector.shape[0] // ways), vector.shape[0] // ways, 0
    )


def place_columns(local, length, thirds, ways, member):
    if thirds:
        slab = jnp.zeros((3, length // 3), jnp.float32)
        placed = lax.dynamic_update_slice_in_dim(
            slab, local.reshape(3, -1), member * (length // 3 // ways), 1
        )
        return placed.reshape(-1)
    return lax.dynamic_update_slice_in_dim(
        jnp.zeros((length,), jnp.float32), local, member * (length // ways), 0
    )


QB = 256
LOG2E = math.log2(math.e)

def roundup(n, m):
    return -(-n // m) * m

def dot_nn(a, b):
    return lax.dot_general(a, b, (((1,), (0,)), ((), ())), preferred_element_type=jnp.float32)

def dot_nt(a, b):
    return lax.dot_general(a, b, (((1,), (1,)), ((), ())), preferred_element_type=jnp.float32)

def pad_rows(x, n):
    return jnp.concatenate([x.astype(jnp.float32), jnp.zeros((n - x.shape[0], x.shape[1]), jnp.float32)], 0).astype(x.dtype)

def lane_keep(x, lo, hi):
    lane = lax.broadcasted_iota(jnp.int32, (1, x.shape[1]), 1)
    keep = jnp.where((lane >= lo) & (lane < hi), 1.0, 0.0).astype(x.dtype)
    return x * keep

def attn_fwd_kernel(heads, e, T, TP, W, packed_ref, qa_ref, ka_ref, o_ref, lse_ref, q_s, k_s, v_s, o_s):
    g = pl.program_id(0)
    base = pl.multiple_of(g * 128, 128)
    q_s[...] = pad_rows(packed_ref[:, pl.ds(base, 128)], TP)
    k_s[:, :128] = pad_rows(packed_ref[:, pl.ds(base + W, 128)], TP)
    k_s[:, 128:] = ka_ref[...]
    v_s[...] = pad_rows(packed_ref[:, pl.ds(base + 2 * W, 128)], TP)
    scale = e ** -0.5 * LOG2E
    lane = lax.broadcasted_iota(jnp.int32, (QB, 128), 1)

    def block(i, _):
        rows = pl.ds(pl.multiple_of(i * QB, QB), QB)
        q = q_s[rows, :]
        qa = qa_ref[rows, :]
        out = jnp.zeros((QB, 128), jnp.float32)
        stats = jnp.zeros((QB, 128), jnp.float32)
        for h in range(heads):
            qq = jnp.concatenate([lane_keep(q, h * e, (h + 1) * e), qa], 1)
            s = dot_nt(qq, k_s[...]) * scale
            peak = jnp.max(s, axis=1, keepdims=True)
            p = jnp.exp2(s - peak)
            total = jnp.sum(p, axis=1, keepdims=True)
            p = (p * (1.0 / total)).astype(jnp.bfloat16)
            o = dot_nn(p, v_s[...])
            mine = (lane >= h * e) & (lane < (h + 1) * e)
            out = jnp.where(mine, o, out)
            stats = jnp.where(lane == h, peak + jnp.log2(total), stats)
        o_s[rows, :] = out.astype(jnp.bfloat16)
        lse_ref[0, :, rows] = stats.T[:8, :]
        return 0

    lax.fori_loop(0, TP // QB, block, 0)
    o_ref[...] = o_s[:T, :]

def attn_fwd(packed, qa, ka, heads, e):
    T, W3 = packed.shape
    W = W3 // 3
    TP = roundup(T, QB)
    groups = W // 128
    return pl.pallas_call(
        functools.partial(attn_fwd_kernel, heads, e, T, TP, W),
        grid=(groups,),
        in_specs=[pl.BlockSpec((T, W3), lambda g: (0, 0)), pl.BlockSpec((TP, 128), lambda g: (0, 0)), pl.BlockSpec((TP, 128), lambda g: (0, 0))],
        out_specs=[pl.BlockSpec((T, 128), lambda g: (0, g)), pl.BlockSpec((1, 8, TP), lambda g: (g, 0, 0))],
        out_shape=[jax.ShapeDtypeStruct((T, W), jnp.bfloat16), jax.ShapeDtypeStruct((groups, 8, TP), jnp.float32)],
        scratch_shapes=[pltpu.VMEM((TP, 128), jnp.bfloat16), pltpu.VMEM((TP, 256), jnp.bfloat16), pltpu.VMEM((TP, 128), jnp.bfloat16), pltpu.VMEM((TP, 128), jnp.bfloat16)],
        compiler_params=pltpu.CompilerParams(vmem_limit_bytes=48 << 20),
        cost_estimate=pl.CostEstimate(flops=groups * heads * 4 * T * T * 256, bytes_accessed=T * W3 * 3, transcendentals=groups * heads * T * T),
        name="attn_fwd",
    )(packed, qa, ka)

def attn_bwd_kernel(heads, e, T, TP, W, packed_ref, do_ref, qa_ref, ka_ref, lse_ref, d_ref, q_s, k_s, v_s, do_s, dk_s, dv_s, dq_s):
    g = pl.program_id(0)
    base = pl.multiple_of(g * 128, 128)
    q_s[:, :128] = pad_rows(packed_ref[:, pl.ds(base, 128)], TP)
    q_s[:, 128:] = qa_ref[...]
    k = pad_rows(packed_ref[:, pl.ds(base + W, 128)], TP)
    k_s[...] = k
    v_s[...] = pad_rows(packed_ref[:, pl.ds(base + 2 * W, 128)], TP)
    do_s[...] = pad_rows(do_ref[...], TP)
    dk_s[...] = jnp.zeros_like(dk_s)
    dv_s[...] = jnp.zeros_like(dv_s)
    kt = k.astype(jnp.float32).T.astype(jnp.bfloat16)
    sub = lax.broadcasted_iota(jnp.int32, (128, 1), 0)
    lane = lax.broadcasted_iota(jnp.int32, (TP, 128), 1)
    scale2 = e ** -0.5 * LOG2E
    scale = e ** -0.5
    for h in range(heads):
        lo, hi = h * e, (h + 1) * e
        kk = jnp.concatenate([lane_keep(k_s[...], lo, hi), ka_ref[...]], 1)
        vh = lane_keep(v_s[...], lo, hi)
        kth = kt * jnp.where((sub >= lo) & (sub < hi), 1.0, 0.0).astype(jnp.bfloat16)

        def block(i, carry):
            rows = pl.ds(pl.multiple_of(i * QB, QB), QB)
            qb = q_s[rows, :]
            dob = do_s[rows, :]
            st = dot_nt(kk, qb) * scale2
            pt = jnp.exp2(st - lse_ref[0, h : h + 1, rows])
            dpt = dot_nt(vh, dob)
            d = jnp.sum(pt * dpt, axis=0, keepdims=True)
            dst = (pt * (dpt - d)).astype(jnp.bfloat16)
            dv = dot_nn(pt.astype(jnp.bfloat16), dob)
            dk = dot_nn(dst, qb[:, :128])
            dqt = dot_nn(kth, dst)
            mine = (lane >= lo) & (lane < hi)
            dv_s[...] += jnp.where(mine, dv, 0.0)
            dk_s[...] += jnp.where(mine, dk, 0.0)
            if h == 0:
                dq_s[:, rows] = dqt
            else:
                dq_s[:, rows] += dqt
            return 0

        lax.fori_loop(0, TP // QB, block, 0)
    dq = dq_s[...].T * scale
    d_ref[:, pl.ds(base, 128)] = dq.astype(jnp.bfloat16)[:T]
    d_ref[:, pl.ds(base + W, 128)] = (dk_s[...] * scale).astype(jnp.bfloat16)[:T]
    d_ref[:, pl.ds(base + 2 * W, 128)] = dv_s[...].astype(jnp.bfloat16)[:T]

def attn_bwd(packed, do, qa, ka, lse, heads, e):
    T, W3 = packed.shape
    W = W3 // 3
    TP = roundup(T, QB)
    groups = W // 128
    full = lambda g: (0, 0)
    return pl.pallas_call(
        functools.partial(attn_bwd_kernel, heads, e, T, TP, W),
        grid=(groups,),
        in_specs=[pl.BlockSpec((T, W3), full), pl.BlockSpec((T, 128), lambda g: (0, g)), pl.BlockSpec((TP, 128), full), pl.BlockSpec((TP, 128), full), pl.BlockSpec((1, 8, TP), lambda g: (g, 0, 0))],
        out_specs=pl.BlockSpec((T, W3), full),
        out_shape=jax.ShapeDtypeStruct((T, W3), jnp.bfloat16),
        scratch_shapes=[pltpu.VMEM((TP, 256), jnp.bfloat16), pltpu.VMEM((TP, 128), jnp.bfloat16), pltpu.VMEM((TP, 128), jnp.bfloat16), pltpu.VMEM((TP, 128), jnp.bfloat16), pltpu.VMEM((TP, 128), jnp.float32), pltpu.VMEM((TP, 128), jnp.float32), pltpu.VMEM((128, TP), jnp.float32)],
        compiler_params=pltpu.CompilerParams(vmem_limit_bytes=48 << 20),
        cost_estimate=pl.CostEstimate(flops=groups * heads * 10 * T * T * 256, bytes_accessed=T * W3 * 5, transcendentals=groups * heads * T * T),
        name="attn_bwd",
    )(packed, do, qa, ka, lse)

def mask_sides(segment, context_row, TP):
    T = segment.shape[0]
    s = jnp.arange(128)[None, :]
    one = (segment[:, None] == s)
    qa = jnp.where(one, -1e30, 0.0).astype(jnp.bfloat16)
    ka = jnp.where((s < 8) & ~(one & (context_row[:, None] > 0)), 1.0, 0.0).astype(jnp.bfloat16)
    qa = jnp.concatenate([qa, jnp.zeros((TP - T, 128), jnp.bfloat16)], 0)
    ka = jnp.concatenate([ka, jnp.broadcast_to(jnp.where(s < 8, 1.0, 0.0).astype(jnp.bfloat16), (TP - T, 128))], 0)
    return qa, ka


CHUNK = 16384
UNIT = 3 * CHUNK
SWAP = ((0, 1), (1, 0))


def swap(x):
    return lax.ppermute(x, "tensor", SWAP)


def tensor_total(part):
    return part + swap(part)


def tensor_back(part):
    low = part.astype(jnp.bfloat16)
    return low.astype(jnp.float32) + swap(low).astype(jnp.float32)


def doubling(x, axis):
    size = lax.axis_size(axis)
    if size & (size - 1):
        return lax.psum(x, axis)
    bit = 1
    while bit < size:
        x = x + lax.ppermute(x, axis, [(i, i ^ bit) for i in range(size)])
        bit *= 2
    return x


def tile_width(label):
    return {"w_qkv": 12, "w_up": 16}.get(label, 8)


def enc_chunks(ways):
    spans = []
    start = 0
    for label, height, breadth in enc_shapes(ways):
        count = height * breadth // CHUNK
        spans.append((start, start + count, breadth // 128))
        start += count
    return spans


def regions(unit, spans, emit):
    first = unit * 3
    wide = [s for s in spans if s[2] == 12]
    flat = [s for s in spans if s[2] != 12]
    in_wide = functools.reduce(jnp.logical_or, [(first >= a) & (first < b) for a, b, _ in wide])

    @pl.when(in_wide)
    def _():
        emit(0, 0, 12, 4)

    @pl.when(jnp.logical_not(in_wide))
    def _():
        for c in range(3):
            for width in (8, 16):
                hit = functools.reduce(
                    jnp.logical_or,
                    [(first + c >= a) & (first + c < b) for a, b, w in flat if w == width],
                )

                @pl.when(hit)
                def _():
                    emit(c * 128, c * 16, width, 16 // width)


def pack_kernel(spans, units, place_ref, x_ref, o_ref):
    def emit(row, tile, width, groups):
        for t in range(groups):
            for j in range(width):
                o_ref[tile + t * width + j] = x_ref[
                    pl.ds(row + t * 8 * width + j, 8, stride=width), :
                ].astype(jnp.bfloat16)

    regions(place_ref[0] * units + pl.program_id(0), spans, emit)


def pack_tiles(flat, place, spans):
    units = flat.shape[0] // 384
    return pl.pallas_call(
        functools.partial(pack_kernel, spans, units),
        grid_spec=pltpu.PrefetchScalarGridSpec(
            num_scalar_prefetch=1,
            grid=(units,),
            in_specs=[pl.BlockSpec((384, 128), lambda i, s: (i, 0))],
            out_specs=pl.BlockSpec((48, 8, 128), lambda i, s: (i, 0, 0)),
        ),
        out_shape=jax.ShapeDtypeStruct((units * 48, 8, 128), jnp.bfloat16),
        name="pack_tiles",
    )(place, flat)


def unpack_kernel(spans, units, place_ref, x_ref, o_ref, sq_ref):
    def emit(row, tile, width, groups):
        for t in range(groups):
            for j in range(width):
                o_ref[pl.ds(row + t * 8 * width + j, 8, stride=width), :] = x_ref[
                    tile + t * width + j
                ].astype(jnp.float32)

    regions(place_ref[0] * units + pl.program_id(0), spans, emit)

    @pl.when(pl.program_id(0) == 0)
    def _():
        sq_ref[...] = jnp.zeros_like(sq_ref)

    values = o_ref[...]
    sq_ref[...] += jnp.sum((values * values).reshape(48, 8, 128), axis=0)


def unpack_tiles(tiles, place, spans):
    units = tiles.shape[0] // 48
    return pl.pallas_call(
        functools.partial(unpack_kernel, spans, units),
        grid_spec=pltpu.PrefetchScalarGridSpec(
            num_scalar_prefetch=1,
            grid=(units,),
            in_specs=[pl.BlockSpec((48, 8, 128), lambda i, s: (i, 0, 0))],
            out_specs=[
                pl.BlockSpec((384, 128), lambda i, s: (i, 0)),
                pl.BlockSpec((8, 128), lambda i, s: (0, 0)),
            ],
        ),
        out_shape=[
            jax.ShapeDtypeStruct((units * 384, 128), jnp.float32),
            jax.ShapeDtypeStruct((8, 128), jnp.float32),
        ],
        name="unpack_tiles",
    )(place, tiles)


def adam_kernel(with_target, scalars, p_ref, m_ref, v_ref, g_ref, *rest):
    if with_target:
        t_ref, po_ref, mo_ref, vo_ref, to_ref = rest
    else:
        po_ref, mo_ref, vo_ref = rest
    grad = g_ref[...] * scalars[0]
    first = BETA_ONE * m_ref[...] + (1 - BETA_ONE) * grad
    second = BETA_TWO * v_ref[...] + (1 - BETA_TWO) * grad * grad
    weight = p_ref[...]
    ratio = (first * scalars[1]) / (jnp.sqrt(second * scalars[2]) + ADAM_EPS)
    weight = weight - RATE_MAT * (ratio + DECAY * weight)
    po_ref[...] = weight
    mo_ref[...] = first
    vo_ref[...] = second
    if with_target:
        to_ref[...] = TAU * t_ref[...] + (1 - TAU) * weight


def adam_flat(scalars, arrays):
    rows = arrays[0].shape[0]
    parts = next((n for n in (9, 6, 3) if rows % (8 * n) == 0), 1)
    with_target = len(arrays) == 5
    spec = pl.BlockSpec((rows // parts, 128), lambda i: (i, 0))
    n_out = 4 if with_target else 3
    return pl.pallas_call(
        functools.partial(adam_kernel, with_target),
        grid=(parts,),
        in_specs=[pl.BlockSpec(memory_space=pltpu.SMEM)] + [spec] * len(arrays),
        out_specs=[spec] * n_out,
        out_shape=[jax.ShapeDtypeStruct((rows, 128), jnp.float32)] * n_out,
        compiler_params=pltpu.CompilerParams(vmem_limit_bytes=32 << 20),
        name="adam",
    )(scalars, *arrays)


def from_tiles(full, ways):
    result = {}
    start = 0
    for label, height, breadth in enc_shapes(ways):
        count = height * breadth // 1024
        piece = full[start : start + count].reshape(height // 8, breadth // 128, 8, 128)
        result[label] = piece.transpose(0, 2, 1, 3).reshape(height, breadth)
        start += count
    return result


def to_tiles(matrix):
    height, breadth = matrix.shape
    return (
        matrix.reshape(height // 8, 8, breadth // 128, 128)
        .transpose(0, 2, 1, 3)
        .reshape(height * breadth // 1024, 8, 128)
    )


def gather_dp(x):
    return lax.all_gather(x, "dp", axis=0, tiled=True)


def gather_flat(flat, shapes):
    return unflat(gather_dp(flat.astype(jnp.bfloat16)).reshape(-1), shapes)


def scatter_flat(grads, shapes, kind):
    whole = jnp.concatenate(
        [grads[label].astype(kind).reshape(-1, 128) for label, _, _ in shapes], 0
    )
    return lax.psum_scatter(whole, "dp", scatter_dimension=0, tiled=True).astype(jnp.float32)


def permute(x, pairs):
    return lax.ppermute(x, "dp", pairs)


XOR_X = [(i, i ^ 1) for i in range(16)]
XOR_Y = [(i, i ^ 2) for i in range(16)]
RING_UP = [(i, (i + 4) % 16) for i in range(16)]
RING_DOWN = [((i + 4) % 16, i) for i in range(16)]


def pick(x, index, axis):
    return lax.dynamic_index_in_dim(x, index, axis, keepdims=False)


def plus(a, b):
    return a.astype(jnp.float32) + b.astype(jnp.float32)


def tree_scatter(tiles, planes):
    low = jnp.bfloat16
    place = lax.axis_index("dp")
    z, y, x = place // 4, place // 2 % 2, place % 2
    count = len(planes)
    copies = 4 // count
    tail = tiles.shape[1:]
    part = tiles.shape[0] // (4 * count * 2 * copies)
    grid = tiles.reshape((count, 2, 2, 2, copies * part) + tail)
    halves = []
    for side in range(2):
        axis_one = 1 if side == 0 else 2
        first_at, second_at = (y, x) if side == 0 else (x, y)
        first_ring, second_ring = (XOR_Y, XOR_X) if side == 0 else (XOR_X, XOR_Y)
        mine = grid[:, :, :, side]
        sent = permute(pick(mine, 1 - first_at, axis_one), first_ring)
        one = plus(pick(mine, first_at, axis_one), sent)
        sent = permute(pick(one, 1 - second_at, 1).astype(low), second_ring)
        two = plus(pick(one, second_at, 1), sent)
        blocks = two.reshape((count, copies, part) + tail).swapaxes(0, 1)
        blocks = blocks.reshape((4, part) + tail)
        step = 1 if side == 0 else -1
        ring = RING_UP if side == 0 else RING_DOWN
        held = pick(blocks, (z - step) % 4, 0)
        for s in range(1, 4):
            held = permute(held, ring) + pick(blocks, (z - step * (s + 1)) % 4, 0)
        pieces = []
        for c in range(copies):
            pairs = [
                ((c * count + j) * 4 + i, planes[j] * 4 + i)
                for j in range(count)
                for i in range(4)
                if c * count + j != planes[j]
            ]
            piece = permute(held.astype(low), pairs).astype(jnp.float32)
            if len(pairs) < 4 * count:
                stay = [planes[j] for j in range(count) if c * count + j == planes[j]]
                here = functools.reduce(jnp.logical_or, [z == p for p in stay])
                piece = jnp.where(here, held, piece)
            pieces.append(piece)
        halves.append(jnp.concatenate(pieces, 0))
    return jnp.concatenate(halves, 0)


def stack_tiles(pieces):
    total = sum(p.shape[0] for p in pieces)
    stacked = jnp.zeros((total,) + pieces[0].shape[1:], pieces[0].dtype)
    start = 0
    for piece in pieces:
        stacked = lax.dynamic_update_slice_in_dim(stacked, piece, start, 0)
        start += piece.shape[0]
    return stacked


def group_pad(x, axis, e, per_group):
    used = e * per_group
    shape = x.shape
    parts = x.reshape(shape[:axis] + (shape[axis] // used, used) + shape[axis + 1 :])
    widths = [(0, 0)] * parts.ndim
    widths[axis + 1] = (0, 128 - used)
    padded = jnp.pad(parts, widths)
    return padded.reshape(shape[:axis] + (shape[axis] // used * 128,) + shape[axis + 1 :])


def group_cut(x, axis, e, per_group):
    used = e * per_group
    shape = x.shape
    parts = x.reshape(shape[:axis] + (shape[axis] // 128, 128) + shape[axis + 1 :])
    parts = lax.slice_in_dim(parts, 0, used, axis=axis + 1)
    return parts.reshape(shape[:axis] + (shape[axis] // 128 * used,) + shape[axis + 1 :])


def layer_forward(stream, mats, vectors, tag, per_group, head_dim, sides, ways, member):
    normed_low = layer_norm(stream, vectors[tag + "ln1_g"], vectors[tag + "ln1_b"]).astype(
        jnp.bfloat16
    )
    bias = group_pad(
        local_columns(vectors["b_" + tag + "qkv"], True, ways, member), 0, head_dim, per_group
    )
    packed = (matmul(normed_low, mats["w_" + tag + "qkv"]) + bias).astype(jnp.bfloat16)
    mixed_rows, log_totals = attn_fwd(packed, sides[0], sides[1], per_group, head_dim)
    attn_part = matmul(mixed_rows, mats["w_" + tag + "out"])
    middle = stream + tensor_total(attn_part) + vectors["b_" + tag + "out"]
    normed_two = layer_norm(middle, vectors[tag + "ln2_g"], vectors[tag + "ln2_b"]).astype(
        jnp.bfloat16
    )
    hidden = matmul(normed_two, mats["w_" + tag + "up"]) + local_columns(
        vectors["b_" + tag + "up"], False, ways, member
    )
    activated = jax.nn.gelu(hidden).astype(jnp.bfloat16)
    down_part = matmul(activated, mats["w_" + tag + "down"])
    result = middle + tensor_total(down_part) + vectors["b_" + tag + "down"]
    kept = (
        stream,
        normed_low,
        packed,
        mixed_rows,
        log_totals,
        middle,
        normed_two,
        hidden,
        activated,
    )
    return (result, kept)


def layer_backward(grad_out, kept, mats, vectors, tag, per_group, head_dim, sides):
    (
        stream,
        normed_low,
        packed,
        mixed_rows,
        log_totals,
        middle,
        normed_two,
        hidden,
        activated,
    ) = kept
    grads = {}
    grad_low = grad_out.astype(jnp.bfloat16)
    grads["w_" + tag + "down"] = matmul_tn(activated, grad_low)
    grads["b_" + tag + "down"] = jnp.sum(grad_out, axis=0)
    grad_act = matmul_nt(grad_low, mats["w_" + tag + "down"])
    grad_hidden = jax.vjp(jax.nn.gelu, hidden)[1](grad_act)[0].astype(jnp.bfloat16)
    grads["w_" + tag + "up"] = matmul_tn(normed_two, grad_hidden)
    grads["b_" + tag + "up"] = jnp.sum(grad_hidden.astype(jnp.float32), axis=0)
    grad_normed = tensor_back(matmul_nt(grad_hidden, mats["w_" + tag + "up"]))
    grad_middle, grads[tag + "ln2_g"], grads[tag + "ln2_b"] = norm_backward(
        middle, vectors[tag + "ln2_g"], vectors[tag + "ln2_b"], grad_normed
    )
    grad_middle = grad_middle + grad_out
    grad_mid_low = grad_middle.astype(jnp.bfloat16)
    grads["w_" + tag + "out"] = group_cut(
        matmul_tn(mixed_rows, grad_mid_low), 0, head_dim, per_group
    )
    grads["b_" + tag + "out"] = jnp.sum(grad_middle, axis=0)
    grad_mixed = matmul_nt(grad_mid_low, mats["w_" + tag + "out"]).astype(jnp.bfloat16)
    grad_packed = attn_bwd(
        packed, grad_mixed, sides[0], sides[1], log_totals, per_group, head_dim
    )
    grads["w_" + tag + "qkv"] = group_cut(
        matmul_tn(normed_low, grad_packed), 1, head_dim, per_group
    )
    grads["b_" + tag + "qkv"] = group_cut(
        jnp.sum(grad_packed.astype(jnp.float32), axis=0), 0, head_dim, per_group
    )
    grad_first = tensor_back(matmul_nt(grad_packed, mats["w_" + tag + "qkv"]))
    grad_stream, grads[tag + "ln1_g"], grads[tag + "ln1_b"] = norm_backward(
        stream, vectors[tag + "ln1_g"], vectors[tag + "ln1_b"], grad_first
    )
    return (grad_stream + grad_middle, grads)


def adam(weight, first, second, grad, rate, decay, count):
    first_new = BETA_ONE * first + (1 - BETA_ONE) * grad
    second_new = BETA_TWO * second + (1 - BETA_TWO) * grad * grad
    first_hat = first_new / (1 - BETA_ONE**count)
    second_hat = second_new / (1 - BETA_TWO**count)
    weight_new = weight - rate * (first_hat / (jnp.sqrt(second_hat) + ADAM_EPS) + decay * weight)
    return (weight_new, first_new, second_new)


ENC_GROUP = 2
PRED_GROUP = 3


def shards(
    enc_params,
    enc_m1,
    enc_m2,
    pred_params,
    pred_m1,
    pred_m2,
    target_params,
    vecs,
    vec_m1,
    vec_m2,
    target_vecs,
    patches,
    segment,
    context,
    step_count,
):
    ways = lax.axis_size("tensor")
    member = lax.axis_index("tensor")
    dp_count = lax.axis_size("dp")
    place = lax.axis_index("dp").astype(jnp.int32).reshape(1)
    spans = enc_chunks(ways)
    rows = lambda x: x.reshape(-1, 128)
    tiled = dp_count == 16 and enc_params.shape[1] % UNIT == 0 and all(
        a % 3 == 0 and b % 3 == 0 for a, b, w in spans if w == 12
    )
    if tiled:
        enc_tiles = gather_dp(pack_tiles(rows(enc_params), place, spans))
        mats = from_tiles(enc_tiles, ways)
        target_tiles = pack_tiles(rows(target_params), place, spans)
    else:
        mats = gather_flat(rows(enc_params), enc_shapes(ways))
    mats.update(gather_flat(rows(pred_params), pred_shapes(ways)))
    mats["w_pqkv"] = group_pad(mats["w_pqkv"], 1, PHEAD_DIM, PRED_GROUP)
    mats["w_pout"] = group_pad(mats["w_pout"], 0, PHEAD_DIM, PRED_GROUP)
    vectors = split_vector(vecs, enc_vectors() + pred_vectors())
    target_vectors = split_vector(target_vecs, enc_vectors())
    places = positions(segment)
    context_mask = context > 0
    padded = roundup(segment.shape[0], QB)
    online_sides = mask_sides(segment, context, padded)
    all_sides = mask_sides(segment, jnp.ones_like(context), padded)
    embed_pos = sincos(places, D)

    def embed(patch_rows, weight_set, vector_set):
        return (
            tensor_total(matmul(patch_rows, weight_set["w_patch"])) + vector_set["b_patch"] + embed_pos
        )

    online_mid, online_kept = layer_forward(
        embed(patches, mats, vectors), mats, vectors, "", ENC_GROUP, HEAD_DIM, online_sides, ways, member
    )
    encoded_low = layer_norm(online_mid, vectors["lnf_g"], vectors["lnf_b"]).astype(jnp.bfloat16)
    pin_local = matmul(encoded_low, mats["w_pin"]) + local_columns(
        vectors["b_pin"], False, ways, member
    )
    pin_other = swap(pin_local)
    pin_full = jnp.where(
        member == 0,
        jnp.concatenate([pin_local, pin_other], 1),
        jnp.concatenate([pin_other, pin_local], 1),
    )
    pred_in = jnp.where(context_mask[:, None], pin_full, vectors["mask_tok"][None, :]) + sincos(
        places, PD
    )
    pred_mid, pred_kept = layer_forward(
        pred_in, mats, vectors, "p", PRED_GROUP, PHEAD_DIM, all_sides, ways, member
    )
    pred_rows = layer_norm(pred_mid, vectors["plnf_g"], vectors["plnf_b"]).astype(jnp.bfloat16)
    predicted = matmul(pred_rows, mats["w_pproj"]) + local_columns(
        vectors["b_pproj"], False, ways, member
    )
    if tiled:
        target_mats = from_tiles(gather_dp(target_tiles), ways)
    else:
        target_mats = gather_flat(rows(target_params), enc_shapes(ways))
    target_patches, predicted = lax.optimization_barrier((patches, predicted))
    target_mid, _ = layer_forward(
        embed(target_patches, target_mats, target_vectors),
        target_mats,
        target_vectors,
        "",
        ENC_GROUP,
        HEAD_DIM,
        all_sides,
        ways,
        member,
    )
    targets = plain_norm(layer_norm(target_mid, target_vectors["lnf_g"], target_vectors["lnf_b"]))
    target_cols = lax.dynamic_slice_in_dim(targets, member * (D // ways), D // ways, 1)
    target_mask = (1 - context).astype(jnp.float32)
    width = D // ways
    sums = doubling(
        jnp.concatenate(
            [
                jnp.sum(target_mask[:, None] * predicted, axis=0),
                jnp.sum(target_mask[:, None] * predicted * predicted, axis=0),
                jnp.broadcast_to(jnp.sum(target_mask), (128,)),
            ]
        ),
        "dp",
    )
    sum_all, square_all, count_all = sums[:width], sums[width : 2 * width], sums[2 * width]
    difference = predicted - target_cols
    error = jnp.sum(target_mask[:, None] * jnp.abs(difference)) / (count_all * D)
    column_mean = sum_all / count_all
    column_var = square_all / count_all - column_mean * column_mean
    spread = jnp.sqrt(column_var + VAR_EPS)
    local_loss = error + jnp.sum((spread - 1.0) ** 2) / D / dp_count
    grad_var = (spread - 1.0) / (D * spread)
    grad_pred = target_mask[:, None] * (
        jnp.sign(difference) / (count_all * D)
        + 2.0 * grad_var * (predicted - column_mean) / count_all
    )
    grads = {}
    grad_low = grad_pred.astype(jnp.bfloat16)
    grads["w_pproj"] = matmul_tn(pred_rows, grad_low)
    grads["b_pproj"] = jnp.sum(grad_pred, axis=0)
    grad_normed = tensor_back(matmul_nt(grad_low, mats["w_pproj"]))
    grad_mid, grads["plnf_g"], grads["plnf_b"] = norm_backward(
        pred_mid, vectors["plnf_g"], vectors["plnf_b"], grad_normed
    )
    grad_in, layer_grads = layer_backward(
        grad_mid, pred_kept, mats, vectors, "p", PRED_GROUP, PHEAD_DIM, all_sides
    )
    grads.update(layer_grads)
    grads["mask_tok"] = jnp.sum(jnp.where(context_mask[:, None], 0.0, grad_in), axis=0)
    grad_pin = lax.dynamic_slice_in_dim(
        jnp.where(context_mask[:, None], grad_in, 0.0), member * (PD // ways), PD // ways, 1
    )
    grad_pin_low = grad_pin.astype(jnp.bfloat16)
    grads["w_pin"] = matmul_tn(encoded_low, grad_pin_low)
    grads["b_pin"] = jnp.sum(grad_pin, axis=0)
    grad_encoded = tensor_back(matmul_nt(grad_pin_low, mats["w_pin"]))
    grad_mid, grads["lnf_g"], grads["lnf_b"] = norm_backward(
        online_mid, vectors["lnf_g"], vectors["lnf_b"], grad_encoded
    )
    pred_share = scatter_flat(grads, pred_shapes(ways), jnp.float32)
    grad_in, layer_grads = layer_backward(
        grad_mid, online_kept, mats, vectors, "", ENC_GROUP, HEAD_DIM, online_sides
    )
    grads.update(layer_grads)
    grads["w_patch"] = matmul_tn(patches, grad_in.astype(jnp.bfloat16))
    grads["b_patch"] = jnp.sum(grad_in, axis=0)
    if tiled:
        pieces = {
            label: to_tiles(grads[label].astype(jnp.bfloat16)) for label, _, _ in enc_shapes(ways)
        }
        groups = []
        quarter = sum(p.shape[0] for p in pieces.values()) // 4
        for planes in ((2, 3), (1,), (0,)):
            low, high = planes[0] * quarter, (planes[-1] + 1) * quarter
            chosen = []
            start = 0
            for label, _, _ in enc_shapes(ways):
                end = start + pieces[label].shape[0]
                if start < high and end > low:
                    chosen.append(pieces[label][max(low - start, 0) : min(high, end) - start])
                start = end
            groups.append(tree_scatter(stack_tiles(chosen), planes))
        share = jnp.where(
            place[0] >= 8, groups[0], jnp.where(place[0] >= 4, groups[1], groups[2])
        )
        enc_share, enc_square = unpack_tiles(share, place, spans)
    else:
        enc_share = scatter_flat(grads, enc_shapes(ways), jnp.float32)
        enc_square = enc_share * enc_share
    halves = []
    for label, length in enc_vectors() + pred_vectors():
        if label in LOCAL_BIAS:
            halves.append(place_columns(grads[label], length, LOCAL_BIAS[label], ways, member))
        else:
            halves.append(0.5 * grads[label])
    halves.append(jnp.broadcast_to(local_loss, (128,)))
    vector_sum = doubling(doubling(jnp.concatenate(halves), "tensor"), "dp")
    vector_grad, loss_value = vector_sum[: vecs.shape[0]], vector_sum[vecs.shape[0]]
    square_sum = jnp.sum(enc_square) + jnp.sum(pred_share * pred_share)
    square_total = doubling(doubling(jnp.broadcast_to(square_sum, (128,)), "tensor"), "dp")[0]
    grad_norm = jnp.sqrt(square_total + jnp.sum(vector_grad * vector_grad))
    factor = jnp.minimum(1.0, CLIP / (grad_norm + 1e-06))
    count = step_count[0].astype(jnp.float32)
    scalars = jnp.stack(
        [factor, 1.0 / (1 - BETA_ONE**count), 1.0 / (1 - BETA_TWO**count)]
    ).astype(jnp.float32)
    back = lambda x: x.reshape(1, -1)
    new_enc, enc_first, enc_second, new_target = map(
        back,
        adam_flat(
            scalars,
            [rows(enc_params), rows(enc_m1), rows(enc_m2), enc_share, rows(target_params)],
        ),
    )
    new_pred, pred_first, pred_second = map(
        back, adam_flat(scalars, [rows(pred_params), rows(pred_m1), rows(pred_m2), pred_share])
    )
    new_vec, vec_first, vec_second = adam(
        vecs, vec_m1, vec_m2, vector_grad * factor, RATE_VEC, 0.0, count
    )
    new_target_vec = TAU * target_vecs + (1 - TAU) * new_vec[: target_vecs.shape[0]]
    return (
        new_enc,
        enc_first,
        enc_second,
        new_enc.astype(jnp.bfloat16),
        new_pred,
        pred_first,
        pred_second,
        new_pred.astype(jnp.bfloat16),
        new_target,
        new_vec,
        vec_first,
        vec_second,
        new_target_vec,
        loss_value,
        grad_norm,
    )


def solution(mesh):
    placed = (
        P("tensor", "dp"),
        P("tensor", "dp"),
        P("tensor", "dp"),
        P("tensor", "dp"),
        P("tensor", "dp"),
        P("tensor", "dp"),
        P("tensor", "dp"),
        P(),
        P(),
        P(),
        P(),
        P("dp", "tensor"),
        P("dp"),
        P("dp"),
        P(),
    )
    return jax.shard_map(
        shards,
        mesh=mesh,
        in_specs=placed,
        out_specs=(
            P("tensor", "dp"),
            P("tensor", "dp"),
            P("tensor", "dp"),
            P("tensor", "dp"),
            P("tensor", "dp"),
            P("tensor", "dp"),
            P("tensor", "dp"),
            P("tensor", "dp"),
            P("tensor", "dp"),
            P(),
            P(),
            P(),
            P(),
            P(),
            P(),
        ),
        check_vma=False,
    )
```

```python
import functools
import math

import jax
import jax.numpy as jnp
from jax import lax
from jax.experimental import pallas as pl
from jax.experimental.pallas import tpu as pltpu
from jax.sharding import PartitionSpec as P

D = 1024
HEADS = 16
HEAD_DIM = 64
MLP = 4096
PATCH = 1536
PD = 384
PHEADS = 12
PHEAD_DIM = 32
PMLP = 1536


BETA_ONE = 0.9
BETA_TWO = 0.999
ADAM_EPS = 1e-08
RATE_MAT = 0.01
RATE_VEC = 0.05
DECAY = 0.05
CLIP = 0.0002
TAU = 0.75
NORM_EPS = 1e-06
VAR_EPS = 0.0001
LOCAL_BIAS = {
    "b_qkv": True,
    "b_pqkv": True,
    "b_up": False,
    "b_pup": False,
    "b_pin": False,
    "b_pproj": False,
}
ROW_GAINS = ("ln2_g", "ln2_b", "pln2_g", "pln2_b")


def enc_shapes(ways):
    return [
        ("w_patch", PATCH // ways, D),
        ("w_qkv", D, 3 * D // ways),
        ("w_out", D // ways, D),
        ("w_up", D, MLP // ways),
        ("w_down", MLP // ways, D),
    ]


def pred_shapes(ways):
    return [
        ("w_pin", D, PD // ways),
        ("w_pqkv", PD, 3 * PD // ways),
        ("w_pout", PD // ways, PD),
        ("w_pup", PD, PMLP // ways),
        ("w_pdown", PMLP // ways, PD),
        ("w_pproj", PD, D // ways),
    ]


def enc_vectors():
    return [
        ("b_patch", D),
        ("ln1_g", D),
        ("ln1_b", D),
        ("b_qkv", 3 * D),
        ("b_out", D),
        ("ln2_g", D),
        ("ln2_b", D),
        ("b_up", MLP),
        ("b_down", D),
        ("lnf_g", D),
        ("lnf_b", D),
    ]


def pred_vectors():
    return [
        ("b_pin", PD),
        ("mask_tok", PD),
        ("pln1_g", PD),
        ("pln1_b", PD),
        ("b_pqkv", 3 * PD),
        ("b_pout", PD),
        ("pln2_g", PD),
        ("pln2_b", PD),
        ("b_pup", PMLP),
        ("b_pdown", PD),
        ("plnf_g", PD),
        ("plnf_b", PD),
        ("b_pproj", D),
    ]


def unflat(flat_row, shapes):
    result = {}
    offset = 0
    for label, height, breadth in shapes:
        result[label] = flat_row[offset : offset + height * breadth].reshape(height, breadth)
        offset += height * breadth
    return result


def split_vector(vector, sections):
    result = {}
    offset = 0
    for label, length in sections:
        result[label] = vector[offset : offset + length]
        offset += length
    return result


def positions(segment_row):
    earlier = jnp.sum((segment_row[None, :] < segment_row[:, None]).astype(jnp.int32), axis=1)
    return (jnp.arange(segment_row.shape[0], dtype=jnp.int32) - earlier).astype(jnp.float32)


def sincos(places, width):
    half_width = width // 2
    freqs = jnp.exp(-math.log(10000.0) * jnp.arange(half_width).astype(jnp.float32) / half_width)
    angles = places[:, None] * freqs[None, :]
    return jnp.concatenate([jnp.sin(angles), jnp.cos(angles)], axis=1)


def layer_norm(values, gain, shift):
    centered = values - jnp.mean(values, axis=-1, keepdims=True)
    spread = jnp.mean(centered * centered, axis=-1, keepdims=True)
    return centered * lax.rsqrt(spread + NORM_EPS) * gain + shift


def plain_norm(values):
    centered = values - jnp.mean(values, axis=-1, keepdims=True)
    return centered * lax.rsqrt(jnp.mean(centered * centered, axis=-1, keepdims=True) + NORM_EPS)


def norm_backward(values, gain, shift, cotangent):
    return jax.vjp(layer_norm, values, gain, shift)[1](cotangent)


def matmul(left, right):
    return jnp.dot(left, right, preferred_element_type=jnp.float32)


def matmul_tn(left, right):
    return lax.dot_general(
        left, right, (((0,), (0,)), ((), ())), preferred_element_type=jnp.float32
    )


def matmul_nt(left, right):
    return lax.dot_general(
        left, right, (((1,), (1,)), ((), ())), preferred_element_type=jnp.float32
    )


def local_columns(vector, thirds, ways, member):
    if thirds:
        width = vector.shape[0] // 3
        slab = vector.reshape(3, width)
        return lax.dynamic_slice_in_dim(slab, member * (width // ways), width // ways, 1).reshape(
            -1
        )
    return lax.dynamic_slice_in_dim(
        vector, member * (vector.shape[0] // ways), vector.shape[0] // ways, 0
    )


def place_columns(local, length, thirds, ways, member):
    if thirds:
        slab = jnp.zeros((3, length // 3), jnp.float32)
        placed = lax.dynamic_update_slice_in_dim(
            slab, local.reshape(3, -1), member * (length // 3 // ways), 1
        )
        return placed.reshape(-1)
    return lax.dynamic_update_slice_in_dim(
        jnp.zeros((length,), jnp.float32), local, member * (length // ways), 0
    )


QB = 256
LOG2E = math.log2(math.e)

def roundup(n, m):
    return -(-n // m) * m

def dot_nn(a, b):
    return lax.dot_general(a, b, (((1,), (0,)), ((), ())), preferred_element_type=jnp.float32)

def dot_nt(a, b):
    return lax.dot_general(a, b, (((1,), (1,)), ((), ())), preferred_element_type=jnp.float32)

def pad_rows(x, n):
    return jnp.concatenate([x.astype(jnp.float32), jnp.zeros((n - x.shape[0], x.shape[1]), jnp.float32)], 0).astype(x.dtype)

def lane_keep(x, lo, hi):
    lane = lax.broadcasted_iota(jnp.int32, (1, x.shape[1]), 1)
    keep = jnp.where((lane >= lo) & (lane < hi), 1.0, 0.0).astype(x.dtype)
    return x * keep

def attn_fwd_kernel(heads, e, T, TP, W, packed_ref, qa_ref, ka_ref, o_ref, lse_ref, q_s, k_s, v_s, o_s, s_s, p_s):
    g = pl.program_id(0)
    base = pl.multiple_of(g * 128, 128)
    q_s[...] = pad_rows(packed_ref[:, pl.ds(base, 128)], TP)
    k_s[:, :128] = pad_rows(packed_ref[:, pl.ds(base + W, 128)], TP)
    k_s[:, 128:] = ka_ref[...]
    v_s[...] = pad_rows(packed_ref[:, pl.ds(base + 2 * W, 128)], TP)
    scale = e ** -0.5 * LOG2E
    lane = lax.broadcasted_iota(jnp.int32, (QB, 128), 1)
    step = 16
    units = [(i, h) for i in range(TP // QB) for h in range(heads)]

    def scores(n):
        i, h = units[n]
        rows = slice(i * QB, (i + 1) * QB)
        qq = jnp.concatenate([lane_keep(q_s[rows, :], h * e, (h + 1) * e), qa_ref[rows, :]], 1)
        s_s[n % 2] = dot_nt(qq, k_s[...])

    scores(0)
    for n, (i, h) in enumerate(units):
        if n + 1 < len(units):
            scores(n + 1)
        rows = slice(i * QB, (i + 1) * QB)
        peaks, totals = [], []
        for r in range(0, QB, step):
            s = s_s[n % 2, r : r + step, :] * scale
            peak = jnp.max(s, axis=1, keepdims=True)
            p = jnp.exp2(s - peak)
            total = jnp.sum(p, axis=1, keepdims=True)
            p_s[n % 2, r : r + step, :] = (p * (1.0 / total)).astype(jnp.bfloat16)
            peaks.append(peak)
            totals.append(total)
        o = dot_nn(p_s[n % 2], v_s[...])
        stat = jnp.concatenate(peaks, 0) + jnp.log2(jnp.concatenate(totals, 0))
        if h == 0:
            out = o
            stats = jnp.broadcast_to(stat, (QB, 128))
        else:
            out = jnp.where(lane < h * e, out, o)
            stats = jnp.where(lane < h, stats, stat)
        if h == heads - 1:
            if heads * e < 128:
                out = jnp.where(lane < heads * e, out, 0.0)
            o_s[rows, :] = out.astype(jnp.bfloat16)
            lse_ref[0, :, rows] = stats.T[:8, :]
    o_ref[...] = o_s[:T, :]

def attn_fwd(packed, qa, ka, heads, e):
    T, W3 = packed.shape
    W = W3 // 3
    TP = roundup(T, QB)
    groups = W // 128
    return pl.pallas_call(
        functools.partial(attn_fwd_kernel, heads, e, T, TP, W),
        grid=(groups,),
        in_specs=[pl.BlockSpec((T, W3), lambda g: (0, 0)), pl.BlockSpec((TP, 128), lambda g: (0, 0)), pl.BlockSpec((TP, 128), lambda g: (0, 0))],
        out_specs=[pl.BlockSpec((T, 128), lambda g: (0, g)), pl.BlockSpec((1, 8, TP), lambda g: (g, 0, 0))],
        out_shape=[jax.ShapeDtypeStruct((T, W), jnp.bfloat16), jax.ShapeDtypeStruct((groups, 8, TP), jnp.float32)],
        scratch_shapes=[pltpu.VMEM((TP, 128), jnp.bfloat16), pltpu.VMEM((TP, 256), jnp.bfloat16), pltpu.VMEM((TP, 128), jnp.bfloat16), pltpu.VMEM((TP, 128), jnp.bfloat16), pltpu.VMEM((2, QB, TP), jnp.float32), pltpu.VMEM((2, QB, TP), jnp.bfloat16)],
        compiler_params=pltpu.CompilerParams(vmem_limit_bytes=48 << 20),
        cost_estimate=pl.CostEstimate(flops=groups * heads * 4 * T * T * 256, bytes_accessed=T * W3 * 3, transcendentals=groups * heads * T * T),
        name="attn_fwd",
    )(packed, qa, ka)

def attn_bwd_kernel(heads, e, T, TP, W, first, chained, packed_ref, do_ref, qa_ref, ka_ref, lse_ref, *rest):
    d_ref, q_s, k_s, v_s, do_s, dk_s, dv_s, dq_s, out_s, s_s, d_s, p_s, ds_s, sems = rest[1:] if chained else rest
    g = pl.program_id(0) + first
    base = pl.multiple_of(g * 128, 128)
    q_s[:, :128] = pad_rows(packed_ref[:, pl.ds(base, 128)], TP)
    q_s[:, 128:] = qa_ref[...]
    k = pad_rows(packed_ref[:, pl.ds(base + W, 128)], TP)
    k_s[...] = k
    v_s[...] = pad_rows(packed_ref[:, pl.ds(base + 2 * W, 128)], TP)
    do_s[...] = pad_rows(do_ref[...], TP)
    kt = k.astype(jnp.float32).T.astype(jnp.bfloat16)
    sub = lax.broadcasted_iota(jnp.int32, (128, 1), 0)
    lane = lax.broadcasted_iota(jnp.int32, (TP, 128), 1)
    scale2 = e ** -0.5 * LOG2E
    scale = e ** -0.5
    step = 64
    blocks = TP // QB
    units = [(h, i) for h in range(heads) for i in range(blocks)]

    def products(n):
        h, i = units[n]
        rows = slice(i * QB, (i + 1) * QB)
        lo, hi = h * e, (h + 1) * e
        kk = jnp.concatenate([lane_keep(k_s[...], lo, hi), ka_ref[...]], 1)
        s_s[n % 2] = dot_nt(kk, q_s[rows, :])
        d_s[n % 2] = dot_nt(lane_keep(v_s[...], lo, hi), do_s[rows, :])

    def gather(h):
        lo, hi = h * e, (h + 1) * e
        dv = dot_nn(p_s[h % 2], do_s[...])
        dk = dot_nn(ds_s[h % 2], q_s[:, :128])
        dq = dot_nn(kt * jnp.where((sub >= lo) & (sub < hi), 1.0, 0.0).astype(jnp.bfloat16), ds_s[h % 2])
        if h == 0:
            dv_s[...], dk_s[...], dq_s[...] = dv, dk, dq
        else:
            dv_s[...] = jnp.where(lane < lo, dv_s[...], dv)
            dk_s[...] = jnp.where(lane < lo, dk_s[...], dk)
            dq_s[...] += dq

    products(0)
    for n, (h, i) in enumerate(units):
        if n + 1 < len(units):
            products(n + 1)
        rows = slice(i * QB, (i + 1) * QB)
        lse = lse_ref[0, h : h + 1, rows]
        d = jnp.zeros((8, QB), jnp.float32)
        for r in range(0, TP, step):
            part = slice(r, r + step)
            pt = jnp.exp2(s_s[n % 2, part, :] * scale2 - lse)
            s_s[n % 2, part, :] = pt
            p_s[h % 2, part, rows] = pt.astype(jnp.bfloat16)
            d += jnp.sum((pt * d_s[n % 2, part, :]).reshape(step // 8, 8, QB), axis=0)
        d = jnp.sum(d, axis=0, keepdims=True)
        for r in range(0, TP, step):
            part = slice(r, r + step)
            ds_s[h % 2, part, rows] = (s_s[n % 2, part, :] * (d_s[n % 2, part, :] - d)).astype(jnp.bfloat16)
        if h and i == 0:
            gather(h - 1)
    gather(heads - 1)
    if heads * e < 128:
        dv_s[...] = jnp.where(lane < heads * e, dv_s[...], 0.0)
        dk_s[...] = jnp.where(lane < heads * e, dk_s[...], 0.0)
    dq = dq_s[...].T * scale
    out_s[0] = dq.astype(jnp.bfloat16)[:T]
    out_s[1] = (dk_s[...] * scale).astype(jnp.bfloat16)[:T]
    out_s[2] = dv_s[...].astype(jnp.bfloat16)[:T]
    copies = [
        pltpu.make_async_copy(out_s.at[i], d_ref.at[:, pl.ds(base + i * W, 128)], sems.at[i])
        for i in range(3)
    ]
    for copy in copies:
        copy.start()
    for copy in copies:
        copy.wait()

def attn_bwd(packed, do, qa, ka, lse, heads, e, first=0, groups=None, so_far=None):
    T, W3 = packed.shape
    W = W3 // 3
    TP = roundup(T, QB)
    groups = W // 128 if groups is None else groups
    chained = so_far is not None
    full = lambda g: (0, 0)
    return pl.pallas_call(
        functools.partial(attn_bwd_kernel, heads, e, T, TP, W, first, chained),
        grid=(groups,),
        in_specs=[pl.BlockSpec((T, W3), full), pl.BlockSpec((T, 128), lambda g: (0, g + first)), pl.BlockSpec((TP, 128), full), pl.BlockSpec((TP, 128), full), pl.BlockSpec((1, 8, TP), lambda g: (g + first, 0, 0))]
        + ([pl.BlockSpec(memory_space=pl.ANY)] if chained else []),
        out_specs=pl.BlockSpec(memory_space=pl.ANY),
        input_output_aliases={5: 0} if chained else {},
        out_shape=jax.ShapeDtypeStruct((T, W3), jnp.bfloat16),
        scratch_shapes=[pltpu.VMEM((TP, 256), jnp.bfloat16), pltpu.VMEM((TP, 128), jnp.bfloat16), pltpu.VMEM((TP, 128), jnp.bfloat16), pltpu.VMEM((TP, 128), jnp.bfloat16), pltpu.VMEM((TP, 128), jnp.float32), pltpu.VMEM((TP, 128), jnp.float32), pltpu.VMEM((128, TP), jnp.float32), pltpu.VMEM((3, T, 128), jnp.bfloat16), pltpu.VMEM((2, TP, QB), jnp.float32), pltpu.VMEM((2, TP, QB), jnp.float32), pltpu.VMEM((2, TP, TP), jnp.bfloat16), pltpu.VMEM((2, TP, TP), jnp.bfloat16), pltpu.SemaphoreType.DMA((3,))],
        compiler_params=pltpu.CompilerParams(vmem_limit_bytes=48 << 20),
        cost_estimate=pl.CostEstimate(flops=groups * heads * 10 * T * T * 256, bytes_accessed=T * W3 * 5, transcendentals=groups * heads * T * T),
        name="attn_bwd",
    )(packed, do, qa, ka, lse, *([so_far] if chained else []))

def mask_sides(segment, context_row, TP):
    T = segment.shape[0]
    s = jnp.arange(128)[None, :]
    one = (segment[:, None] == s)
    qa = jnp.where(one, -1e30, 0.0).astype(jnp.bfloat16)
    ka = jnp.where((s < 8) & ~(one & (context_row[:, None] > 0)), 1.0, 0.0).astype(jnp.bfloat16)
    qa = jnp.concatenate([qa, jnp.zeros((TP - T, 128), jnp.bfloat16)], 0)
    ka = jnp.concatenate([ka, jnp.broadcast_to(jnp.where(s < 8, 1.0, 0.0).astype(jnp.bfloat16), (TP - T, 128))], 0)
    return qa, ka


CHUNK = 16384
UNIT = 3 * CHUNK
SWAP = ((0, 1), (1, 0))


def swap(x):
    return lax.ppermute(x, "tensor", SWAP)


def tensor_total(part):
    return part + swap(part)


def tensor_back(part):
    low = part.astype(jnp.bfloat16)
    return low.astype(jnp.float32) + swap(low).astype(jnp.float32)


def doubling(x, axis, after=None):
    size = lax.axis_size(axis)
    if size & (size - 1):
        return lax.psum(x, axis)
    stride = 1
    while stride < size:
        reach = 4 if size // stride % 4 == 0 else 2
        others = [
            lax.ppermute(x, axis, [(i, i ^ (m * stride)) for i in range(size)])
            for m in range(1, reach)
        ]
        if stride * reach >= size:
            others = pin(others, after)
        x = x + others[0]
        if reach == 4:
            x = x + (others[1] + others[2])
        stride *= reach
    return x


def pin(x, after):
    return x if after is None else lax.optimization_barrier((x, after))[0]


def tile_width(label):
    return {"w_qkv": 12, "w_up": 16}.get(label, 8)


def enc_chunks(ways):
    spans = []
    start = 0
    for label, height, breadth in enc_shapes(ways):
        count = height * breadth // CHUNK
        spans.append((start, start + count, breadth // 128))
        start += count
    return spans


def regions(unit, spans, emit):
    first = unit * 3
    wide = [s for s in spans if s[2] == 12]
    flat = [s for s in spans if s[2] != 12]
    in_wide = functools.reduce(jnp.logical_or, [(first >= a) & (first < b) for a, b, _ in wide])

    @pl.when(in_wide)
    def _():
        emit(0, 0, 12, 4)

    @pl.when(jnp.logical_not(in_wide))
    def _():
        for c in range(3):
            for width in (8, 16):
                hit = functools.reduce(
                    jnp.logical_or,
                    [(first + c >= a) & (first + c < b) for a, b, w in flat if w == width],
                )

                @pl.when(hit)
                def _():
                    emit(c * 128, c * 16, width, 16 // width)


def pack_kernel(spans, units, place_ref, x_ref, o_ref):
    def emit(row, tile, width, groups):
        for t in range(groups):
            for j in range(width):
                o_ref[tile + t * width + j] = x_ref[
                    pl.ds(row + t * 8 * width + j, 8, stride=width), :
                ].astype(jnp.bfloat16)

    regions(place_ref[0] * units + pl.program_id(0), spans, emit)


def pack_tiles(flat, place, spans):
    units = flat.shape[0] // 384
    return pl.pallas_call(
        functools.partial(pack_kernel, spans, units),
        grid_spec=pltpu.PrefetchScalarGridSpec(
            num_scalar_prefetch=1,
            grid=(units,),
            in_specs=[pl.BlockSpec((384, 128), lambda i, s: (i, 0))],
            out_specs=pl.BlockSpec((48, 8, 128), lambda i, s: (i, 0, 0)),
        ),
        out_shape=jax.ShapeDtypeStruct((units * 48, 8, 128), jnp.bfloat16),
        name="pack",
    )(place, flat)


def unpack_kernel(spans, units, place_ref, x_ref, o_ref):
    def emit(row, tile, width, groups):
        for t in range(groups):
            for j in range(width):
                o_ref[pl.ds(row + t * 8 * width + j, 8, stride=width), :] = x_ref[
                    tile + t * width + j
                ].astype(jnp.float32)

    regions(place_ref[0] * units + pl.program_id(0), spans, emit)


def unpack_tiles(tiles, place, spans):
    units = tiles.shape[0] // 48
    return pl.pallas_call(
        functools.partial(unpack_kernel, spans, units),
        grid_spec=pltpu.PrefetchScalarGridSpec(
            num_scalar_prefetch=1,
            grid=(units,),
            in_specs=[pl.BlockSpec((48, 8, 128), lambda i, s: (i, 0, 0))],
            out_specs=pl.BlockSpec((384, 128), lambda i, s: (i, 0)),
        ),
        out_shape=jax.ShapeDtypeStruct((units * 384, 128), jnp.float32),
        name="unpack",
    )(place, tiles)


def adam_kernel(with_target, scalars, p_ref, m_ref, v_ref, g_ref, *rest):
    if with_target:
        t_ref, po_ref, mo_ref, vo_ref, to_ref = rest
    else:
        po_ref, mo_ref, vo_ref = rest
    grad = g_ref[...] * scalars[0]
    first = BETA_ONE * m_ref[...] + (1 - BETA_ONE) * grad
    second = BETA_TWO * v_ref[...] + (1 - BETA_TWO) * grad * grad
    weight = p_ref[...]
    ratio = (first * scalars[1]) / (jnp.sqrt(second * scalars[2]) + ADAM_EPS)
    weight = weight - RATE_MAT * (ratio + DECAY * weight)
    po_ref[...] = weight
    mo_ref[...] = first
    vo_ref[...] = second
    if with_target:
        to_ref[...] = TAU * t_ref[...] + (1 - TAU) * weight


def adam_flat(scalars, arrays):
    rows = arrays[0].shape[0]
    parts = next((n for n in (9, 6, 3) if rows % (8 * n) == 0), 1)
    with_target = len(arrays) == 5
    spec = pl.BlockSpec((rows // parts, 128), lambda i: (i, 0))
    n_out = 4 if with_target else 3
    return pl.pallas_call(
        functools.partial(adam_kernel, with_target),
        grid=(parts,),
        in_specs=[pl.BlockSpec(memory_space=pltpu.SMEM)] + [spec] * len(arrays),
        out_specs=[spec] * n_out,
        out_shape=[jax.ShapeDtypeStruct((rows, 128), jnp.float32)] * n_out,
        compiler_params=pltpu.CompilerParams(vmem_limit_bytes=32 << 20),
        name="adam",
    )(scalars, *arrays)


def from_tiles(parts, ways):
    result = {}
    for tiles, (label, height, breadth) in zip(parts, enc_shapes(ways)):
        piece = tiles.reshape(height // 8, breadth // 128, 8, 128)
        result[label] = piece.transpose(0, 2, 1, 3).reshape(height, breadth)
    return result


def to_tiles(matrix):
    height, breadth = matrix.shape
    return (
        matrix.reshape(height // 8, 8, breadth // 128, 128)
        .transpose(0, 2, 1, 3)
        .reshape(height * breadth // 1024, 8, 128)
    )


def gather_dp(x):
    return lax.all_gather(x, "dp", axis=0, tiled=True)


def split_gathered(gathered, sizes, part, first, total):
    results = []
    start = 0
    for size in sizes:
        moves = []
        for device in range(gathered.shape[0] // total):
            low, high = max(start, device * part), min(start + size, (device + 1) * part)
            if low < high:
                source = device * total + first + low - device * part
                moves.append((0, source, low - start, high - low))
        results.append(copy_tiles([gathered], moves, size, pltpu.HBM, 52))
        start += size
    return results


def gather_flat(flat, shapes):
    return unflat(gather_dp(flat.astype(jnp.bfloat16)).reshape(-1), shapes)


def flat_kernel(shapes, *refs):
    ins, out, column = refs[:-2], refs[-2], refs[-1]

    def by_turns(ref, first, width, height):
        column[:height, :width] = ref[:, first : first + width]
        pairs = height // 2
        return column[pl.ds(0, pairs, stride=2), :], column[pl.ds(1, pairs, stride=2), :]

    base = 0
    for ref, (height, breadth) in zip(ins, shapes):
        full = breadth // 128
        if breadth % 128 == 0:
            for j in range(full):
                out[pl.ds(base + j, height, stride=full), :] = ref[:, j * 128 : (j + 1) * 128]
        else:
            pairs = height // 2
            step = 2 * full + 1
            even, odd = zip(*[by_turns(ref, j * 128, 128, height) for j in range(full)])
            even_end, odd_end = [e[:, :64] for e in by_turns(ref, full * 128, 64, height)]
            rows = list(even) + [jnp.concatenate([even_end, odd[0][:, :64]], 1)]
            for j in range(full):
                after = odd[j + 1][:, :64] if j + 1 < full else odd_end
                rows.append(jnp.concatenate([odd[j][:, 64:], after], 1))
            for j, row in enumerate(rows):
                out[pl.ds(base + j, pairs, stride=step), :] = row
        base += height * breadth // 128


def flatten_matrices(matrices):
    shapes = [m.shape for m in matrices]
    total = sum(h * b for h, b in shapes) // 128
    return pl.pallas_call(
        functools.partial(flat_kernel, shapes),
        in_specs=[pl.BlockSpec(memory_space=pltpu.VMEM)] * len(matrices),
        out_specs=pl.BlockSpec(memory_space=pltpu.VMEM),
        out_shape=jax.ShapeDtypeStruct((total, 128), jnp.float32),
        scratch_shapes=[pltpu.VMEM((max(h for h, _ in shapes), 128), jnp.float32)],
        compiler_params=pltpu.CompilerParams(vmem_limit_bytes=40 << 20),
        name="flatten",
    )(*matrices)


def scatter_flat(grads, shapes, kind):
    whole = jnp.concatenate(
        [grads[label].astype(kind).reshape(-1, 128) for label, _, _ in shapes], 0
    )
    return lax.psum_scatter(whole, "dp", scatter_dimension=0, tiled=True).astype(jnp.float32)


def permute(x, pairs):
    return lax.ppermute(x, "dp", pairs)


ENC_TILES = [(label, height * breadth // 1024) for label, height, breadth in enc_shapes(2)]


def plus(a, b):
    return a.astype(jnp.float32) + b.astype(jnp.float32)


def pick(x, index, axis):
    return lax.dynamic_index_in_dim(x, index, axis, keepdims=False)


def stack_kernel(moves, count, *refs):
    ins, out, sems = refs[:count], refs[count], refs[count + 1]
    copies = [
        pltpu.make_async_copy(
            ins[source].at[pl.ds(first, length)], out.at[pl.ds(target, length)], sems.at[number]
        )
        for number, (source, first, target, length) in enumerate(moves)
    ]
    for copy in copies:
        copy.start()
    for copy in copies:
        copy.wait()


def copy_tiles(sources, moves, length, space=pl.ANY, room=24):
    return pl.pallas_call(
        functools.partial(stack_kernel, moves, len(sources)),
        in_specs=[pl.BlockSpec(memory_space=space)] * len(sources),
        out_specs=pl.BlockSpec(memory_space=pltpu.VMEM),
        out_shape=jax.ShapeDtypeStruct((length, 8, 128), jnp.bfloat16),
        scratch_shapes=[pltpu.SemaphoreType.DMA((len(moves),))],
        compiler_params=pltpu.CompilerParams(vmem_limit_bytes=room << 20),
        name="stack",
    )(*sources)


def stack_tiles(pieces, planes):
    shard = sum(size for _, size in ENC_TILES) // 16
    low, high = planes[0] * 4 * shard, (planes[-1] + 1) * 4 * shard
    moves, used = [], []
    start = 0
    for label, size in ENC_TILES:
        first, last = max(low, start), min(high, start + size)
        if first < last:
            moves.append((len(used), first - start, first - low, last - first))
            used.append(pieces[label])
        start += size
    return copy_tiles(used, moves, high - low)


def tree_scatter(tiles, planes):
    low = jnp.bfloat16
    place = lax.axis_index("dp")
    z, near = place // 4, place % 4
    count = len(planes)
    copies = 4 // count
    size = tiles.shape[0] // (4 * count * copies)
    grid = tiles.reshape((count, 4, copies, size) + tiles.shape[1:])

    def exchange(take, at, stride):
        ready = [take(at ^ m) for m in range(1, 4)]
        sent = [
            permute(ready[m - 1], [(i, i ^ (m * stride)) for i in range(16)]) for m in range(1, 4)
        ]
        return ready, sent

    ready, sent = exchange(lambda n: pick(grid, n, 1).astype(low), near, 1)
    after = yield ready
    sent = pin(sent, after)
    plane_sum = sum(part.astype(jnp.float32) for part in [pick(grid, near, 1)] + sent)
    blocks = plane_sum.swapaxes(0, 1).reshape((4, size) + tiles.shape[1:])
    ready, sent = exchange(lambda n: pick(blocks, n, 0).astype(low), z, 4)
    after = yield ready
    sent = pin(sent, after)
    held = sum(part.astype(jnp.float32) for part in [pick(blocks, z, 0)] + sent)
    if copies == 1:
        yield held
    held = held.astype(low)
    got = []
    for c in range(copies):
        pairs = [
            ((c * count + j) * 4 + i, planes[j] * 4 + i)
            for j in range(count)
            for i in range(4)
            if c * count + j != planes[j]
        ]
        stay = [planes[j] for j in range(count) if c * count + j == planes[j]]
        piece = permute(held, pairs) if pairs else held
        if pairs and stay:
            piece = jnp.where(functools.reduce(jnp.logical_or, [z == p for p in stay]), held, piece)
        got.append(piece)
    after = yield [held]
    yield jnp.concatenate(pin(got, after), 0)


def advance(tree, after):
    return tree.send(after)


def group_pad(x, axis, e, per_group):
    used = e * per_group
    shape = x.shape
    parts = x.reshape(shape[:axis] + (shape[axis] // used, used) + shape[axis + 1 :])
    widths = [(0, 0)] * parts.ndim
    widths[axis + 1] = (0, 128 - used)
    padded = jnp.pad(parts, widths)
    return padded.reshape(shape[:axis] + (shape[axis] // used * 128,) + shape[axis + 1 :])


def group_cut(x, axis, e, per_group):
    used = e * per_group
    shape = x.shape
    parts = x.reshape(shape[:axis] + (shape[axis] // 128, 128) + shape[axis + 1 :])
    parts = lax.slice_in_dim(parts, 0, used, axis=axis + 1)
    return parts.reshape(shape[:axis] + (shape[axis] // 128 * used,) + shape[axis + 1 :])


def layer_forward(
    stream, mats, vectors, tag, per_group, head_dim, sides, ways, member, watch=lambda value: None
):
    normed_low = layer_norm(stream, vectors[tag + "ln1_g"], vectors[tag + "ln1_b"]).astype(
        jnp.bfloat16
    )
    bias = group_pad(
        local_columns(vectors["b_" + tag + "qkv"], True, ways, member), 0, head_dim, per_group
    )
    packed = (matmul(normed_low, mats["w_" + tag + "qkv"]) + bias).astype(jnp.bfloat16)
    mixed_rows, log_totals = attn_fwd(packed, sides[0], sides[1], per_group, head_dim)
    attn_part = matmul(mixed_rows, mats["w_" + tag + "out"])
    middle = stream + tensor_total(attn_part) + vectors["b_" + tag + "out"]
    normed_two = layer_norm(middle, vectors[tag + "ln2_g"], vectors[tag + "ln2_b"]).astype(
        jnp.bfloat16
    )
    normed_two = pin(normed_two, watch(normed_two))
    hidden = matmul(normed_two, mats["w_" + tag + "up"]) + local_columns(
        vectors["b_" + tag + "up"], False, ways, member
    )
    activated = lax.optimization_barrier(jax.nn.gelu(hidden).astype(jnp.bfloat16))
    down_part = matmul(activated, mats["w_" + tag + "down"])
    result = middle + tensor_total(down_part) + vectors["b_" + tag + "down"]
    kept = (
        stream,
        normed_low,
        packed,
        mixed_rows,
        log_totals,
        middle,
        normed_two,
        hidden,
        activated,
    )
    return (result, kept)


def layer_backward(grad_out, kept, mats, vectors, tag, per_group, head_dim, sides, watch):
    (
        stream,
        normed_low,
        packed,
        mixed_rows,
        log_totals,
        middle,
        normed_two,
        hidden,
        activated,
    ) = kept
    grads = {}
    grad_low = grad_out.astype(jnp.bfloat16)
    grads["w_" + tag + "down"] = matmul_tn(activated, grad_low)
    grads["b_" + tag + "down"] = jnp.sum(grad_out, axis=0)
    grad_act = matmul_nt(grad_low, mats["w_" + tag + "down"])
    grad_hidden = jax.vjp(jax.nn.gelu, hidden)[1](grad_act)[0].astype(jnp.bfloat16)
    grads["w_" + tag + "up"] = matmul_tn(normed_two, grad_hidden)
    grads["b_" + tag + "up"] = jnp.sum(grad_hidden.astype(jnp.float32), axis=0)
    grad_hidden = pin(grad_hidden, watch(AT_HIDDEN, grads, grad_hidden))
    grad_normed = tensor_back(matmul_nt(grad_hidden, mats["w_" + tag + "up"]))
    grad_middle, grads[tag + "ln2_g"], grads[tag + "ln2_b"] = norm_backward(
        middle, vectors[tag + "ln2_g"], vectors[tag + "ln2_b"], grad_normed
    )
    grad_middle = grad_middle + grad_out
    grad_mid_low = grad_middle.astype(jnp.bfloat16)
    grads["w_" + tag + "out"] = group_cut(
        matmul_tn(mixed_rows, grad_mid_low), 0, head_dim, per_group
    )
    grads["b_" + tag + "out"] = jnp.sum(grad_middle, axis=0)
    grad_mixed = matmul_nt(grad_mid_low, mats["w_" + tag + "out"]).astype(jnp.bfloat16)
    groups = packed.shape[1] // 384
    if tag:
        grad_packed = attn_bwd(
            packed, grad_mixed, sides[0], sides[1], log_totals, per_group, head_dim
        )
    else:
        grad_packed = attn_bwd(
            packed,
            grad_mixed,
            sides[0],
            sides[1],
            log_totals,
            per_group,
            head_dim,
            groups=groups // 2,
        )
        grad_mixed = pin(grad_mixed, watch(AT_HALF, grads, grad_packed))
        grad_packed = attn_bwd(
            packed,
            grad_mixed,
            sides[0],
            sides[1],
            log_totals,
            per_group,
            head_dim,
            first=groups // 2,
            groups=groups // 2,
            so_far=grad_packed,
        )
    grads["w_" + tag + "qkv"] = group_cut(
        matmul_tn(normed_low, grad_packed), 1, head_dim, per_group
    )
    grads["b_" + tag + "qkv"] = group_cut(
        jnp.sum(grad_packed.astype(jnp.float32), axis=0), 0, head_dim, per_group
    )
    grad_packed = pin(grad_packed, watch(AT_PACKED, grads, grad_packed))
    first_part = matmul_nt(grad_packed, mats["w_" + tag + "qkv"]).astype(jnp.bfloat16)
    first_part = pin(first_part, watch(AT_PART, grads, first_part))
    grad_first = tensor_back(first_part)
    grad_first = pin(grad_first, watch(AT_FIRST, grads, grad_first))
    grad_stream, grads[tag + "ln1_g"], grads[tag + "ln1_b"] = norm_backward(
        stream, vectors[tag + "ln1_g"], vectors[tag + "ln1_b"], grad_first
    )
    return (grad_stream + grad_middle, grads)


def adam(weight, first, second, grad, rate, decay, count):
    first_new = BETA_ONE * first + (1 - BETA_ONE) * grad
    second_new = BETA_TWO * second + (1 - BETA_TWO) * grad * grad
    first_hat = first_new / (1 - BETA_ONE**count)
    second_hat = second_new / (1 - BETA_TWO**count)
    weight_new = weight - rate * (first_hat / (jnp.sqrt(second_hat) + ADAM_EPS) + decay * weight)
    return (weight_new, first_new, second_new)


UPPER, MIDDLE, LOWER = range(3)
AT_HIDDEN, AT_HALF, AT_PACKED, AT_PART, AT_FIRST = range(5)
SQUARE, LOSS = range(2)
ENC_GROUP = 2
PRED_GROUP = 3


def shards(
    enc_params,
    enc_m1,
    enc_m2,
    pred_params,
    pred_m1,
    pred_m2,
    target_params,
    vecs,
    vec_m1,
    vec_m2,
    target_vecs,
    patches,
    segment,
    context,
    step_count,
):
    ways = lax.axis_size("tensor")
    member = lax.axis_index("tensor")
    dp_count = lax.axis_size("dp")
    place = lax.axis_index("dp").astype(jnp.int32).reshape(1)
    spans = enc_chunks(ways)
    rows = lambda x: x.reshape(-1, 128)
    tiled = dp_count == 16 and enc_params.shape[1] % UNIT == 0 and all(
        a % 3 == 0 and b % 3 == 0 for a, b, w in spans if w == 12
    )
    vectors = split_vector(vecs, enc_vectors() + pred_vectors())
    target_vectors = split_vector(target_vecs, enc_vectors())
    places = positions(segment)
    context_mask = context > 0
    padded = roundup(segment.shape[0], QB)
    online_sides = mask_sides(segment, context, padded)
    all_sides = mask_sides(segment, jnp.ones_like(context), padded)
    embed_pos = sincos(places, D)
    pred_pos = sincos(places, PD)
    if tiled:
        pred_tiles = rows(pred_params).astype(jnp.bfloat16).reshape(-1, 8, 128)
        own_tiles = jnp.concatenate([pack_tiles(rows(enc_params), place, spans), pred_tiles], 0)
        enc_tiles = gather_dp(own_tiles)
        target_tiles = pack_tiles(rows(target_params), place, spans)
        enc_tiles, target_tiles, embed_pos, pred_pos, online_sides, all_sides = (
            lax.optimization_barrier(
                (enc_tiles, target_tiles, embed_pos, pred_pos, online_sides, all_sides)
            )
        )
        sizes = [size for _, size in ENC_TILES]
        shard, both = sum(sizes) // 16, own_tiles.shape[0]
        mats = from_tiles(split_gathered(enc_tiles, sizes, shard, 0, both), ways)
        pred_count = [16 * (both - shard)]
        pred_whole = split_gathered(enc_tiles, pred_count, both - shard, shard, both)[0]
    else:
        mats = gather_flat(rows(enc_params), enc_shapes(ways))
    def embed(patch_rows, weight_set, vector_set):
        return (
            tensor_total(matmul(patch_rows, weight_set["w_patch"])) + vector_set["b_patch"] + embed_pos
        )

    online_mid, online_kept = layer_forward(
        embed(patches, mats, vectors),
        mats,
        vectors,
        "",
        ENC_GROUP,
        HEAD_DIM,
        online_sides,
        ways,
        member,
    )
    if tiled:
        mats.update(unflat(pred_whole.reshape(-1), pred_shapes(ways)))
    else:
        mats.update(gather_flat(rows(pred_params), pred_shapes(ways)))
    mats["w_pqkv"] = group_pad(mats["w_pqkv"], 1, PHEAD_DIM, PRED_GROUP)
    mats["w_pout"] = group_pad(mats["w_pout"], 0, PHEAD_DIM, PRED_GROUP)
    encoded_low = layer_norm(online_mid, vectors["lnf_g"], vectors["lnf_b"]).astype(jnp.bfloat16)
    pin_local = matmul(encoded_low, mats["w_pin"]) + local_columns(
        vectors["b_pin"], False, ways, member
    )
    pin_other = swap(pin_local)
    pin_full = jnp.where(
        member == 0,
        jnp.concatenate([pin_local, pin_other], 1),
        jnp.concatenate([pin_other, pin_local], 1),
    )
    pred_in = jnp.where(context_mask[:, None], pin_full, vectors["mask_tok"][None, :])
    pred_in = pred_in + pred_pos
    if tiled:
        target_whole = gather_dp(target_tiles)
    pred_mid, pred_kept = layer_forward(
        pred_in,
        mats,
        vectors,
        "p",
        PRED_GROUP,
        PHEAD_DIM,
        all_sides,
        ways,
        member,
        (lambda value: target_whole) if tiled else (lambda value: None),
    )
    pred_rows = layer_norm(pred_mid, vectors["plnf_g"], vectors["plnf_b"]).astype(jnp.bfloat16)
    predicted = matmul(pred_rows, mats["w_pproj"]) + local_columns(
        vectors["b_pproj"], False, ways, member
    )
    if tiled:
        target_mats = from_tiles(split_gathered(target_whole, sizes, shard, 0, shard), ways)
    else:
        target_mats = gather_flat(rows(target_params), enc_shapes(ways))
    target_patches, predicted = lax.optimization_barrier((patches, predicted))
    target_mid, _ = layer_forward(
        embed(target_patches, target_mats, target_vectors),
        target_mats,
        target_vectors,
        "",
        ENC_GROUP,
        HEAD_DIM,
        all_sides,
        ways,
        member,
    )
    targets = plain_norm(layer_norm(target_mid, target_vectors["lnf_g"], target_vectors["lnf_b"]))
    target_cols = lax.dynamic_slice_in_dim(targets, member * (D // ways), D // ways, 1)
    target_mask = (1 - context).astype(jnp.float32)
    width = D // ways
    sums = doubling(
        jnp.concatenate(
            [
                jnp.sum(target_mask[:, None] * predicted, axis=0),
                jnp.sum(target_mask[:, None] * predicted * predicted, axis=0),
                jnp.broadcast_to(jnp.sum(target_mask), (128,)),
            ]
        ),
        "dp",
    )
    sum_all, square_all, count_all = sums[:width], sums[width : 2 * width], sums[2 * width]
    difference = predicted - target_cols
    error = jnp.sum(target_mask[:, None] * jnp.abs(difference)) / (count_all * D)
    column_mean = sum_all / count_all
    column_var = square_all / count_all - column_mean * column_mean
    spread = jnp.sqrt(column_var + VAR_EPS)
    local_loss = error + jnp.sum((spread - 1.0) ** 2) / D / dp_count
    grad_var = (spread - 1.0) / (D * spread)
    grad_pred = target_mask[:, None] * (
        jnp.sign(difference) / (count_all * D)
        + 2.0 * grad_var * (predicted - column_mean) / count_all
    )
    grads = {}
    grad_low = grad_pred.astype(jnp.bfloat16)
    grads["w_pproj"] = matmul_tn(pred_rows, grad_low)
    grads["b_pproj"] = jnp.sum(grad_pred, axis=0)
    grad_normed = tensor_back(matmul_nt(grad_low, mats["w_pproj"]))
    grad_mid, grads["plnf_g"], grads["plnf_b"] = norm_backward(
        pred_mid, vectors["plnf_g"], vectors["plnf_b"], grad_normed
    )
    grad_in, layer_grads = layer_backward(
        grad_mid, pred_kept, mats, vectors, "p", PRED_GROUP, PHEAD_DIM, all_sides, lambda *_: None
    )
    grads.update(layer_grads)
    grads["mask_tok"] = jnp.sum(jnp.where(context_mask[:, None], 0.0, grad_in), axis=0)
    grad_pin = lax.dynamic_slice_in_dim(
        jnp.where(context_mask[:, None], grad_in, 0.0), member * (PD // ways), PD // ways, 1
    )
    grad_pin_low = grad_pin.astype(jnp.bfloat16)
    grads["w_pin"] = matmul_tn(encoded_low, grad_pin_low)
    grads["b_pin"] = jnp.sum(grad_pin, axis=0)
    grad_encoded = tensor_back(matmul_nt(grad_pin_low, mats["w_pin"]))
    grad_mid, grads["lnf_g"], grads["lnf_b"] = norm_backward(
        online_mid, vectors["lnf_g"], vectors["lnf_b"], grad_encoded
    )
    pred_flat = flatten_matrices([grads[label] for label, _, _ in pred_shapes(ways)])
    pred_flat, grad_mid = lax.optimization_barrier((pred_flat, grad_mid))
    pred_share = None
    if tiled:
        pred_tree = tree_scatter(pred_flat.reshape(-1, 8, 128), (0, 1, 2, 3))
        next(pred_tree)
    else:
        pred_share = lax.psum_scatter(pred_flat, "dp", scatter_dimension=0, tiled=True)
    sections = enc_vectors() + pred_vectors()
    early = []
    pred_shares = []

    def shared_part(found, label, length):
        if label in LOCAL_BIAS:
            return place_columns(found[label], length, LOCAL_BIAS[label], ways, member)
        return 0.5 * found[label]

    def all_devices(parts, after=None):
        total = doubling(doubling(jnp.concatenate(list(parts.values())), "tensor"), "dp", after)
        result = {}
        start = 0
        for label, part in parts.items():
            result[label] = total[start : start + part.shape[0]]
            start += part.shape[0]
        return result

    def early_sum(found):
        found = {**grads, **found}
        parts = {
            label: shared_part(found, label, length)
            for label, length in sections
            if label in found
        }
        parts[LOSS] = jnp.broadcast_to(local_loss, (128,))
        return all_devices(parts)

    pieces = {}
    trees = {}

    def watch(name, so_far, value):
        if not tiled:
            return None
        for label, grad in so_far.items():
            if label.startswith("w_") and label not in pieces:
                pieces[label] = to_tiles(grad.astype(jnp.bfloat16))
        if name == AT_HIDDEN:
            pred_ready = advance(pred_tree, value)
            trees[UPPER] = tree_scatter(stack_tiles(pieces, (2, 3)), (2, 3))
            return (next(trees[UPPER]), pred_ready)
        if name == AT_PACKED:
            trees[MIDDLE] = tree_scatter(stack_tiles(pieces, (1,)), (1,))
            return (advance(trees[UPPER], value), next(trees[MIDDLE]))
        if name == AT_HALF:
            pred_shares.append(advance(pred_tree, value).reshape(-1, 128))
            early.append(early_sum(so_far))
        return None

    grad_in, layer_grads = layer_backward(
        grad_mid, online_kept, mats, vectors, "", ENC_GROUP, HEAD_DIM, online_sides, watch
    )
    grads.update(layer_grads)
    grad_in_low = grad_in.astype(jnp.bfloat16)
    grads["w_patch"] = matmul_tn(patches, grad_in_low)
    grads["b_patch"] = jnp.sum(grad_in, axis=0)
    if tiled:
        pieces["w_patch"] = to_tiles(grads["w_patch"].astype(jnp.bfloat16))
        trees[LOWER] = tree_scatter(stack_tiles(pieces, (0,)), (0,))
        token = next(trees[LOWER])
        token = [advance(trees[UPPER], token), advance(trees[MIDDLE], token)]
        token = advance(trees[LOWER], token)
        token = advance(trees[MIDDLE], token)
        shares = {UPPER: advance(trees[UPPER], token)}
        token = advance(trees[LOWER], token)
        shares[MIDDLE] = advance(trees[MIDDLE], token)
        shares[LOWER] = advance(trees[LOWER], token)
        share = jnp.where(
            place[0] >= 8,
            shares[UPPER],
            jnp.where(place[0] >= 4, shares[MIDDLE], shares[LOWER]),
        )
        enc_square = jnp.square(share.astype(jnp.float32))
        enc_share = unpack_tiles(share, place, spans)
    else:
        enc_share = scatter_flat(grads, enc_shapes(ways), jnp.float32)
        enc_square = enc_share * enc_share
    if not early:
        early.append(early_sum(grads))
    sums = dict(early[0])
    loss_value = sums.pop(LOSS)[0]
    if tiled:
        pred_share = pred_shares[0]
    square_sum = jnp.sum(enc_square) + jnp.sum(pred_share * pred_share)
    late = {label: shared_part(grads, label, length) for label, length in sections}
    late = {label: part for label, part in late.items() if label not in sums}
    late[SQUARE] = jnp.broadcast_to(square_sum, (128,))
    sums.update(all_devices(late, enc_share))
    square_total = sums.pop(SQUARE)[0]
    vector_grad = jnp.concatenate([sums[label] for label, _ in sections])
    grad_norm = jnp.sqrt(square_total + jnp.sum(vector_grad * vector_grad))
    factor = jnp.minimum(1.0, CLIP / (grad_norm + 1e-06))
    count = step_count[0].astype(jnp.float32)
    scalars = jnp.stack(
        [factor, 1.0 / (1 - BETA_ONE**count), 1.0 / (1 - BETA_TWO**count)]
    ).astype(jnp.float32)
    back = lambda x: x.reshape(1, -1)
    new_enc, enc_first, enc_second, new_target = map(
        back,
        adam_flat(
            scalars,
            [rows(enc_params), rows(enc_m1), rows(enc_m2), enc_share, rows(target_params)],
        ),
    )
    new_pred, pred_first, pred_second = map(
        back, adam_flat(scalars, [rows(pred_params), rows(pred_m1), rows(pred_m2), pred_share])
    )
    new_vec, vec_first, vec_second = adam(
        vecs, vec_m1, vec_m2, vector_grad * factor, RATE_VEC, 0.0, count
    )
    new_target_vec = TAU * target_vecs + (1 - TAU) * new_vec[: target_vecs.shape[0]]
    return (
        new_enc,
        enc_first,
        enc_second,
        new_enc.astype(jnp.bfloat16),
        new_pred,
        pred_first,
        pred_second,
        new_pred.astype(jnp.bfloat16),
        new_target,
        new_vec,
        vec_first,
        vec_second,
        new_target_vec,
        loss_value,
        grad_norm,
    )


def solution(mesh):
    placed = (
        P("tensor", "dp"),
        P("tensor", "dp"),
        P("tensor", "dp"),
        P("tensor", "dp"),
        P("tensor", "dp"),
        P("tensor", "dp"),
        P("tensor", "dp"),
        P(),
        P(),
        P(),
        P(),
        P("dp", "tensor"),
        P("dp"),
        P("dp"),
        P(),
    )
    return jax.shard_map(
        shards,
        mesh=mesh,
        in_specs=placed,
        out_specs=(
            P("tensor", "dp"),
            P("tensor", "dp"),
            P("tensor", "dp"),
            P("tensor", "dp"),
            P("tensor", "dp"),
            P("tensor", "dp"),
            P("tensor", "dp"),
            P("tensor", "dp"),
            P("tensor", "dp"),
            P(),
            P(),
            P(),
            P(),
            P(),
            P(),
        ),
        check_vma=False,
    )
```

```python
import functools
import math

import jax
import jax.numpy as jnp
from jax import lax
from jax.experimental import pallas as pl
from jax.experimental.pallas import tpu as pltpu
from jax.sharding import PartitionSpec as P

D = 1024
HEADS = 16
HEAD_DIM = 64
MLP = 4096
PATCH = 1536
PD = 384
PHEADS = 12
PHEAD_DIM = 32
PMLP = 1536


BETA_ONE = 0.9
BETA_TWO = 0.999
ADAM_EPS = 1e-08
RATE_MAT = 0.01
RATE_VEC = 0.05
DECAY = 0.05
CLIP = 0.0002
TAU = 0.75
NORM_EPS = 1e-06
VAR_EPS = 0.0001
LOCAL_BIAS = {
    "b_qkv": True,
    "b_pqkv": True,
    "b_up": False,
    "b_pup": False,
    "b_pin": False,
    "b_pproj": False,
}
ROW_GAINS = ("ln2_g", "ln2_b", "pln2_g", "pln2_b")


def enc_shapes(ways):
    return [
        ("w_patch", PATCH // ways, D),
        ("w_qkv", D, 3 * D // ways),
        ("w_out", D // ways, D),
        ("w_up", D, MLP // ways),
        ("w_down", MLP // ways, D),
    ]


def pred_shapes(ways):
    return [
        ("w_pin", D, PD // ways),
        ("w_pqkv", PD, 3 * PD // ways),
        ("w_pout", PD // ways, PD),
        ("w_pup", PD, PMLP // ways),
        ("w_pdown", PMLP // ways, PD),
        ("w_pproj", PD, D // ways),
    ]


def enc_vectors():
    return [
        ("b_patch", D),
        ("ln1_g", D),
        ("ln1_b", D),
        ("b_qkv", 3 * D),
        ("b_out", D),
        ("ln2_g", D),
        ("ln2_b", D),
        ("b_up", MLP),
        ("b_down", D),
        ("lnf_g", D),
        ("lnf_b", D),
    ]


def pred_vectors():
    return [
        ("b_pin", PD),
        ("mask_tok", PD),
        ("pln1_g", PD),
        ("pln1_b", PD),
        ("b_pqkv", 3 * PD),
        ("b_pout", PD),
        ("pln2_g", PD),
        ("pln2_b", PD),
        ("b_pup", PMLP),
        ("b_pdown", PD),
        ("plnf_g", PD),
        ("plnf_b", PD),
        ("b_pproj", D),
    ]


def unflat(flat_row, shapes):
    result = {}
    offset = 0
    for label, height, breadth in shapes:
        result[label] = flat_row[offset : offset + height * breadth].reshape(height, breadth)
        offset += height * breadth
    return result


def split_vector(vector, sections):
    result = {}
    offset = 0
    for label, length in sections:
        result[label] = vector[offset : offset + length]
        offset += length
    return result


def positions(segment_row):
    earlier = jnp.sum((segment_row[None, :] < segment_row[:, None]).astype(jnp.int32), axis=1)
    return (jnp.arange(segment_row.shape[0], dtype=jnp.int32) - earlier).astype(jnp.float32)


def sincos(places, width):
    half_width = width // 2
    freqs = jnp.exp(-math.log(10000.0) * jnp.arange(half_width).astype(jnp.float32) / half_width)
    angles = places[:, None] * freqs[None, :]
    return jnp.concatenate([jnp.sin(angles), jnp.cos(angles)], axis=1)


def layer_norm(values, gain, shift):
    centered = values - jnp.mean(values, axis=-1, keepdims=True)
    spread = jnp.mean(centered * centered, axis=-1, keepdims=True)
    return centered * lax.rsqrt(spread + NORM_EPS) * gain + shift


def plain_norm(values):
    centered = values - jnp.mean(values, axis=-1, keepdims=True)
    return centered * lax.rsqrt(jnp.mean(centered * centered, axis=-1, keepdims=True) + NORM_EPS)


def norm_backward(values, gain, shift, cotangent):
    return jax.vjp(layer_norm, values, gain, shift)[1](cotangent)


def matmul(left, right):
    return jnp.dot(left, right, preferred_element_type=jnp.float32)


def matmul_tn(left, right):
    return lax.dot_general(
        left, right, (((0,), (0,)), ((), ())), preferred_element_type=jnp.float32
    )


def matmul_nt(left, right):
    return lax.dot_general(
        left, right, (((1,), (1,)), ((), ())), preferred_element_type=jnp.float32
    )


def local_columns(vector, thirds, ways, member):
    if thirds:
        width = vector.shape[0] // 3
        slab = vector.reshape(3, width)
        return lax.dynamic_slice_in_dim(slab, member * (width // ways), width // ways, 1).reshape(
            -1
        )
    return lax.dynamic_slice_in_dim(
        vector, member * (vector.shape[0] // ways), vector.shape[0] // ways, 0
    )


def place_columns(local, length, thirds, ways, member):
    if thirds:
        slab = jnp.zeros((3, length // 3), jnp.float32)
        placed = lax.dynamic_update_slice_in_dim(
            slab, local.reshape(3, -1), member * (length // 3 // ways), 1
        )
        return placed.reshape(-1)
    return lax.dynamic_update_slice_in_dim(
        jnp.zeros((length,), jnp.float32), local, member * (length // ways), 0
    )


QB = 256
LOG2E = math.log2(math.e)

def roundup(n, m):
    return -(-n // m) * m

def dot_nn(a, b):
    return lax.dot_general(a, b, (((1,), (0,)), ((), ())), preferred_element_type=jnp.float32)

def dot_nt(a, b):
    return lax.dot_general(a, b, (((1,), (1,)), ((), ())), preferred_element_type=jnp.float32)

def pad_rows(x, n):
    return jnp.concatenate([x.astype(jnp.float32), jnp.zeros((n - x.shape[0], x.shape[1]), jnp.float32)], 0).astype(x.dtype)

def lane_keep(x, lo, hi):
    lane = lax.broadcasted_iota(jnp.int32, (1, x.shape[1]), 1)
    keep = jnp.where((lane >= lo) & (lane < hi), 1.0, 0.0).astype(x.dtype)
    return x * keep

def attn_fwd_kernel(heads, e, T, TP, W, packed_ref, qa_ref, ka_ref, o_ref, lse_ref, q_s, k_s, v_s, o_s, s_s, p_s):
    g = pl.program_id(0)
    base = pl.multiple_of(g * 128, 128)
    q_s[...] = pad_rows(packed_ref[:, pl.ds(base, 128)], TP)
    k_s[:, :128] = pad_rows(packed_ref[:, pl.ds(base + W, 128)], TP)
    k_s[:, 128:] = ka_ref[...]
    v_s[...] = pad_rows(packed_ref[:, pl.ds(base + 2 * W, 128)], TP)
    scale = e ** -0.5 * LOG2E
    lane = lax.broadcasted_iota(jnp.int32, (QB, 128), 1)
    step = 16
    units = [(i, h) for i in range(TP // QB) for h in range(heads)]

    def scores(n):
        i, h = units[n]
        rows = slice(i * QB, (i + 1) * QB)
        qq = jnp.concatenate([lane_keep(q_s[rows, :], h * e, (h + 1) * e), qa_ref[rows, :]], 1)
        s_s[n % 2] = dot_nt(qq, k_s[...])

    scores(0)
    for n, (i, h) in enumerate(units):
        if n + 1 < len(units):
            scores(n + 1)
        rows = slice(i * QB, (i + 1) * QB)
        peaks, totals = [], []
        for r in range(0, QB, step):
            s = s_s[n % 2, r : r + step, :] * scale
            peak = jnp.max(s, axis=1, keepdims=True)
            p = jnp.exp2(s - peak)
            total = jnp.sum(p, axis=1, keepdims=True)
            p_s[n % 2, r : r + step, :] = p.astype(jnp.bfloat16)
            peaks.append(peak)
            totals.append(total)
        total = jnp.concatenate(totals, 0)
        o = dot_nn(p_s[n % 2], v_s[...]) * (1.0 / total)
        stat = jnp.concatenate(peaks, 0) + jnp.log2(total)
        if h == 0:
            out = o
            stats = jnp.broadcast_to(stat, (QB, 128))
        else:
            out = jnp.where(lane < h * e, out, o)
            stats = jnp.where(lane < h, stats, stat)
        if h == heads - 1:
            if heads * e < 128:
                out = jnp.where(lane < heads * e, out, 0.0)
            o_s[rows, :] = out.astype(jnp.bfloat16)
            lse_ref[0, :, rows] = stats.T[:8, :]
    o_ref[...] = o_s[:T, :]

def attn_fwd(packed, qa, ka, heads, e):
    T, W3 = packed.shape
    W = W3 // 3
    TP = roundup(T, QB)
    groups = W // 128
    return pl.pallas_call(
        functools.partial(attn_fwd_kernel, heads, e, T, TP, W),
        grid=(groups,),
        in_specs=[pl.BlockSpec((T, W3), lambda g: (0, 0)), pl.BlockSpec((TP, 128), lambda g: (0, 0)), pl.BlockSpec((TP, 128), lambda g: (0, 0))],
        out_specs=[pl.BlockSpec((T, 128), lambda g: (0, g)), pl.BlockSpec((1, 8, TP), lambda g: (g, 0, 0))],
        out_shape=[jax.ShapeDtypeStruct((T, W), jnp.bfloat16), jax.ShapeDtypeStruct((groups, 8, TP), jnp.float32)],
        scratch_shapes=[pltpu.VMEM((TP, 128), jnp.bfloat16), pltpu.VMEM((TP, 256), jnp.bfloat16), pltpu.VMEM((TP, 128), jnp.bfloat16), pltpu.VMEM((TP, 128), jnp.bfloat16), pltpu.VMEM((2, QB, TP), jnp.float32), pltpu.VMEM((2, QB, TP), jnp.bfloat16)],
        compiler_params=pltpu.CompilerParams(vmem_limit_bytes=48 << 20),
        cost_estimate=pl.CostEstimate(flops=groups * heads * 4 * T * T * 256, bytes_accessed=T * W3 * 3, transcendentals=groups * heads * T * T),
        name="attn_fwd",
    )(packed, qa, ka)

def attn_bwd_kernel(heads, e, T, TP, W, first, chained, packed_ref, do_ref, qa_ref, ka_ref, lse_ref, *rest):
    d_ref, q_s, k_s, v_s, do_s, dk_s, dv_s, dq_s, out_s, s_s, d_s, p_s, ds_s, sems = rest[1:] if chained else rest
    g = pl.program_id(0) + first
    base = pl.multiple_of(g * 128, 128)
    q_s[:, :128] = pad_rows(packed_ref[:, pl.ds(base, 128)], TP)
    q_s[:, 128:] = qa_ref[...]
    k = pad_rows(packed_ref[:, pl.ds(base + W, 128)], TP)
    k_s[...] = k
    v_s[...] = pad_rows(packed_ref[:, pl.ds(base + 2 * W, 128)], TP)
    do_s[...] = pad_rows(do_ref[...], TP)
    kt = k.astype(jnp.float32).T.astype(jnp.bfloat16)
    sub = lax.broadcasted_iota(jnp.int32, (128, 1), 0)
    lane = lax.broadcasted_iota(jnp.int32, (TP, 128), 1)
    scale2 = e ** -0.5 * LOG2E
    scale = e ** -0.5
    step = 64
    blocks = TP // QB
    units = [(h, i) for h in range(heads) for i in range(blocks)]

    def products(n):
        h, i = units[n]
        rows = slice(i * QB, (i + 1) * QB)
        lo, hi = h * e, (h + 1) * e
        kk = jnp.concatenate([lane_keep(k_s[...], lo, hi), ka_ref[...]], 1)
        s_s[n % 2] = dot_nt(kk, q_s[rows, :])
        d_s[n % 2] = dot_nt(lane_keep(v_s[...], lo, hi), do_s[rows, :])

    def gather(h):
        lo, hi = h * e, (h + 1) * e
        dv = dot_nn(p_s[h % 2], do_s[...])
        dk = dot_nn(ds_s[h % 2], q_s[:, :128])
        dq = dot_nn(kt * jnp.where((sub >= lo) & (sub < hi), 1.0, 0.0).astype(jnp.bfloat16), ds_s[h % 2])
        if h == 0:
            dv_s[...], dk_s[...], dq_s[...] = dv, dk, dq
        else:
            dv_s[...] = jnp.where(lane < lo, dv_s[...], dv)
            dk_s[...] = jnp.where(lane < lo, dk_s[...], dk)
            dq_s[...] += dq

    products(0)
    for n, (h, i) in enumerate(units):
        if n + 1 < len(units):
            products(n + 1)
        rows = slice(i * QB, (i + 1) * QB)
        lse = lse_ref[0, h : h + 1, rows]
        d = jnp.zeros((8, QB), jnp.float32)
        for r in range(0, TP, step):
            part = slice(r, r + step)
            pt = jnp.exp2(s_s[n % 2, part, :] * scale2 - lse)
            s_s[n % 2, part, :] = pt
            p_s[h % 2, part, rows] = pt.astype(jnp.bfloat16)
            d += jnp.sum((pt * d_s[n % 2, part, :]).reshape(step // 8, 8, QB), axis=0)
        d = jnp.sum(d, axis=0, keepdims=True)
        for r in range(0, TP, step):
            part = slice(r, r + step)
            ds_s[h % 2, part, rows] = (s_s[n % 2, part, :] * (d_s[n % 2, part, :] - d)).astype(jnp.bfloat16)
        if h and i == 0:
            gather(h - 1)
    gather(heads - 1)
    if heads * e < 128:
        dv_s[...] = jnp.where(lane < heads * e, dv_s[...], 0.0)
        dk_s[...] = jnp.where(lane < heads * e, dk_s[...], 0.0)
    dq = dq_s[...].T * scale
    out_s[0] = dq.astype(jnp.bfloat16)[:T]
    out_s[1] = (dk_s[...] * scale).astype(jnp.bfloat16)[:T]
    out_s[2] = dv_s[...].astype(jnp.bfloat16)[:T]
    copies = [
        pltpu.make_async_copy(out_s.at[i], d_ref.at[:, pl.ds(base + i * W, 128)], sems.at[i])
        for i in range(3)
    ]
    for copy in copies:
        copy.start()
    for copy in copies:
        copy.wait()

def attn_bwd(packed, do, qa, ka, lse, heads, e, first=0, groups=None, so_far=None):
    T, W3 = packed.shape
    W = W3 // 3
    TP = roundup(T, QB)
    groups = W // 128 if groups is None else groups
    chained = so_far is not None
    full = lambda g: (0, 0)
    return pl.pallas_call(
        functools.partial(attn_bwd_kernel, heads, e, T, TP, W, first, chained),
        grid=(groups,),
        in_specs=[pl.BlockSpec((T, W3), full), pl.BlockSpec((T, 128), lambda g: (0, g + first)), pl.BlockSpec((TP, 128), full), pl.BlockSpec((TP, 128), full), pl.BlockSpec((1, 8, TP), lambda g: (g + first, 0, 0))]
        + ([pl.BlockSpec(memory_space=pl.ANY)] if chained else []),
        out_specs=pl.BlockSpec(memory_space=pl.ANY),
        input_output_aliases={5: 0} if chained else {},
        out_shape=jax.ShapeDtypeStruct((T, W3), jnp.bfloat16),
        scratch_shapes=[pltpu.VMEM((TP, 256), jnp.bfloat16), pltpu.VMEM((TP, 128), jnp.bfloat16), pltpu.VMEM((TP, 128), jnp.bfloat16), pltpu.VMEM((TP, 128), jnp.bfloat16), pltpu.VMEM((TP, 128), jnp.float32), pltpu.VMEM((TP, 128), jnp.float32), pltpu.VMEM((128, TP), jnp.float32), pltpu.VMEM((3, T, 128), jnp.bfloat16), pltpu.VMEM((2, TP, QB), jnp.float32), pltpu.VMEM((2, TP, QB), jnp.float32), pltpu.VMEM((2, TP, TP), jnp.bfloat16), pltpu.VMEM((2, TP, TP), jnp.bfloat16), pltpu.SemaphoreType.DMA((3,))],
        compiler_params=pltpu.CompilerParams(vmem_limit_bytes=48 << 20),
        cost_estimate=pl.CostEstimate(flops=groups * heads * 10 * T * T * 256, bytes_accessed=T * W3 * 5, transcendentals=groups * heads * T * T),
        name="attn_bwd",
    )(packed, do, qa, ka, lse, *([so_far] if chained else []))

def mask_sides(segment, context_row, TP):
    T = segment.shape[0]
    s = jnp.arange(128)[None, :]
    one = (segment[:, None] == s)
    qa = jnp.where(one, -1e30, 0.0).astype(jnp.bfloat16)
    ka = jnp.where((s < 8) & ~(one & (context_row[:, None] > 0)), 1.0, 0.0).astype(jnp.bfloat16)
    qa = jnp.concatenate([qa, jnp.zeros((TP - T, 128), jnp.bfloat16)], 0)
    ka = jnp.concatenate([ka, jnp.broadcast_to(jnp.where(s < 8, 1.0, 0.0).astype(jnp.bfloat16), (TP - T, 128))], 0)
    return qa, ka


CHUNK = 16384
UNIT = 3 * CHUNK
SWAP = ((0, 1), (1, 0))


def swap(x):
    return lax.ppermute(x, "tensor", SWAP)


def tensor_total(part):
    return part + swap(part)


def tensor_back(part):
    low = part.astype(jnp.bfloat16)
    return low.astype(jnp.float32) + swap(low).astype(jnp.float32)


def doubling(x, axis, after=None):
    size = lax.axis_size(axis)
    if size & (size - 1):
        return lax.psum(x, axis)
    stride = 1
    while stride < size:
        reach = 4 if size // stride % 4 == 0 else 2
        others = [
            lax.ppermute(x, axis, [(i, i ^ (m * stride)) for i in range(size)])
            for m in range(1, reach)
        ]
        if stride * reach >= size:
            others = pin(others, after)
        x = x + others[0]
        if reach == 4:
            x = x + (others[1] + others[2])
        stride *= reach
    return x


def pin(x, after):
    return x if after is None else lax.optimization_barrier((x, after))[0]


def tile_width(label):
    return {"w_qkv": 12, "w_up": 16}.get(label, 8)


def enc_chunks(ways):
    spans = []
    start = 0
    for label, height, breadth in enc_shapes(ways):
        count = height * breadth // CHUNK
        spans.append((start, start + count, breadth // 128))
        start += count
    return spans


def regions(unit, spans, emit):
    first = unit * 3
    wide = [s for s in spans if s[2] == 12]
    flat = [s for s in spans if s[2] != 12]
    in_wide = functools.reduce(jnp.logical_or, [(first >= a) & (first < b) for a, b, _ in wide])

    @pl.when(in_wide)
    def _():
        emit(0, 0, 12, 4)

    @pl.when(jnp.logical_not(in_wide))
    def _():
        for c in range(3):
            for width in (8, 16):
                hit = functools.reduce(
                    jnp.logical_or,
                    [(first + c >= a) & (first + c < b) for a, b, w in flat if w == width],
                )

                @pl.when(hit)
                def _():
                    emit(c * 128, c * 16, width, 16 // width)


def pack_kernel(spans, units, place_ref, x_ref, o_ref):
    def emit(row, tile, width, groups):
        for t in range(groups):
            for j in range(width):
                o_ref[tile + t * width + j] = x_ref[
                    pl.ds(row + t * 8 * width + j, 8, stride=width), :
                ].astype(jnp.bfloat16)

    regions(place_ref[0] * units + pl.program_id(0), spans, emit)


def pack_tiles(flat, place, spans):
    units = flat.shape[0] // 384
    return pl.pallas_call(
        functools.partial(pack_kernel, spans, units),
        grid_spec=pltpu.PrefetchScalarGridSpec(
            num_scalar_prefetch=1,
            grid=(units,),
            in_specs=[pl.BlockSpec((384, 128), lambda i, s: (i, 0))],
            out_specs=pl.BlockSpec((48, 8, 128), lambda i, s: (i, 0, 0)),
        ),
        out_shape=jax.ShapeDtypeStruct((units * 48, 8, 128), jnp.bfloat16),
        name="pack",
    )(place, flat)


def unpack_kernel(spans, units, place_ref, x_ref, o_ref):
    def emit(row, tile, width, groups):
        for t in range(groups):
            for j in range(width):
                o_ref[pl.ds(row + t * 8 * width + j, 8, stride=width), :] = x_ref[
                    tile + t * width + j
                ].astype(jnp.float32)

    regions(place_ref[0] * units + pl.program_id(0), spans, emit)


def unpack_tiles(tiles, place, spans):
    units = tiles.shape[0] // 48
    return pl.pallas_call(
        functools.partial(unpack_kernel, spans, units),
        grid_spec=pltpu.PrefetchScalarGridSpec(
            num_scalar_prefetch=1,
            grid=(units,),
            in_specs=[pl.BlockSpec((48, 8, 128), lambda i, s: (i, 0, 0))],
            out_specs=pl.BlockSpec((384, 128), lambda i, s: (i, 0)),
        ),
        out_shape=jax.ShapeDtypeStruct((units * 384, 128), jnp.float32),
        name="unpack",
    )(place, tiles)


def adam_kernel(with_target, scalars, p_ref, m_ref, v_ref, g_ref, *rest):
    if with_target:
        t_ref, po_ref, mo_ref, vo_ref, to_ref = rest
    else:
        po_ref, mo_ref, vo_ref = rest
    grad = g_ref[...] * scalars[0]
    first = BETA_ONE * m_ref[...] + (1 - BETA_ONE) * grad
    second = BETA_TWO * v_ref[...] + (1 - BETA_TWO) * grad * grad
    weight = p_ref[...]
    ratio = (first * scalars[1]) / (jnp.sqrt(second * scalars[2]) + ADAM_EPS)
    weight = weight - RATE_MAT * (ratio + DECAY * weight)
    po_ref[...] = weight
    mo_ref[...] = first
    vo_ref[...] = second
    if with_target:
        to_ref[...] = TAU * t_ref[...] + (1 - TAU) * weight


def adam_flat(scalars, arrays):
    rows = arrays[0].shape[0]
    parts = next((n for n in (9, 6, 3) if rows % (8 * n) == 0), 1)
    with_target = len(arrays) == 5
    spec = pl.BlockSpec((rows // parts, 128), lambda i: (i, 0))
    n_out = 4 if with_target else 3
    return pl.pallas_call(
        functools.partial(adam_kernel, with_target),
        grid=(parts,),
        in_specs=[pl.BlockSpec(memory_space=pltpu.SMEM)] + [spec] * len(arrays),
        out_specs=[spec] * n_out,
        out_shape=[jax.ShapeDtypeStruct((rows, 128), jnp.float32)] * n_out,
        compiler_params=pltpu.CompilerParams(vmem_limit_bytes=32 << 20),
        name="adam",
    )(scalars, *arrays)


def from_tiles(parts, ways):
    result = {}
    for tiles, (label, height, breadth) in zip(parts, enc_shapes(ways)):
        piece = tiles.reshape(height // 8, breadth // 128, 8, 128)
        result[label] = piece.transpose(0, 2, 1, 3).reshape(height, breadth)
    return result


def to_tiles(matrix):
    height, breadth = matrix.shape
    return (
        matrix.reshape(height // 8, 8, breadth // 128, 128)
        .transpose(0, 2, 1, 3)
        .reshape(height * breadth // 1024, 8, 128)
    )


def gather_dp(x):
    return lax.all_gather(x, "dp", axis=0, tiled=True)


def tree_gather(tiles):
    place = lax.axis_index("dp")
    z, y, x = place // 4, place // 2 % 2, place % 2
    half = tiles.shape[0] // 2
    over_x, over_y = ([(i, i ^ bit) for i in range(16)] for bit in (1, 2))
    ring_up = [(i, (i + 4) % 16) for i in range(16)]
    ring_down = [(j, i) for i, j in ring_up]
    a, b = tiles[:half], tiles[half:]
    arrived = []
    waits = None
    for k in range(4):
        ax, by = permute(a, over_x), permute(b, over_y)
        ay, bx = permute(a, over_y), permute(b, over_x)
        axy, byx = permute(ax, over_y), permute(by, over_x)
        za, zb = (z - k) % 4, (z + k) % 4
        arrived.append([(0, za, y, x, a), (1, zb, y, x, b)])
        arrived.append([(0, za, y, 1 - x, ax), (1, zb, 1 - y, x, by)])
        arrived.append([(0, za, 1 - y, x, ay), (1, zb, y, 1 - x, bx)])
        arrived.append([(0, za, 1 - y, 1 - x, axy), (1, zb, 1 - y, 1 - x, byx)])
        if k == 1:
            begun = (a, b)
        if k == 2:
            first = (ax, by, ay, bx) + last
        if k == 3:
            first = first + (a, b)
        last = (axy, byx)
        a, b = pin((a, b), waits)
        waits = (ax, by, ay, bx) if k == 0 else (ax, by, ay, bx, axy, byx)
        if k < 3:
            a, b = permute(a, ring_up), permute(b, ring_down)
    zero = pin(jnp.zeros((), tiles.dtype), first)
    whole = jnp.broadcast_to(zero, (32, half) + tiles.shape[1:])
    for n in sorted(range(16), key=lambda n: (n // 4 * 2 + n % 4, n)):
        for side, pz, py, px, piece in arrived[n]:
            slot = (pz * 4 + py * 2 + px) * 2 + side
            whole = lax.dynamic_update_index_in_dim(whole, piece, slot, 0)
    return whole.reshape((32 * half,) + tiles.shape[1:]), begun


def split_gathered(gathered, sizes, part, first, total):
    results = []
    start = 0
    for size in sizes:
        moves = []
        for device in range(gathered.shape[0] // total):
            low, high = max(start, device * part), min(start + size, (device + 1) * part)
            if low < high:
                source = device * total + first + low - device * part
                moves.append((0, source, low - start, high - low))
        results.append(copy_tiles([gathered], moves, size, pltpu.HBM, 52))
        start += size
    return results


def gather_flat(flat, shapes):
    return unflat(gather_dp(flat.astype(jnp.bfloat16)).reshape(-1), shapes)


def flat_kernel(shapes, *refs):
    ins, out, column = refs[:-2], refs[-2], refs[-1]

    def by_turns(ref, first, width, height):
        column[:height, :width] = ref[:, first : first + width]
        pairs = height // 2
        return column[pl.ds(0, pairs, stride=2), :], column[pl.ds(1, pairs, stride=2), :]

    base = 0
    for ref, (height, breadth) in zip(ins, shapes):
        full = breadth // 128
        if breadth % 128 == 0:
            for j in range(full):
                out[pl.ds(base + j, height, stride=full), :] = ref[:, j * 128 : (j + 1) * 128]
        else:
            pairs = height // 2
            step = 2 * full + 1
            even, odd = zip(*[by_turns(ref, j * 128, 128, height) for j in range(full)])
            even_end, odd_end = [e[:, :64] for e in by_turns(ref, full * 128, 64, height)]
            rows = list(even) + [jnp.concatenate([even_end, odd[0][:, :64]], 1)]
            for j in range(full):
                after = odd[j + 1][:, :64] if j + 1 < full else odd_end
                rows.append(jnp.concatenate([odd[j][:, 64:], after], 1))
            for j, row in enumerate(rows):
                out[pl.ds(base + j, pairs, stride=step), :] = row
        base += height * breadth // 128


def flatten_matrices(matrices):
    shapes = [m.shape for m in matrices]
    total = sum(h * b for h, b in shapes) // 128
    return pl.pallas_call(
        functools.partial(flat_kernel, shapes),
        in_specs=[pl.BlockSpec(memory_space=pltpu.VMEM)] * len(matrices),
        out_specs=pl.BlockSpec(memory_space=pltpu.VMEM),
        out_shape=jax.ShapeDtypeStruct((total, 128), jnp.float32),
        scratch_shapes=[pltpu.VMEM((max(h for h, _ in shapes), 128), jnp.float32)],
        compiler_params=pltpu.CompilerParams(vmem_limit_bytes=40 << 20),
        name="flatten",
    )(*matrices)


def scatter_flat(grads, shapes, kind):
    whole = jnp.concatenate(
        [grads[label].astype(kind).reshape(-1, 128) for label, _, _ in shapes], 0
    )
    return lax.psum_scatter(whole, "dp", scatter_dimension=0, tiled=True).astype(jnp.float32)


def permute(x, pairs):
    return lax.ppermute(x, "dp", pairs)


ENC_TILES = [(label, height * breadth // 1024) for label, height, breadth in enc_shapes(2)]


def plus(a, b):
    return a.astype(jnp.float32) + b.astype(jnp.float32)


def pick(x, index, axis):
    return lax.dynamic_index_in_dim(x, index, axis, keepdims=False)


def stack_kernel(moves, count, *refs):
    ins, out, sems = refs[:count], refs[count], refs[count + 1]
    copies = [
        pltpu.make_async_copy(
            ins[source].at[pl.ds(first, length)], out.at[pl.ds(target, length)], sems.at[number]
        )
        for number, (source, first, target, length) in enumerate(moves)
    ]
    for copy in copies:
        copy.start()
    for copy in copies:
        copy.wait()


def copy_tiles(sources, moves, length, space=pl.ANY, room=24):
    return pl.pallas_call(
        functools.partial(stack_kernel, moves, len(sources)),
        in_specs=[pl.BlockSpec(memory_space=space)] * len(sources),
        out_specs=pl.BlockSpec(memory_space=pltpu.VMEM),
        out_shape=jax.ShapeDtypeStruct((length, 8, 128), jnp.bfloat16),
        scratch_shapes=[pltpu.SemaphoreType.DMA((len(moves),))],
        compiler_params=pltpu.CompilerParams(vmem_limit_bytes=room << 20),
        name="stack",
    )(*sources)


def stack_tiles(pieces, planes):
    shard = sum(size for _, size in ENC_TILES) // 16
    low, high = planes[0] * 4 * shard, (planes[-1] + 1) * 4 * shard
    moves, used = [], []
    start = 0
    for label, size in ENC_TILES:
        first, last = max(low, start), min(high, start + size)
        if first < last:
            moves.append((len(used), first - start, first - low, last - first))
            used.append(pieces[label])
        start += size
    return copy_tiles(used, moves, high - low)


def tree_scatter(tiles, planes):
    low = jnp.bfloat16
    place = lax.axis_index("dp")
    z, near = place // 4, place % 4
    count = len(planes)
    copies = 4 // count
    size = tiles.shape[0] // (4 * count * copies)
    grid = tiles.reshape((count, 4, copies, size) + tiles.shape[1:])

    def exchange(take, at, stride):
        ready = [take(at ^ m) for m in range(1, 4)]
        sent = [
            permute(ready[m - 1], [(i, i ^ (m * stride)) for i in range(16)]) for m in range(1, 4)
        ]
        return ready, sent

    ready, sent = exchange(lambda n: pick(grid, n, 1).astype(low), near, 1)
    after = yield ready
    sent = pin(sent, after)
    plane_sum = sum(part.astype(jnp.float32) for part in [pick(grid, near, 1)] + sent)
    blocks = plane_sum.swapaxes(0, 1).reshape((4, size) + tiles.shape[1:])
    ready, sent = exchange(lambda n: pick(blocks, n, 0).astype(low), z, 4)
    after = yield ready
    sent = pin(sent, after)
    held = sum(part.astype(jnp.float32) for part in [pick(blocks, z, 0)] + sent)
    if copies == 1:
        yield held
    held = held.astype(low)
    got = []
    for c in range(copies):
        pairs = [
            ((c * count + j) * 4 + i, planes[j] * 4 + i)
            for j in range(count)
            for i in range(4)
            if c * count + j != planes[j]
        ]
        stay = [planes[j] for j in range(count) if c * count + j == planes[j]]
        piece = permute(held, pairs) if pairs else held
        if pairs and stay:
            piece = jnp.where(functools.reduce(jnp.logical_or, [z == p for p in stay]), held, piece)
        got.append(piece)
    after = yield [held]
    yield jnp.concatenate(pin(got, after), 0)


def advance(tree, after):
    return tree.send(after)


def group_pad(x, axis, e, per_group):
    used = e * per_group
    shape = x.shape
    parts = x.reshape(shape[:axis] + (shape[axis] // used, used) + shape[axis + 1 :])
    widths = [(0, 0)] * parts.ndim
    widths[axis + 1] = (0, 128 - used)
    padded = jnp.pad(parts, widths)
    return padded.reshape(shape[:axis] + (shape[axis] // used * 128,) + shape[axis + 1 :])


def group_cut(x, axis, e, per_group):
    used = e * per_group
    shape = x.shape
    parts = x.reshape(shape[:axis] + (shape[axis] // 128, 128) + shape[axis + 1 :])
    parts = lax.slice_in_dim(parts, 0, used, axis=axis + 1)
    return parts.reshape(shape[:axis] + (shape[axis] // 128 * used,) + shape[axis + 1 :])


def layer_forward(
    stream, mats, vectors, tag, per_group, head_dim, sides, ways, member, watch=lambda value: None
):
    normed_low = layer_norm(stream, vectors[tag + "ln1_g"], vectors[tag + "ln1_b"]).astype(
        jnp.bfloat16
    )
    bias = group_pad(
        local_columns(vectors["b_" + tag + "qkv"], True, ways, member), 0, head_dim, per_group
    )
    packed = (matmul(normed_low, mats["w_" + tag + "qkv"]) + bias).astype(jnp.bfloat16)
    mixed_rows, log_totals = attn_fwd(packed, sides[0], sides[1], per_group, head_dim)
    attn_part = matmul(mixed_rows, mats["w_" + tag + "out"])
    middle = stream + tensor_total(attn_part) + vectors["b_" + tag + "out"]
    normed_two = layer_norm(middle, vectors[tag + "ln2_g"], vectors[tag + "ln2_b"]).astype(
        jnp.bfloat16
    )
    normed_two = pin(normed_two, watch(normed_two))
    hidden = matmul(normed_two, mats["w_" + tag + "up"]) + local_columns(
        vectors["b_" + tag + "up"], False, ways, member
    )
    activated = lax.optimization_barrier(jax.nn.gelu(hidden).astype(jnp.bfloat16))
    down_part = matmul(activated, mats["w_" + tag + "down"])
    result = middle + tensor_total(down_part) + vectors["b_" + tag + "down"]
    kept = (
        stream,
        normed_low,
        packed,
        mixed_rows,
        log_totals,
        middle,
        normed_two,
        hidden,
        activated,
    )
    return (result, kept)


def gelu_slope(x):
    scale, cubic = math.sqrt(2 / math.pi), 0.044715
    square = x * x
    bend = jnp.tanh(scale * x * (1 + cubic * square))
    return 0.5 * (1 + bend) + (0.5 * scale) * x * (1 - bend * bend) * (1 + 3 * cubic * square)


def layer_backward(grad_out, kept, mats, vectors, tag, per_group, head_dim, sides, watch):
    (
        stream,
        normed_low,
        packed,
        mixed_rows,
        log_totals,
        middle,
        normed_two,
        hidden,
        activated,
    ) = kept
    grads = {}
    grad_low = grad_out.astype(jnp.bfloat16)
    grads["w_" + tag + "down"] = matmul_tn(activated, grad_low)
    grads["b_" + tag + "down"] = jnp.sum(grad_out, axis=0)
    grad_act = matmul_nt(grad_low, mats["w_" + tag + "down"])
    grad_hidden = (grad_act * gelu_slope(hidden)).astype(jnp.bfloat16)
    grads["w_" + tag + "up"] = matmul_tn(normed_two, grad_hidden)
    grads["b_" + tag + "up"] = jnp.sum(grad_hidden.astype(jnp.float32), axis=0)
    grad_hidden = pin(grad_hidden, watch(AT_HIDDEN, grads, grad_hidden))
    grad_normed = tensor_back(matmul_nt(grad_hidden, mats["w_" + tag + "up"]))
    grad_middle, grads[tag + "ln2_g"], grads[tag + "ln2_b"] = norm_backward(
        middle, vectors[tag + "ln2_g"], vectors[tag + "ln2_b"], grad_normed
    )
    grad_middle = grad_middle + grad_out
    grad_mid_low = grad_middle.astype(jnp.bfloat16)
    grads["w_" + tag + "out"] = group_cut(
        matmul_tn(mixed_rows, grad_mid_low), 0, head_dim, per_group
    )
    grads["b_" + tag + "out"] = jnp.sum(grad_middle, axis=0)
    grad_mixed = matmul_nt(grad_mid_low, mats["w_" + tag + "out"]).astype(jnp.bfloat16)
    groups = packed.shape[1] // 384
    if tag:
        grad_packed = attn_bwd(
            packed, grad_mixed, sides[0], sides[1], log_totals, per_group, head_dim
        )
    else:
        grad_packed = attn_bwd(
            packed,
            grad_mixed,
            sides[0],
            sides[1],
            log_totals,
            per_group,
            head_dim,
            groups=groups // 2,
        )
        grad_mixed = pin(grad_mixed, watch(AT_HALF, grads, grad_packed))
        grad_packed = attn_bwd(
            packed,
            grad_mixed,
            sides[0],
            sides[1],
            log_totals,
            per_group,
            head_dim,
            first=groups // 2,
            groups=groups // 2,
            so_far=grad_packed,
        )
    grads["w_" + tag + "qkv"] = group_cut(
        matmul_tn(normed_low, grad_packed), 1, head_dim, per_group
    )
    grads["b_" + tag + "qkv"] = group_cut(
        jnp.sum(grad_packed.astype(jnp.float32), axis=0), 0, head_dim, per_group
    )
    grad_packed = pin(grad_packed, watch(AT_PACKED, grads, grad_packed))
    first_part = matmul_nt(grad_packed, mats["w_" + tag + "qkv"]).astype(jnp.bfloat16)
    first_part = pin(first_part, watch(AT_PART, grads, first_part))
    grad_first = tensor_back(first_part)
    grad_first = pin(grad_first, watch(AT_FIRST, grads, grad_first))
    grad_stream, grads[tag + "ln1_g"], grads[tag + "ln1_b"] = norm_backward(
        stream, vectors[tag + "ln1_g"], vectors[tag + "ln1_b"], grad_first
    )
    return (grad_stream + grad_middle, grads)


def adam(weight, first, second, grad, rate, decay, count):
    first_new = BETA_ONE * first + (1 - BETA_ONE) * grad
    second_new = BETA_TWO * second + (1 - BETA_TWO) * grad * grad
    first_hat = first_new / (1 - BETA_ONE**count)
    second_hat = second_new / (1 - BETA_TWO**count)
    weight_new = weight - rate * (first_hat / (jnp.sqrt(second_hat) + ADAM_EPS) + decay * weight)
    return (weight_new, first_new, second_new)


UPPER, MIDDLE, LOWER = range(3)
AT_HIDDEN, AT_HALF, AT_PACKED, AT_PART, AT_FIRST = range(5)
SQUARE, LOSS = range(2)
ENC_GROUP = 2
PRED_GROUP = 3


def shards(
    enc_params,
    enc_m1,
    enc_m2,
    pred_params,
    pred_m1,
    pred_m2,
    target_params,
    vecs,
    vec_m1,
    vec_m2,
    target_vecs,
    patches,
    segment,
    context,
    step_count,
):
    ways = lax.axis_size("tensor")
    member = lax.axis_index("tensor")
    dp_count = lax.axis_size("dp")
    place = lax.axis_index("dp").astype(jnp.int32).reshape(1)
    spans = enc_chunks(ways)
    rows = lambda x: x.reshape(-1, 128)
    tiled = dp_count == 16 and enc_params.shape[1] % UNIT == 0 and all(
        a % 3 == 0 and b % 3 == 0 for a, b, w in spans if w == 12
    )
    vectors = split_vector(vecs, enc_vectors() + pred_vectors())
    target_vectors = split_vector(target_vecs, enc_vectors())
    begun = None
    if tiled:
        pred_tiles = rows(pred_params).astype(jnp.bfloat16).reshape(-1, 8, 128)
        own_tiles = jnp.concatenate([pack_tiles(rows(enc_params), place, spans), pred_tiles], 0)
        enc_tiles, begun = tree_gather(own_tiles)
    segment, target_local = pin((segment, target_params), begun)
    places = positions(segment)
    context_mask = context > 0
    padded = roundup(segment.shape[0], QB)
    online_sides = mask_sides(segment, context, padded)
    all_sides = mask_sides(segment, jnp.ones_like(context), padded)
    embed_pos = sincos(places, D)
    pred_pos = sincos(places, PD)
    if tiled:
        target_tiles = pack_tiles(rows(target_local), place, spans)
        enc_tiles, target_tiles, embed_pos, pred_pos, online_sides, all_sides = (
            lax.optimization_barrier(
                (enc_tiles, target_tiles, embed_pos, pred_pos, online_sides, all_sides)
            )
        )
        sizes = [size for _, size in ENC_TILES]
        shard, both = sum(sizes) // 16, own_tiles.shape[0]
        mats = from_tiles(split_gathered(enc_tiles, sizes, shard, 0, both), ways)
        pred_count = [16 * (both - shard)]
        pred_whole = split_gathered(enc_tiles, pred_count, both - shard, shard, both)[0]
    else:
        mats = gather_flat(rows(enc_params), enc_shapes(ways))
    def embed(patch_rows, weight_set, vector_set):
        return (
            tensor_total(matmul(patch_rows, weight_set["w_patch"])) + vector_set["b_patch"] + embed_pos
        )

    online_mid, online_kept = layer_forward(
        embed(patches, mats, vectors),
        mats,
        vectors,
        "",
        ENC_GROUP,
        HEAD_DIM,
        online_sides,
        ways,
        member,
    )
    if tiled:
        mats.update(unflat(pred_whole.reshape(-1), pred_shapes(ways)))
    else:
        mats.update(gather_flat(rows(pred_params), pred_shapes(ways)))
    mats["w_pqkv"] = group_pad(mats["w_pqkv"], 1, PHEAD_DIM, PRED_GROUP)
    mats["w_pout"] = group_pad(mats["w_pout"], 0, PHEAD_DIM, PRED_GROUP)
    encoded_low = layer_norm(online_mid, vectors["lnf_g"], vectors["lnf_b"]).astype(jnp.bfloat16)
    pin_local = matmul(encoded_low, mats["w_pin"]) + local_columns(
        vectors["b_pin"], False, ways, member
    )
    pin_other = swap(pin_local)
    pin_full = jnp.where(
        member == 0,
        jnp.concatenate([pin_local, pin_other], 1),
        jnp.concatenate([pin_other, pin_local], 1),
    )
    pred_in = jnp.where(context_mask[:, None], pin_full, vectors["mask_tok"][None, :])
    pred_in = pred_in + pred_pos
    if tiled:
        target_whole = gather_dp(target_tiles)
    pred_mid, pred_kept = layer_forward(
        pred_in,
        mats,
        vectors,
        "p",
        PRED_GROUP,
        PHEAD_DIM,
        all_sides,
        ways,
        member,
        (lambda value: target_whole) if tiled else (lambda value: None),
    )
    pred_rows = layer_norm(pred_mid, vectors["plnf_g"], vectors["plnf_b"]).astype(jnp.bfloat16)
    predicted = matmul(pred_rows, mats["w_pproj"]) + local_columns(
        vectors["b_pproj"], False, ways, member
    )
    if tiled:
        target_mats = from_tiles(split_gathered(target_whole, sizes, shard, 0, shard), ways)
    else:
        target_mats = gather_flat(rows(target_params), enc_shapes(ways))
    target_patches, predicted = lax.optimization_barrier((patches, predicted))
    target_mid, _ = layer_forward(
        embed(target_patches, target_mats, target_vectors),
        target_mats,
        target_vectors,
        "",
        ENC_GROUP,
        HEAD_DIM,
        all_sides,
        ways,
        member,
    )
    targets = plain_norm(layer_norm(target_mid, target_vectors["lnf_g"], target_vectors["lnf_b"]))
    target_cols = lax.dynamic_slice_in_dim(targets, member * (D // ways), D // ways, 1)
    target_mask = (1 - context).astype(jnp.float32)
    width = D // ways
    sums = doubling(
        jnp.concatenate(
            [
                jnp.sum(target_mask[:, None] * predicted, axis=0),
                jnp.sum(target_mask[:, None] * predicted * predicted, axis=0),
                jnp.broadcast_to(jnp.sum(target_mask), (128,)),
            ]
        ),
        "dp",
    )
    sum_all, square_all, count_all = sums[:width], sums[width : 2 * width], sums[2 * width]
    difference = predicted - target_cols
    error = jnp.sum(target_mask[:, None] * jnp.abs(difference)) / (count_all * D)
    column_mean = sum_all / count_all
    column_var = square_all / count_all - column_mean * column_mean
    spread = jnp.sqrt(column_var + VAR_EPS)
    local_loss = error + jnp.sum((spread - 1.0) ** 2) / D / dp_count
    grad_var = (spread - 1.0) / (D * spread)
    grad_pred = target_mask[:, None] * (
        jnp.sign(difference) / (count_all * D)
        + 2.0 * grad_var * (predicted - column_mean) / count_all
    )
    grads = {}
    grad_low = grad_pred.astype(jnp.bfloat16)
    grads["w_pproj"] = matmul_tn(pred_rows, grad_low)
    grads["b_pproj"] = jnp.sum(grad_pred, axis=0)
    grad_normed = tensor_back(matmul_nt(grad_low, mats["w_pproj"]))
    grad_mid, grads["plnf_g"], grads["plnf_b"] = norm_backward(
        pred_mid, vectors["plnf_g"], vectors["plnf_b"], grad_normed
    )
    grad_in, layer_grads = layer_backward(
        grad_mid, pred_kept, mats, vectors, "p", PRED_GROUP, PHEAD_DIM, all_sides, lambda *_: None
    )
    grads.update(layer_grads)
    grads["mask_tok"] = jnp.sum(jnp.where(context_mask[:, None], 0.0, grad_in), axis=0)
    grad_pin = lax.dynamic_slice_in_dim(
        jnp.where(context_mask[:, None], grad_in, 0.0), member * (PD // ways), PD // ways, 1
    )
    grad_pin_low = grad_pin.astype(jnp.bfloat16)
    grads["w_pin"] = matmul_tn(encoded_low, grad_pin_low)
    grads["b_pin"] = jnp.sum(grad_pin, axis=0)
    grad_encoded = tensor_back(matmul_nt(grad_pin_low, mats["w_pin"]))
    grad_mid, grads["lnf_g"], grads["lnf_b"] = norm_backward(
        online_mid, vectors["lnf_g"], vectors["lnf_b"], grad_encoded
    )
    pred_flat = flatten_matrices([grads[label] for label, _, _ in pred_shapes(ways)])
    pred_flat, grad_mid = lax.optimization_barrier((pred_flat, grad_mid))
    pred_share = None
    if tiled:
        pred_tree = tree_scatter(pred_flat.reshape(-1, 8, 128), (0, 1, 2, 3))
        next(pred_tree)
    else:
        pred_share = lax.psum_scatter(pred_flat, "dp", scatter_dimension=0, tiled=True)
    sections = enc_vectors() + pred_vectors()
    early = []
    pred_shares = []

    def shared_part(found, label, length):
        if label in LOCAL_BIAS:
            return place_columns(found[label], length, LOCAL_BIAS[label], ways, member)
        return 0.5 * found[label]

    def all_devices(parts, after=None):
        total = doubling(doubling(jnp.concatenate(list(parts.values())), "tensor"), "dp", after)
        result = {}
        start = 0
        for label, part in parts.items():
            result[label] = total[start : start + part.shape[0]]
            start += part.shape[0]
        return result

    def early_sum(found):
        found = {**grads, **found}
        parts = {
            label: shared_part(found, label, length)
            for label, length in sections
            if label in found
        }
        parts[LOSS] = jnp.broadcast_to(local_loss, (128,))
        return all_devices(parts)

    pieces = {}
    trees = {}

    def watch(name, so_far, value):
        if not tiled:
            return None
        for label, grad in so_far.items():
            if label.startswith("w_") and label not in pieces:
                pieces[label] = to_tiles(grad.astype(jnp.bfloat16))
        if name == AT_HIDDEN:
            pred_ready = advance(pred_tree, value)
            trees[UPPER] = tree_scatter(stack_tiles(pieces, (2, 3)), (2, 3))
            return (next(trees[UPPER]), pred_ready)
        if name == AT_PACKED:
            trees[MIDDLE] = tree_scatter(stack_tiles(pieces, (1,)), (1,))
            return (advance(trees[UPPER], value), next(trees[MIDDLE]))
        if name == AT_HALF:
            pred_shares.append(advance(pred_tree, value).reshape(-1, 128))
            early.append(early_sum(so_far))
        return None

    grad_in, layer_grads = layer_backward(
        grad_mid, online_kept, mats, vectors, "", ENC_GROUP, HEAD_DIM, online_sides, watch
    )
    grads.update(layer_grads)
    grad_in_low = grad_in.astype(jnp.bfloat16)
    grads["w_patch"] = matmul_tn(patches, grad_in_low)
    grads["b_patch"] = jnp.sum(grad_in, axis=0)
    if tiled:
        pieces["w_patch"] = to_tiles(grads["w_patch"].astype(jnp.bfloat16))
        trees[LOWER] = tree_scatter(stack_tiles(pieces, (0,)), (0,))
        token = next(trees[LOWER])
        token = [advance(trees[UPPER], token), advance(trees[MIDDLE], token)]
        token = advance(trees[LOWER], token)
        token = advance(trees[MIDDLE], token)
        shares = {UPPER: advance(trees[UPPER], token)}
        token = advance(trees[LOWER], token)
        shares[MIDDLE] = advance(trees[MIDDLE], token)
        shares[LOWER] = advance(trees[LOWER], token)
        share = jnp.where(
            place[0] >= 8,
            shares[UPPER],
            jnp.where(place[0] >= 4, shares[MIDDLE], shares[LOWER]),
        )
        enc_square = jnp.square(share.astype(jnp.float32))
        enc_share = unpack_tiles(share, place, spans)
    else:
        enc_share = scatter_flat(grads, enc_shapes(ways), jnp.float32)
        enc_square = enc_share * enc_share
    if not early:
        early.append(early_sum(grads))
    sums = dict(early[0])
    loss_value = sums.pop(LOSS)[0]
    if tiled:
        pred_share = pred_shares[0]
    square_sum = jnp.sum(enc_square) + jnp.sum(pred_share * pred_share)
    late = {label: shared_part(grads, label, length) for label, length in sections}
    late = {label: part for label, part in late.items() if label not in sums}
    late[SQUARE] = jnp.broadcast_to(square_sum, (128,))
    sums.update(all_devices(late, enc_share))
    square_total = sums.pop(SQUARE)[0]
    vector_grad = jnp.concatenate([sums[label] for label, _ in sections])
    grad_norm = jnp.sqrt(square_total + jnp.sum(vector_grad * vector_grad))
    factor = jnp.minimum(1.0, CLIP / (grad_norm + 1e-06))
    count = step_count[0].astype(jnp.float32)
    scalars = jnp.stack(
        [factor, 1.0 / (1 - BETA_ONE**count), 1.0 / (1 - BETA_TWO**count)]
    ).astype(jnp.float32)
    back = lambda x: x.reshape(1, -1)
    new_enc, enc_first, enc_second, new_target = map(
        back,
        adam_flat(
            scalars,
            [rows(enc_params), rows(enc_m1), rows(enc_m2), enc_share, rows(target_params)],
        ),
    )
    new_pred, pred_first, pred_second = map(
        back, adam_flat(scalars, [rows(pred_params), rows(pred_m1), rows(pred_m2), pred_share])
    )
    new_vec, vec_first, vec_second = adam(
        vecs, vec_m1, vec_m2, vector_grad * factor, RATE_VEC, 0.0, count
    )
    new_target_vec = TAU * target_vecs + (1 - TAU) * new_vec[: target_vecs.shape[0]]
    return (
        new_enc,
        enc_first,
        enc_second,
        new_enc.astype(jnp.bfloat16),
        new_pred,
        pred_first,
        pred_second,
        new_pred.astype(jnp.bfloat16),
        new_target,
        new_vec,
        vec_first,
        vec_second,
        new_target_vec,
        loss_value,
        grad_norm,
    )


def solution(mesh):
    placed = (
        P("tensor", "dp"),
        P("tensor", "dp"),
        P("tensor", "dp"),
        P("tensor", "dp"),
        P("tensor", "dp"),
        P("tensor", "dp"),
        P("tensor", "dp"),
        P(),
        P(),
        P(),
        P(),
        P("dp", "tensor"),
        P("dp"),
        P("dp"),
        P(),
    )
    return jax.shard_map(
        shards,
        mesh=mesh,
        in_specs=placed,
        out_specs=(
            P("tensor", "dp"),
            P("tensor", "dp"),
            P("tensor", "dp"),
            P("tensor", "dp"),
            P("tensor", "dp"),
            P("tensor", "dp"),
            P("tensor", "dp"),
            P("tensor", "dp"),
            P("tensor", "dp"),
            P(),
            P(),
            P(),
            P(),
            P(),
            P(),
        ),
        check_vma=False,
    )
```

```python
import functools
import math

import jax
import jax.numpy as jnp
from jax import lax
from jax.experimental import pallas as pl
from jax.experimental.pallas import tpu as pltpu
from jax.sharding import PartitionSpec as P

D = 1024
HEADS = 16
HEAD_DIM = 64
MLP = 4096
PATCH = 1536
PD = 384
PHEADS = 12
PHEAD_DIM = 32
PMLP = 1536


BETA_ONE = 0.9
BETA_TWO = 0.999
ADAM_EPS = 1e-08
RATE_MAT = 0.01
RATE_VEC = 0.05
DECAY = 0.05
CLIP = 0.0002
TAU = 0.75
NORM_EPS = 1e-06
VAR_EPS = 0.0001
LOCAL_BIAS = {
    "b_qkv": True,
    "b_pqkv": True,
    "b_up": False,
    "b_pup": False,
    "b_pin": False,
    "b_pproj": False,
}
ROW_GAINS = ("ln2_g", "ln2_b", "pln2_g", "pln2_b")


def enc_shapes(ways):
    return [
        ("w_patch", PATCH // ways, D),
        ("w_qkv", D, 3 * D // ways),
        ("w_out", D // ways, D),
        ("w_up", D, MLP // ways),
        ("w_down", MLP // ways, D),
    ]


def pred_shapes(ways):
    return [
        ("w_pin", D, PD // ways),
        ("w_pqkv", PD, 3 * PD // ways),
        ("w_pout", PD // ways, PD),
        ("w_pup", PD, PMLP // ways),
        ("w_pdown", PMLP // ways, PD),
        ("w_pproj", PD, D // ways),
    ]


def enc_vectors():
    return [
        ("b_patch", D),
        ("ln1_g", D),
        ("ln1_b", D),
        ("b_qkv", 3 * D),
        ("b_out", D),
        ("ln2_g", D),
        ("ln2_b", D),
        ("b_up", MLP),
        ("b_down", D),
        ("lnf_g", D),
        ("lnf_b", D),
    ]


def pred_vectors():
    return [
        ("b_pin", PD),
        ("mask_tok", PD),
        ("pln1_g", PD),
        ("pln1_b", PD),
        ("b_pqkv", 3 * PD),
        ("b_pout", PD),
        ("pln2_g", PD),
        ("pln2_b", PD),
        ("b_pup", PMLP),
        ("b_pdown", PD),
        ("plnf_g", PD),
        ("plnf_b", PD),
        ("b_pproj", D),
    ]


def unflat(flat_row, shapes):
    result = {}
    offset = 0
    for label, height, breadth in shapes:
        result[label] = flat_row[offset : offset + height * breadth].reshape(height, breadth)
        offset += height * breadth
    return result


def split_vector(vector, sections):
    result = {}
    offset = 0
    for label, length in sections:
        result[label] = vector[offset : offset + length]
        offset += length
    return result


def positions(segment_row):
    earlier = jnp.sum((segment_row[None, :] < segment_row[:, None]).astype(jnp.int32), axis=1)
    return (jnp.arange(segment_row.shape[0], dtype=jnp.int32) - earlier).astype(jnp.float32)


def sincos(places, width):
    half_width = width // 2
    freqs = jnp.exp(-math.log(10000.0) * jnp.arange(half_width).astype(jnp.float32) / half_width)
    angles = places[:, None] * freqs[None, :]
    return jnp.concatenate([jnp.sin(angles), jnp.cos(angles)], axis=1)


def layer_norm(values, gain, shift):
    centered = values - jnp.mean(values, axis=-1, keepdims=True)
    spread = jnp.mean(centered * centered, axis=-1, keepdims=True)
    return centered * lax.rsqrt(spread + NORM_EPS) * gain + shift


def plain_norm(values):
    centered = values - jnp.mean(values, axis=-1, keepdims=True)
    return centered * lax.rsqrt(jnp.mean(centered * centered, axis=-1, keepdims=True) + NORM_EPS)


def norm_backward(values, gain, shift, cotangent):
    return jax.vjp(layer_norm, values, gain, shift)[1](cotangent)


def matmul(left, right):
    return jnp.dot(left, right, preferred_element_type=jnp.float32)


def matmul_tn(left, right):
    return lax.dot_general(
        left, right, (((0,), (0,)), ((), ())), preferred_element_type=jnp.float32
    )


def matmul_nt(left, right):
    return lax.dot_general(
        left, right, (((1,), (1,)), ((), ())), preferred_element_type=jnp.float32
    )


def local_columns(vector, thirds, ways, member):
    if thirds:
        width = vector.shape[0] // 3
        slab = vector.reshape(3, width)
        return lax.dynamic_slice_in_dim(slab, member * (width // ways), width // ways, 1).reshape(
            -1
        )
    return lax.dynamic_slice_in_dim(
        vector, member * (vector.shape[0] // ways), vector.shape[0] // ways, 0
    )


def place_columns(local, length, thirds, ways, member):
    if thirds:
        slab = jnp.zeros((3, length // 3), jnp.float32)
        placed = lax.dynamic_update_slice_in_dim(
            slab, local.reshape(3, -1), member * (length // 3 // ways), 1
        )
        return placed.reshape(-1)
    return lax.dynamic_update_slice_in_dim(
        jnp.zeros((length,), jnp.float32), local, member * (length // ways), 0
    )


QB = 256
LOG2E = math.log2(math.e)

def roundup(n, m):
    return -(-n // m) * m

def dot_nn(a, b):
    return lax.dot_general(a, b, (((1,), (0,)), ((), ())), preferred_element_type=jnp.float32)

def dot_nt(a, b):
    return lax.dot_general(a, b, (((1,), (1,)), ((), ())), preferred_element_type=jnp.float32)

def pad_rows(x, n):
    return jnp.concatenate([x.astype(jnp.float32), jnp.zeros((n - x.shape[0], x.shape[1]), jnp.float32)], 0).astype(x.dtype)

def lane_keep(x, lo, hi):
    lane = lax.broadcasted_iota(jnp.int32, (1, x.shape[1]), 1)
    keep = jnp.where((lane >= lo) & (lane < hi), 1.0, 0.0).astype(x.dtype)
    return x * keep

def attn_fwd_kernel(heads, e, T, TP, W, packed_ref, qa_ref, ka_ref, o_ref, lse_ref, q_s, k_s, v_s, o_s, s_s, p_s):
    g = pl.program_id(0)
    base = pl.multiple_of(g * 128, 128)
    q_s[...] = pad_rows(packed_ref[:, pl.ds(base, 128)], TP)
    k_s[:, :128] = pad_rows(packed_ref[:, pl.ds(base + W, 128)], TP)
    k_s[:, 128:] = ka_ref[...]
    v_s[...] = pad_rows(packed_ref[:, pl.ds(base + 2 * W, 128)], TP)
    scale = e ** -0.5 * LOG2E
    lane = lax.broadcasted_iota(jnp.int32, (QB, 128), 1)
    step = 16
    units = [(i, h) for i in range(TP // QB) for h in range(heads)]

    def scores(n):
        i, h = units[n]
        rows = slice(i * QB, (i + 1) * QB)
        qq = jnp.concatenate([lane_keep(q_s[rows, :], h * e, (h + 1) * e), qa_ref[rows, :]], 1)
        s_s[n % 2] = dot_nt(qq, k_s[...])

    scores(0)
    for n, (i, h) in enumerate(units):
        if n + 1 < len(units):
            scores(n + 1)
        rows = slice(i * QB, (i + 1) * QB)
        peaks, totals = [], []
        for r in range(0, QB, step):
            s = s_s[n % 2, r : r + step, :] * scale
            peak = jnp.max(s, axis=1, keepdims=True)
            p = jnp.exp2(s - peak)
            total = jnp.sum(p, axis=1, keepdims=True)
            p_s[n % 2, r : r + step, :] = p.astype(jnp.bfloat16)
            peaks.append(peak)
            totals.append(total)
        total = jnp.concatenate(totals, 0)
        o = dot_nn(p_s[n % 2], v_s[...]) * (1.0 / total)
        stat = jnp.concatenate(peaks, 0) + jnp.log2(total)
        if h == 0:
            out = o
            stats = jnp.broadcast_to(stat, (QB, 128))
        else:
            out = jnp.where(lane < h * e, out, o)
            stats = jnp.where(lane < h, stats, stat)
        if h == heads - 1:
            if heads * e < 128:
                out = jnp.where(lane < heads * e, out, 0.0)
            o_s[rows, :] = out.astype(jnp.bfloat16)
            lse_ref[0, :, rows] = stats.T[:8, :]
    o_ref[...] = o_s[:T, :]

def attn_fwd(packed, qa, ka, heads, e):
    T, W3 = packed.shape
    W = W3 // 3
    TP = roundup(T, QB)
    groups = W // 128
    return pl.pallas_call(
        functools.partial(attn_fwd_kernel, heads, e, T, TP, W),
        grid=(groups,),
        in_specs=[pl.BlockSpec((T, W3), lambda g: (0, 0)), pl.BlockSpec((TP, 128), lambda g: (0, 0)), pl.BlockSpec((TP, 128), lambda g: (0, 0))],
        out_specs=[pl.BlockSpec((T, 128), lambda g: (0, g)), pl.BlockSpec((1, 8, TP), lambda g: (g, 0, 0))],
        out_shape=[jax.ShapeDtypeStruct((T, W), jnp.bfloat16), jax.ShapeDtypeStruct((groups, 8, TP), jnp.float32)],
        scratch_shapes=[pltpu.VMEM((TP, 128), jnp.bfloat16), pltpu.VMEM((TP, 256), jnp.bfloat16), pltpu.VMEM((TP, 128), jnp.bfloat16), pltpu.VMEM((TP, 128), jnp.bfloat16), pltpu.VMEM((2, QB, TP), jnp.float32), pltpu.VMEM((2, QB, TP), jnp.bfloat16)],
        compiler_params=pltpu.CompilerParams(vmem_limit_bytes=48 << 20),
        cost_estimate=pl.CostEstimate(flops=groups * heads * 4 * T * T * 256, bytes_accessed=T * W3 * 3, transcendentals=groups * heads * T * T),
        name="attn_fwd",
    )(packed, qa, ka)

def attn_bwd_kernel(heads, e, T, TP, W, first, chained, packed_ref, do_ref, qa_ref, ka_ref, lse_ref, *rest):
    d_ref, q_s, k_s, v_s, do_s, dk_s, dv_s, dq_s, out_s, s_s, d_s, p_s, ds_s, sems = rest[1:] if chained else rest
    g = pl.program_id(0) + first
    base = pl.multiple_of(g * 128, 128)
    q_s[:, :128] = pad_rows(packed_ref[:, pl.ds(base, 128)], TP)
    q_s[:, 128:] = qa_ref[...]
    k = pad_rows(packed_ref[:, pl.ds(base + W, 128)], TP)
    k_s[...] = k
    v_s[...] = pad_rows(packed_ref[:, pl.ds(base + 2 * W, 128)], TP)
    do_s[...] = pad_rows(do_ref[...], TP)
    kt = k.astype(jnp.float32).T.astype(jnp.bfloat16)
    sub = lax.broadcasted_iota(jnp.int32, (128, 1), 0)
    lane = lax.broadcasted_iota(jnp.int32, (TP, 128), 1)
    scale2 = e ** -0.5 * LOG2E
    scale = e ** -0.5
    step = 64
    blocks = TP // QB
    units = [(h, i) for h in range(heads) for i in range(blocks)]

    def products(n):
        h, i = units[n]
        rows = slice(i * QB, (i + 1) * QB)
        lo, hi = h * e, (h + 1) * e
        kk = jnp.concatenate([lane_keep(k_s[...], lo, hi), ka_ref[...]], 1)
        s_s[n % 2] = dot_nt(kk, q_s[rows, :])
        d_s[n % 2] = dot_nt(lane_keep(v_s[...], lo, hi), do_s[rows, :])

    def gather(h):
        lo, hi = h * e, (h + 1) * e
        dv = dot_nn(p_s[h % 2], do_s[...])
        dk = dot_nn(ds_s[h % 2], q_s[:, :128])
        dq = dot_nn(kt * jnp.where((sub >= lo) & (sub < hi), 1.0, 0.0).astype(jnp.bfloat16), ds_s[h % 2])
        if h == 0:
            dv_s[...], dk_s[...], dq_s[...] = dv, dk, dq
        else:
            dv_s[...] = jnp.where(lane < lo, dv_s[...], dv)
            dk_s[...] = jnp.where(lane < lo, dk_s[...], dk)
            dq_s[...] += dq

    products(0)
    for n, (h, i) in enumerate(units):
        if n + 1 < len(units):
            products(n + 1)
        rows = slice(i * QB, (i + 1) * QB)
        lse = lse_ref[0, h : h + 1, rows]
        d = jnp.zeros((8, QB), jnp.float32)
        for r in range(0, TP, step):
            part = slice(r, r + step)
            pt = jnp.exp2(s_s[n % 2, part, :] * scale2 - lse)
            s_s[n % 2, part, :] = pt
            p_s[h % 2, part, rows] = pt.astype(jnp.bfloat16)
            d += jnp.sum((pt * d_s[n % 2, part, :]).reshape(step // 8, 8, QB), axis=0)
        d = jnp.sum(d, axis=0, keepdims=True)
        for r in range(0, TP, step):
            part = slice(r, r + step)
            ds_s[h % 2, part, rows] = (s_s[n % 2, part, :] * (d_s[n % 2, part, :] - d)).astype(jnp.bfloat16)
        if h and i == 0:
            gather(h - 1)
    gather(heads - 1)
    if heads * e < 128:
        dv_s[...] = jnp.where(lane < heads * e, dv_s[...], 0.0)
        dk_s[...] = jnp.where(lane < heads * e, dk_s[...], 0.0)
    dq = dq_s[...].T * scale
    out_s[0] = dq.astype(jnp.bfloat16)[:T]
    out_s[1] = (dk_s[...] * scale).astype(jnp.bfloat16)[:T]
    out_s[2] = dv_s[...].astype(jnp.bfloat16)[:T]
    copies = [
        pltpu.make_async_copy(out_s.at[i], d_ref.at[:, pl.ds(base + i * W, 128)], sems.at[i])
        for i in range(3)
    ]
    for copy in copies:
        copy.start()
    for copy in copies:
        copy.wait()

def attn_bwd(packed, do, qa, ka, lse, heads, e, first=0, groups=None, so_far=None):
    T, W3 = packed.shape
    W = W3 // 3
    TP = roundup(T, QB)
    groups = W // 128 if groups is None else groups
    chained = so_far is not None
    full = lambda g: (0, 0)
    return pl.pallas_call(
        functools.partial(attn_bwd_kernel, heads, e, T, TP, W, first, chained),
        grid=(groups,),
        in_specs=[pl.BlockSpec((T, W3), full), pl.BlockSpec((T, 128), lambda g: (0, g + first)), pl.BlockSpec((TP, 128), full), pl.BlockSpec((TP, 128), full), pl.BlockSpec((1, 8, TP), lambda g: (g + first, 0, 0))]
        + ([pl.BlockSpec(memory_space=pl.ANY)] if chained else []),
        out_specs=pl.BlockSpec(memory_space=pl.ANY),
        input_output_aliases={5: 0} if chained else {},
        out_shape=jax.ShapeDtypeStruct((T, W3), jnp.bfloat16),
        scratch_shapes=[pltpu.VMEM((TP, 256), jnp.bfloat16), pltpu.VMEM((TP, 128), jnp.bfloat16), pltpu.VMEM((TP, 128), jnp.bfloat16), pltpu.VMEM((TP, 128), jnp.bfloat16), pltpu.VMEM((TP, 128), jnp.float32), pltpu.VMEM((TP, 128), jnp.float32), pltpu.VMEM((128, TP), jnp.float32), pltpu.VMEM((3, T, 128), jnp.bfloat16), pltpu.VMEM((2, TP, QB), jnp.float32), pltpu.VMEM((2, TP, QB), jnp.float32), pltpu.VMEM((2, TP, TP), jnp.bfloat16), pltpu.VMEM((2, TP, TP), jnp.bfloat16), pltpu.SemaphoreType.DMA((3,))],
        compiler_params=pltpu.CompilerParams(vmem_limit_bytes=48 << 20),
        cost_estimate=pl.CostEstimate(flops=groups * heads * 10 * T * T * 256, bytes_accessed=T * W3 * 5, transcendentals=groups * heads * T * T),
        name="attn_bwd",
    )(packed, do, qa, ka, lse, *([so_far] if chained else []))

def mask_sides(segment, context_row, TP):
    T = segment.shape[0]
    s = jnp.arange(128)[None, :]
    one = (segment[:, None] == s)
    qa = jnp.where(one, -1e30, 0.0).astype(jnp.bfloat16)
    ka = jnp.where((s < 8) & ~(one & (context_row[:, None] > 0)), 1.0, 0.0).astype(jnp.bfloat16)
    qa = jnp.concatenate([qa, jnp.zeros((TP - T, 128), jnp.bfloat16)], 0)
    ka = jnp.concatenate([ka, jnp.broadcast_to(jnp.where(s < 8, 1.0, 0.0).astype(jnp.bfloat16), (TP - T, 128))], 0)
    return qa, ka


CHUNK = 16384
UNIT = 3 * CHUNK
SWAP = ((0, 1), (1, 0))


def swap(x):
    return lax.ppermute(x, "tensor", SWAP)


def tensor_total(part):
    return part + swap(part)


def tensor_back(part):
    low = part.astype(jnp.bfloat16)
    return low.astype(jnp.float32) + swap(low).astype(jnp.float32)


def doubling(x, axis, after=None):
    size = lax.axis_size(axis)
    if size & (size - 1):
        return lax.psum(x, axis)
    stride = 1
    while stride < size:
        reach = 4 if size // stride % 4 == 0 else 2
        others = [
            lax.ppermute(x, axis, [(i, i ^ (m * stride)) for i in range(size)])
            for m in range(1, reach)
        ]
        if stride * reach >= size:
            others = pin(others, after)
        x = x + others[0]
        if reach == 4:
            x = x + (others[1] + others[2])
        stride *= reach
    return x


def pin(x, after):
    return x if after is None else lax.optimization_barrier((x, after))[0]


def tile_width(label):
    return {"w_qkv": 12, "w_up": 16}.get(label, 8)


def enc_chunks(ways):
    spans = []
    start = 0
    for label, height, breadth in enc_shapes(ways):
        count = height * breadth // CHUNK
        spans.append((start, start + count, breadth // 128))
        start += count
    return spans


def regions(unit, spans, emit):
    first = unit * 3
    wide = [s for s in spans if s[2] == 12]
    flat = [s for s in spans if s[2] != 12]
    in_wide = functools.reduce(jnp.logical_or, [(first >= a) & (first < b) for a, b, _ in wide])

    @pl.when(in_wide)
    def _():
        emit(0, 0, 12, 4)

    @pl.when(jnp.logical_not(in_wide))
    def _():
        for c in range(3):
            for width in (8, 16):
                hit = functools.reduce(
                    jnp.logical_or,
                    [(first + c >= a) & (first + c < b) for a, b, w in flat if w == width],
                )

                @pl.when(hit)
                def _():
                    emit(c * 128, c * 16, width, 16 // width)


def pack_kernel(spans, units, place_ref, x_ref, o_ref):
    def emit(row, tile, width, groups):
        for t in range(groups):
            for j in range(width):
                o_ref[tile + t * width + j] = x_ref[
                    pl.ds(row + t * 8 * width + j, 8, stride=width), :
                ].astype(jnp.bfloat16)

    regions(place_ref[0] * units + pl.program_id(0), spans, emit)


def pack_tiles(flat, place, spans):
    units = flat.shape[0] // 384
    return pl.pallas_call(
        functools.partial(pack_kernel, spans, units),
        grid_spec=pltpu.PrefetchScalarGridSpec(
            num_scalar_prefetch=1,
            grid=(units,),
            in_specs=[pl.BlockSpec((384, 128), lambda i, s: (i, 0))],
            out_specs=pl.BlockSpec((48, 8, 128), lambda i, s: (i, 0, 0)),
        ),
        out_shape=jax.ShapeDtypeStruct((units * 48, 8, 128), jnp.bfloat16),
        name="pack",
    )(place, flat)


def unpack_kernel(spans, units, place_ref, x_ref, o_ref):
    def emit(row, tile, width, groups):
        for t in range(groups):
            for j in range(width):
                o_ref[pl.ds(row + t * 8 * width + j, 8, stride=width), :] = x_ref[
                    tile + t * width + j
                ].astype(jnp.float32)

    regions(place_ref[0] * units + pl.program_id(0), spans, emit)


def unpack_tiles(tiles, place, spans):
    units = tiles.shape[0] // 48
    return pl.pallas_call(
        functools.partial(unpack_kernel, spans, units),
        grid_spec=pltpu.PrefetchScalarGridSpec(
            num_scalar_prefetch=1,
            grid=(units,),
            in_specs=[pl.BlockSpec((48, 8, 128), lambda i, s: (i, 0, 0))],
            out_specs=pl.BlockSpec((384, 128), lambda i, s: (i, 0)),
        ),
        out_shape=jax.ShapeDtypeStruct((units * 384, 128), jnp.float32),
        name="unpack",
    )(place, tiles)


def adam_kernel(with_target, scalars, p_ref, m_ref, v_ref, g_ref, *rest):
    if with_target:
        t_ref, po_ref, mo_ref, vo_ref, to_ref = rest
    else:
        po_ref, mo_ref, vo_ref = rest
    grad = g_ref[...] * scalars[0]
    first = BETA_ONE * m_ref[...] + (1 - BETA_ONE) * grad
    second = BETA_TWO * v_ref[...] + (1 - BETA_TWO) * grad * grad
    weight = p_ref[...]
    ratio = (first * scalars[1]) / (jnp.sqrt(second * scalars[2]) + ADAM_EPS)
    weight = weight - RATE_MAT * (ratio + DECAY * weight)
    po_ref[...] = weight
    mo_ref[...] = first
    vo_ref[...] = second
    if with_target:
        to_ref[...] = TAU * t_ref[...] + (1 - TAU) * weight


def adam_flat(scalars, arrays):
    rows = arrays[0].shape[0]
    parts = next((n for n in (9, 6, 3) if rows % (8 * n) == 0), 1)
    with_target = len(arrays) == 5
    spec = pl.BlockSpec((rows // parts, 128), lambda i: (i, 0))
    n_out = 4 if with_target else 3
    return pl.pallas_call(
        functools.partial(adam_kernel, with_target),
        grid=(parts,),
        in_specs=[pl.BlockSpec(memory_space=pltpu.SMEM)] + [spec] * len(arrays),
        out_specs=[spec] * n_out,
        out_shape=[jax.ShapeDtypeStruct((rows, 128), jnp.float32)] * n_out,
        compiler_params=pltpu.CompilerParams(vmem_limit_bytes=60 << 20),
        name="adam",
    )(scalars, *arrays)


def from_tiles(parts, ways):
    result = {}
    for tiles, (label, height, breadth) in zip(parts, enc_shapes(ways)):
        piece = tiles.reshape(height // 8, breadth // 128, 8, 128)
        result[label] = piece.transpose(0, 2, 1, 3).reshape(height, breadth)
    return result


def to_tiles(matrix):
    height, breadth = matrix.shape
    return (
        matrix.reshape(height // 8, 8, breadth // 128, 128)
        .transpose(0, 2, 1, 3)
        .reshape(height * breadth // 1024, 8, 128)
    )


def gather_dp(x):
    return lax.all_gather(x, "dp", axis=0, tiled=True)


def tree_gather(tiles):
    place = lax.axis_index("dp")
    z, y, x = place // 4, place // 2 % 2, place % 2
    half = tiles.shape[0] // 2
    over_x, over_y = ([(i, i ^ bit) for i in range(16)] for bit in (1, 2))
    ring_up = [(i, (i + 4) % 16) for i in range(16)]
    ring_down = [(j, i) for i, j in ring_up]
    a, b = tiles[:half], tiles[half:]
    arrived = []
    waits = None
    for k in range(4):
        ax, by = permute(a, over_x), permute(b, over_y)
        ay, bx = permute(a, over_y), permute(b, over_x)
        axy, byx = permute(ax, over_y), permute(by, over_x)
        za, zb = (z - k) % 4, (z + k) % 4
        arrived.append([(0, za, y, x, a), (1, zb, y, x, b)])
        arrived.append([(0, za, y, 1 - x, ax), (1, zb, 1 - y, x, by)])
        arrived.append([(0, za, 1 - y, x, ay), (1, zb, y, 1 - x, bx)])
        arrived.append([(0, za, 1 - y, 1 - x, axy), (1, zb, 1 - y, 1 - x, byx)])
        if k == 1:
            begun = (a, b)
        if k == 2:
            first = (ax, by, ay, bx) + last
        if k == 3:
            first = first + (a, b)
            nearly = (ax, by, ay, bx)
        last = (axy, byx)
        a, b = pin((a, b), waits)
        waits = (ax, by, ay, bx) if k == 0 else (ax, by, ay, bx, axy, byx)
        if k < 3:
            a, b = permute(a, ring_up), permute(b, ring_down)
    zero = pin(jnp.zeros((), tiles.dtype), first)
    whole = jnp.broadcast_to(zero, (32, half) + tiles.shape[1:])
    for n in sorted(range(16), key=lambda n: (n // 4 * 2 + n % 4, n)):
        for side, pz, py, px, piece in arrived[n]:
            slot = (pz * 4 + py * 2 + px) * 2 + side
            whole = lax.dynamic_update_index_in_dim(whole, piece, slot, 0)
    return whole.reshape((32 * half,) + tiles.shape[1:]), begun, nearly


def split_gathered(gathered, sizes, part, first, total):
    results = []
    start = 0
    for size in sizes:
        moves = []
        for device in range(gathered.shape[0] // total):
            low, high = max(start, device * part), min(start + size, (device + 1) * part)
            if low < high:
                source = device * total + first + low - device * part
                moves.append((0, source, low - start, high - low))
        results.append(copy_tiles([gathered], moves, size, pltpu.HBM, 52))
        start += size
    return results


def gather_flat(flat, shapes):
    return unflat(gather_dp(flat.astype(jnp.bfloat16)).reshape(-1), shapes)


def flat_kernel(shapes, *refs):
    ins, out, column = refs[:-2], refs[-2], refs[-1]

    def by_turns(ref, first, width, height):
        column[:height, :width] = ref[:, first : first + width]
        pairs = height // 2
        return column[pl.ds(0, pairs, stride=2), :], column[pl.ds(1, pairs, stride=2), :]

    base = 0
    for ref, (height, breadth) in zip(ins, shapes):
        full = breadth // 128
        if breadth % 128 == 0:
            for j in range(full):
                out[pl.ds(base + j, height, stride=full), :] = ref[:, j * 128 : (j + 1) * 128]
        else:
            pairs = height // 2
            step = 2 * full + 1
            even, odd = zip(*[by_turns(ref, j * 128, 128, height) for j in range(full)])
            even_end, odd_end = [e[:, :64] for e in by_turns(ref, full * 128, 64, height)]
            rows = list(even) + [jnp.concatenate([even_end, odd[0][:, :64]], 1)]
            for j in range(full):
                after = odd[j + 1][:, :64] if j + 1 < full else odd_end
                rows.append(jnp.concatenate([odd[j][:, 64:], after], 1))
            for j, row in enumerate(rows):
                out[pl.ds(base + j, pairs, stride=step), :] = row
        base += height * breadth // 128


def flatten_matrices(matrices):
    shapes = [m.shape for m in matrices]
    total = sum(h * b for h, b in shapes) // 128
    return pl.pallas_call(
        functools.partial(flat_kernel, shapes),
        in_specs=[pl.BlockSpec(memory_space=pltpu.VMEM)] * len(matrices),
        out_specs=pl.BlockSpec(memory_space=pltpu.VMEM),
        out_shape=jax.ShapeDtypeStruct((total, 128), jnp.float32),
        scratch_shapes=[pltpu.VMEM((max(h for h, _ in shapes), 128), jnp.float32)],
        compiler_params=pltpu.CompilerParams(vmem_limit_bytes=40 << 20),
        name="flatten",
    )(*matrices)


def scatter_flat(grads, shapes, kind):
    whole = jnp.concatenate(
        [grads[label].astype(kind).reshape(-1, 128) for label, _, _ in shapes], 0
    )
    return lax.psum_scatter(whole, "dp", scatter_dimension=0, tiled=True).astype(jnp.float32)


def permute(x, pairs):
    return lax.ppermute(x, "dp", pairs)


ENC_TILES = [(label, height * breadth // 1024) for label, height, breadth in enc_shapes(2)]


def plus(a, b):
    return a.astype(jnp.float32) + b.astype(jnp.float32)


def pick(x, index, axis):
    return lax.dynamic_index_in_dim(x, index, axis, keepdims=False)


def stack_kernel(moves, count, *refs):
    ins, out, sems = refs[:count], refs[count], refs[count + 1]
    copies = [
        pltpu.make_async_copy(
            ins[source].at[pl.ds(first, length)], out.at[pl.ds(target, length)], sems.at[number]
        )
        for number, (source, first, target, length) in enumerate(moves)
    ]
    for copy in copies:
        copy.start()
    for copy in copies:
        copy.wait()


def copy_tiles(sources, moves, length, space=pl.ANY, room=24):
    return pl.pallas_call(
        functools.partial(stack_kernel, moves, len(sources)),
        in_specs=[pl.BlockSpec(memory_space=space)] * len(sources),
        out_specs=pl.BlockSpec(memory_space=pltpu.VMEM),
        out_shape=jax.ShapeDtypeStruct((length, 8, 128), jnp.bfloat16),
        scratch_shapes=[pltpu.SemaphoreType.DMA((len(moves),))],
        compiler_params=pltpu.CompilerParams(vmem_limit_bytes=room << 20),
        name="stack",
    )(*sources)


def stack_tiles(pieces, planes):
    shard = sum(size for _, size in ENC_TILES) // 16
    low, high = planes[0] * 4 * shard, (planes[-1] + 1) * 4 * shard
    moves, used = [], []
    start = 0
    for label, size in ENC_TILES:
        first, last = max(low, start), min(high, start + size)
        if first < last:
            moves.append((len(used), first - start, first - low, last - first))
            used.append(pieces[label])
        start += size
    return copy_tiles(used, moves, high - low)


def tree_scatter(tiles, planes):
    low = jnp.bfloat16
    place = lax.axis_index("dp")
    z, near = place // 4, place % 4
    count = len(planes)
    copies = 4 // count
    size = tiles.shape[0] // (4 * count * copies)
    grid = tiles.reshape((count, 4, copies, size) + tiles.shape[1:])

    def exchange(take, at, stride):
        ready = [take(at ^ m) for m in range(1, 4)]
        sent = [
            permute(ready[m - 1], [(i, i ^ (m * stride)) for i in range(16)]) for m in range(1, 4)
        ]
        return ready, sent

    ready, sent = exchange(lambda n: pick(grid, n, 1).astype(low), near, 1)
    after = yield ready
    sent = pin(sent, after)
    plane_sum = sum(part.astype(jnp.float32) for part in [pick(grid, near, 1)] + sent)
    blocks = plane_sum.swapaxes(0, 1).reshape((4, size) + tiles.shape[1:])
    ready, sent = exchange(lambda n: pick(blocks, n, 0).astype(low), z, 4)
    after = yield ready
    sent = pin(sent, after)
    held = sum(part.astype(jnp.float32) for part in [pick(blocks, z, 0)] + sent)
    if copies == 1:
        yield held
    held = held.astype(low)
    got = []
    for c in range(copies):
        pairs = [
            ((c * count + j) * 4 + i, planes[j] * 4 + i)
            for j in range(count)
            for i in range(4)
            if c * count + j != planes[j]
        ]
        stay = [planes[j] for j in range(count) if c * count + j == planes[j]]
        piece = permute(held, pairs) if pairs else held
        if pairs and stay:
            piece = jnp.where(functools.reduce(jnp.logical_or, [z == p for p in stay]), held, piece)
        got.append(piece)
    after = yield [held]
    yield jnp.concatenate(pin(got, after), 0)


def advance(tree, after):
    return tree.send(after)


def group_pad(x, axis, e, per_group):
    used = e * per_group
    shape = x.shape
    parts = x.reshape(shape[:axis] + (shape[axis] // used, used) + shape[axis + 1 :])
    widths = [(0, 0)] * parts.ndim
    widths[axis + 1] = (0, 128 - used)
    padded = jnp.pad(parts, widths)
    return padded.reshape(shape[:axis] + (shape[axis] // used * 128,) + shape[axis + 1 :])


def group_cut(x, axis, e, per_group):
    used = e * per_group
    shape = x.shape
    parts = x.reshape(shape[:axis] + (shape[axis] // 128, 128) + shape[axis + 1 :])
    parts = lax.slice_in_dim(parts, 0, used, axis=axis + 1)
    return parts.reshape(shape[:axis] + (shape[axis] // 128 * used,) + shape[axis + 1 :])


def layer_forward(
    stream, mats, vectors, tag, per_group, head_dim, sides, ways, member, watch=lambda value: None
):
    normed_low = layer_norm(stream, vectors[tag + "ln1_g"], vectors[tag + "ln1_b"]).astype(
        jnp.bfloat16
    )
    bias = group_pad(
        local_columns(vectors["b_" + tag + "qkv"], True, ways, member), 0, head_dim, per_group
    )
    packed = (matmul(normed_low, mats["w_" + tag + "qkv"]) + bias).astype(jnp.bfloat16)
    mixed_rows, log_totals = attn_fwd(packed, sides[0], sides[1], per_group, head_dim)
    attn_part = matmul(mixed_rows, mats["w_" + tag + "out"])
    middle = stream + tensor_total(attn_part) + vectors["b_" + tag + "out"]
    normed_two = layer_norm(middle, vectors[tag + "ln2_g"], vectors[tag + "ln2_b"]).astype(
        jnp.bfloat16
    )
    hidden = matmul(normed_two, mats["w_" + tag + "up"]) + local_columns(
        vectors["b_" + tag + "up"], False, ways, member
    )
    activated = lax.optimization_barrier(jax.nn.gelu(hidden).astype(jnp.bfloat16))
    down_part = matmul(activated, mats["w_" + tag + "down"])
    down_part = pin(down_part, watch(down_part))
    result = middle + tensor_total(down_part) + vectors["b_" + tag + "down"]
    kept = (
        stream,
        normed_low,
        packed,
        mixed_rows,
        log_totals,
        middle,
        normed_two,
        hidden,
        activated,
    )
    return (result, kept)


def gelu_slope(x):
    scale, cubic = math.sqrt(2 / math.pi), 0.044715
    square = x * x
    bend = jnp.tanh(scale * x * (1 + cubic * square))
    return 0.5 * (1 + bend) + (0.5 * scale) * x * (1 - bend * bend) * (1 + 3 * cubic * square)


def layer_backward(grad_out, kept, mats, vectors, tag, per_group, head_dim, sides, watch):
    (
        stream,
        normed_low,
        packed,
        mixed_rows,
        log_totals,
        middle,
        normed_two,
        hidden,
        activated,
    ) = kept
    grads = {}
    grad_low = grad_out.astype(jnp.bfloat16)
    grads["w_" + tag + "down"] = matmul_tn(activated, grad_low)
    grads["b_" + tag + "down"] = jnp.sum(grad_out, axis=0)
    grad_act = matmul_nt(grad_low, mats["w_" + tag + "down"])
    grad_hidden = (grad_act * gelu_slope(hidden)).astype(jnp.bfloat16)
    grads["w_" + tag + "up"] = matmul_tn(normed_two, grad_hidden)
    grads["b_" + tag + "up"] = jnp.sum(grad_hidden.astype(jnp.float32), axis=0)
    grad_hidden = pin(grad_hidden, watch(AT_HIDDEN, grads, grad_hidden))
    grad_normed = tensor_back(matmul_nt(grad_hidden, mats["w_" + tag + "up"]))
    grad_middle, grads[tag + "ln2_g"], grads[tag + "ln2_b"] = norm_backward(
        middle, vectors[tag + "ln2_g"], vectors[tag + "ln2_b"], grad_normed
    )
    grad_middle = grad_middle + grad_out
    grad_mid_low = grad_middle.astype(jnp.bfloat16)
    grads["w_" + tag + "out"] = group_cut(
        matmul_tn(mixed_rows, grad_mid_low), 0, head_dim, per_group
    )
    grads["b_" + tag + "out"] = jnp.sum(grad_middle, axis=0)
    grad_mixed = matmul_nt(grad_mid_low, mats["w_" + tag + "out"]).astype(jnp.bfloat16)
    groups = packed.shape[1] // 384
    if tag:
        grad_packed = attn_bwd(
            packed, grad_mixed, sides[0], sides[1], log_totals, per_group, head_dim
        )
    else:
        grad_packed = attn_bwd(
            packed,
            grad_mixed,
            sides[0],
            sides[1],
            log_totals,
            per_group,
            head_dim,
            groups=groups // 2,
        )
        grad_mixed = pin(grad_mixed, watch(AT_HALF, grads, grad_packed))
        grad_packed = attn_bwd(
            packed,
            grad_mixed,
            sides[0],
            sides[1],
            log_totals,
            per_group,
            head_dim,
            first=groups // 2,
            groups=groups // 2,
            so_far=grad_packed,
        )
    grads["w_" + tag + "qkv"] = group_cut(
        matmul_tn(normed_low, grad_packed), 1, head_dim, per_group
    )
    grads["b_" + tag + "qkv"] = group_cut(
        jnp.sum(grad_packed.astype(jnp.float32), axis=0), 0, head_dim, per_group
    )
    grad_packed = pin(grad_packed, watch(AT_PACKED, grads, grad_packed))
    first_part = matmul_nt(grad_packed, mats["w_" + tag + "qkv"]).astype(jnp.bfloat16)
    first_part = pin(first_part, watch(AT_PART, grads, first_part))
    grad_first = tensor_back(first_part)
    grad_first = pin(grad_first, watch(AT_FIRST, grads, grad_first))
    grad_stream, grads[tag + "ln1_g"], grads[tag + "ln1_b"] = norm_backward(
        stream, vectors[tag + "ln1_g"], vectors[tag + "ln1_b"], grad_first
    )
    return (grad_stream + grad_middle, grads)


def adam(weight, first, second, grad, rate, decay, count):
    first_new = BETA_ONE * first + (1 - BETA_ONE) * grad
    second_new = BETA_TWO * second + (1 - BETA_TWO) * grad * grad
    first_hat = first_new / (1 - BETA_ONE**count)
    second_hat = second_new / (1 - BETA_TWO**count)
    weight_new = weight - rate * (first_hat / (jnp.sqrt(second_hat) + ADAM_EPS) + decay * weight)
    return (weight_new, first_new, second_new)


UPPER, MIDDLE, LOWER = range(3)
AT_HIDDEN, AT_HALF, AT_PACKED, AT_PART, AT_FIRST = range(5)
SQUARE, LOSS = range(2)
ENC_GROUP = 2
PRED_GROUP = 3


def shards(
    enc_params,
    enc_m1,
    enc_m2,
    pred_params,
    pred_m1,
    pred_m2,
    target_params,
    vecs,
    vec_m1,
    vec_m2,
    target_vecs,
    patches,
    segment,
    context,
    step_count,
):
    ways = lax.axis_size("tensor")
    member = lax.axis_index("tensor")
    dp_count = lax.axis_size("dp")
    place = lax.axis_index("dp").astype(jnp.int32).reshape(1)
    spans = enc_chunks(ways)
    rows = lambda x: x.reshape(-1, 128)
    tiled = dp_count == 16 and enc_params.shape[1] % UNIT == 0 and all(
        a % 3 == 0 and b % 3 == 0 for a, b, w in spans if w == 12
    )
    vectors = split_vector(vecs, enc_vectors() + pred_vectors())
    target_vectors = split_vector(target_vecs, enc_vectors())
    begun = None
    if tiled:
        pred_tiles = rows(pred_params).astype(jnp.bfloat16).reshape(-1, 8, 128)
        own_tiles = jnp.concatenate([pack_tiles(rows(enc_params), place, spans), pred_tiles], 0)
        enc_tiles, begun, nearly = tree_gather(own_tiles)
    segment, target_local = pin((segment, target_params), begun)
    places = positions(segment)
    context_mask = context > 0
    padded = roundup(segment.shape[0], QB)
    online_sides = mask_sides(segment, context, padded)
    all_sides = mask_sides(segment, jnp.ones_like(context), padded)
    embed_pos = sincos(places, D)
    pred_pos = sincos(places, PD)
    if tiled:
        target_tiles = pack_tiles(rows(target_local), place, spans)
        enc_tiles, embed_pos, pred_pos, online_sides, all_sides = pin(
            (enc_tiles, embed_pos, pred_pos, online_sides, all_sides), target_tiles
        )
        target_tiles = pin(target_tiles, nearly)
        sizes = [size for _, size in ENC_TILES]
        shard, both = sum(sizes) // 16, own_tiles.shape[0]
        mats = from_tiles(split_gathered(enc_tiles, sizes, shard, 0, both), ways)
        pred_count = [16 * (both - shard)]
        pred_whole = split_gathered(enc_tiles, pred_count, both - shard, shard, both)[0]
    else:
        mats = gather_flat(rows(enc_params), enc_shapes(ways))
    def embed(patch_rows, weight_set, vector_set):
        return (
            tensor_total(matmul(patch_rows, weight_set["w_patch"])) + vector_set["b_patch"] + embed_pos
        )

    online_mid, online_kept = layer_forward(
        embed(patches, mats, vectors),
        mats,
        vectors,
        "",
        ENC_GROUP,
        HEAD_DIM,
        online_sides,
        ways,
        member,
    )
    if tiled:
        mats.update(unflat(pred_whole.reshape(-1), pred_shapes(ways)))
    else:
        mats.update(gather_flat(rows(pred_params), pred_shapes(ways)))
    mats["w_pqkv"] = group_pad(mats["w_pqkv"], 1, PHEAD_DIM, PRED_GROUP)
    mats["w_pout"] = group_pad(mats["w_pout"], 0, PHEAD_DIM, PRED_GROUP)
    encoded_low = layer_norm(online_mid, vectors["lnf_g"], vectors["lnf_b"]).astype(jnp.bfloat16)
    pin_local = matmul(encoded_low, mats["w_pin"]) + local_columns(
        vectors["b_pin"], False, ways, member
    )
    pin_other = swap(pin_local)
    pin_full = jnp.where(
        member == 0,
        jnp.concatenate([pin_local, pin_other], 1),
        jnp.concatenate([pin_other, pin_local], 1),
    )
    pred_in = jnp.where(context_mask[:, None], pin_full, vectors["mask_tok"][None, :])
    pred_in = pred_in + pred_pos
    if tiled:
        target_whole = gather_dp(target_tiles)
    pred_mid, pred_kept = layer_forward(
        pred_in,
        mats,
        vectors,
        "p",
        PRED_GROUP,
        PHEAD_DIM,
        all_sides,
        ways,
        member,
        (lambda value: target_whole) if tiled else (lambda value: None),
    )
    pred_rows = layer_norm(pred_mid, vectors["plnf_g"], vectors["plnf_b"]).astype(jnp.bfloat16)
    predicted = matmul(pred_rows, mats["w_pproj"]) + local_columns(
        vectors["b_pproj"], False, ways, member
    )
    if tiled:
        target_mats = from_tiles(split_gathered(target_whole, sizes, shard, 0, shard), ways)
    else:
        target_mats = gather_flat(rows(target_params), enc_shapes(ways))
    target_patches, predicted = lax.optimization_barrier((patches, predicted))
    target_mid, _ = layer_forward(
        embed(target_patches, target_mats, target_vectors),
        target_mats,
        target_vectors,
        "",
        ENC_GROUP,
        HEAD_DIM,
        all_sides,
        ways,
        member,
    )
    targets = plain_norm(layer_norm(target_mid, target_vectors["lnf_g"], target_vectors["lnf_b"]))
    target_cols = lax.dynamic_slice_in_dim(targets, member * (D // ways), D // ways, 1)
    target_mask = (1 - context).astype(jnp.float32)
    width = D // ways
    sums = doubling(
        jnp.concatenate(
            [
                jnp.sum(target_mask[:, None] * predicted, axis=0),
                jnp.sum(target_mask[:, None] * predicted * predicted, axis=0),
                jnp.broadcast_to(jnp.sum(target_mask), (128,)),
            ]
        ),
        "dp",
    )
    sum_all, square_all, count_all = sums[:width], sums[width : 2 * width], sums[2 * width]
    difference = predicted - target_cols
    error = jnp.sum(target_mask[:, None] * jnp.abs(difference)) / (count_all * D)
    column_mean = sum_all / count_all
    column_var = square_all / count_all - column_mean * column_mean
    spread = jnp.sqrt(column_var + VAR_EPS)
    local_loss = error + jnp.sum((spread - 1.0) ** 2) / D / dp_count
    grad_var = (spread - 1.0) / (D * spread)
    grad_pred = target_mask[:, None] * (
        jnp.sign(difference) / (count_all * D)
        + 2.0 * grad_var * (predicted - column_mean) / count_all
    )
    grads = {}
    grad_low = grad_pred.astype(jnp.bfloat16)
    grads["w_pproj"] = matmul_tn(pred_rows, grad_low)
    grads["b_pproj"] = jnp.sum(grad_pred, axis=0)
    grad_normed = tensor_back(matmul_nt(grad_low, mats["w_pproj"]))
    grad_mid, grads["plnf_g"], grads["plnf_b"] = norm_backward(
        pred_mid, vectors["plnf_g"], vectors["plnf_b"], grad_normed
    )
    grad_in, layer_grads = layer_backward(
        grad_mid, pred_kept, mats, vectors, "p", PRED_GROUP, PHEAD_DIM, all_sides, lambda *_: None
    )
    grads.update(layer_grads)
    grads["mask_tok"] = jnp.sum(jnp.where(context_mask[:, None], 0.0, grad_in), axis=0)
    grad_pin = lax.dynamic_slice_in_dim(
        jnp.where(context_mask[:, None], grad_in, 0.0), member * (PD // ways), PD // ways, 1
    )
    grad_pin_low = grad_pin.astype(jnp.bfloat16)
    grads["w_pin"] = matmul_tn(encoded_low, grad_pin_low)
    grads["b_pin"] = jnp.sum(grad_pin, axis=0)
    grad_encoded = tensor_back(matmul_nt(grad_pin_low, mats["w_pin"]))
    grad_mid, grads["lnf_g"], grads["lnf_b"] = norm_backward(
        online_mid, vectors["lnf_g"], vectors["lnf_b"], grad_encoded
    )
    pred_flat = flatten_matrices([grads[label] for label, _, _ in pred_shapes(ways)])
    pred_flat, grad_mid = lax.optimization_barrier((pred_flat, grad_mid))
    pred_share = None
    if tiled:
        pred_tree = tree_scatter(pred_flat.reshape(-1, 8, 128), (0, 1, 2, 3))
        next(pred_tree)
    else:
        pred_share = lax.psum_scatter(pred_flat, "dp", scatter_dimension=0, tiled=True)
    sections = enc_vectors() + pred_vectors()
    early = []
    pred_shares = []

    def shared_part(found, label, length):
        if label in LOCAL_BIAS:
            return place_columns(found[label], length, LOCAL_BIAS[label], ways, member)
        return 0.5 * found[label]

    def all_devices(parts, after=None):
        total = doubling(doubling(jnp.concatenate(list(parts.values())), "tensor"), "dp", after)
        result = {}
        start = 0
        for label, part in parts.items():
            result[label] = total[start : start + part.shape[0]]
            start += part.shape[0]
        return result

    def early_sum(found):
        found = {**grads, **found}
        parts = {
            label: shared_part(found, label, length)
            for label, length in sections
            if label in found
        }
        parts[LOSS] = jnp.broadcast_to(local_loss, (128,))
        return all_devices(parts)

    pieces = {}
    trees = {}

    def watch(name, so_far, value):
        if not tiled:
            return None
        for label, grad in so_far.items():
            if label.startswith("w_") and label not in pieces:
                pieces[label] = to_tiles(grad.astype(jnp.bfloat16))
        if name == AT_HIDDEN:
            pred_ready = advance(pred_tree, value)
            trees[UPPER] = tree_scatter(stack_tiles(pieces, (2, 3)), (2, 3))
            return (next(trees[UPPER]), pred_ready)
        if name == AT_PACKED:
            trees[MIDDLE] = tree_scatter(stack_tiles(pieces, (1,)), (1,))
            return (advance(trees[UPPER], value), next(trees[MIDDLE]))
        if name == AT_HALF:
            pred_shares.append(advance(pred_tree, value).reshape(-1, 128))
            early.append(early_sum(so_far))
        return None

    grad_in, layer_grads = layer_backward(
        grad_mid, online_kept, mats, vectors, "", ENC_GROUP, HEAD_DIM, online_sides, watch
    )
    grads.update(layer_grads)
    grad_in_low = grad_in.astype(jnp.bfloat16)
    grads["w_patch"] = matmul_tn(patches, grad_in_low)
    grads["b_patch"] = jnp.sum(grad_in, axis=0)
    if tiled:
        pieces["w_patch"] = to_tiles(grads["w_patch"].astype(jnp.bfloat16))
        trees[LOWER] = tree_scatter(stack_tiles(pieces, (0,)), (0,))
        token = next(trees[LOWER])
        token = [advance(trees[UPPER], token), advance(trees[MIDDLE], token)]
        token = advance(trees[LOWER], token)
        token = advance(trees[MIDDLE], token)
        shares = {UPPER: advance(trees[UPPER], token)}
        token = advance(trees[LOWER], token)
        shares[MIDDLE] = advance(trees[MIDDLE], token)
        shares[LOWER] = advance(trees[LOWER], token)
        share = jnp.where(
            place[0] >= 8,
            shares[UPPER],
            jnp.where(place[0] >= 4, shares[MIDDLE], shares[LOWER]),
        )
        enc_square = jnp.square(share.astype(jnp.float32))
        enc_share = unpack_tiles(share, place, spans)
    else:
        enc_share = scatter_flat(grads, enc_shapes(ways), jnp.float32)
        enc_square = enc_share * enc_share
    if not early:
        early.append(early_sum(grads))
    sums = dict(early[0])
    loss_value = sums.pop(LOSS)[0]
    if tiled:
        pred_share = pred_shares[0]
    square_sum = jnp.sum(enc_square) + jnp.sum(pred_share * pred_share)
    late = {label: shared_part(grads, label, length) for label, length in sections}
    late = {label: part for label, part in late.items() if label not in sums}
    late[SQUARE] = jnp.broadcast_to(square_sum, (128,))
    sums.update(all_devices(late, enc_share))
    square_total = sums.pop(SQUARE)[0]
    vector_grad = jnp.concatenate([sums[label] for label, _ in sections])
    grad_norm = jnp.sqrt(square_total + jnp.sum(vector_grad * vector_grad))
    factor = jnp.minimum(1.0, CLIP / (grad_norm + 1e-06))
    count = step_count[0].astype(jnp.float32)
    scalars = jnp.stack(
        [factor, 1.0 / (1 - BETA_ONE**count), 1.0 / (1 - BETA_TWO**count)]
    ).astype(jnp.float32)
    back = lambda x: x.reshape(1, -1)
    new_enc, enc_first, enc_second, new_target = map(
        back,
        adam_flat(
            scalars,
            [rows(enc_params), rows(enc_m1), rows(enc_m2), enc_share, rows(target_params)],
        ),
    )
    new_pred, pred_first, pred_second = map(
        back, adam_flat(scalars, [rows(pred_params), rows(pred_m1), rows(pred_m2), pred_share])
    )
    new_vec, vec_first, vec_second = adam(
        vecs, vec_m1, vec_m2, vector_grad * factor, RATE_VEC, 0.0, count
    )
    new_target_vec = TAU * target_vecs + (1 - TAU) * new_vec[: target_vecs.shape[0]]
    return (
        new_enc,
        enc_first,
        enc_second,
        new_enc.astype(jnp.bfloat16),
        new_pred,
        pred_first,
        pred_second,
        new_pred.astype(jnp.bfloat16),
        new_target,
        new_vec,
        vec_first,
        vec_second,
        new_target_vec,
        loss_value,
        grad_norm,
    )


def solution(mesh):
    placed = (
        P("tensor", "dp"),
        P("tensor", "dp"),
        P("tensor", "dp"),
        P("tensor", "dp"),
        P("tensor", "dp"),
        P("tensor", "dp"),
        P("tensor", "dp"),
        P(),
        P(),
        P(),
        P(),
        P("dp", "tensor"),
        P("dp"),
        P("dp"),
        P(),
    )
    return jax.shard_map(
        shards,
        mesh=mesh,
        in_specs=placed,
        out_specs=(
            P("tensor", "dp"),
            P("tensor", "dp"),
            P("tensor", "dp"),
            P("tensor", "dp"),
            P("tensor", "dp"),
            P("tensor", "dp"),
            P("tensor", "dp"),
            P("tensor", "dp"),
            P("tensor", "dp"),
            P(),
            P(),
            P(),
            P(),
            P(),
            P(),
        ),
        check_vma=False,
    )
```
